32 devices in a mesh: band: 8 (over z, core), tp: 4 (over y, x).
Axes of the slice: x: 2, y: 2, z: 4, core: 2. Of those that a mesh axis runs over, the one named last changes fastest.
Arguments:
- tokens: bfloat16 [4, 2048, 2048], P(None, 'band'), may hold values from -6 to 6
- positions: int32 [4, 2048], P(None, 'band'), may hold values from 0 to 2047, as said below
- doc_lengths: int32 [4, 4], replicated, may hold values from 1 to 1024, 2048 in all within a row
- exit_depth: int32 [4, 2048], replicated, may hold values from 1 to 24, as said below
- w_query: bfloat16 [2048, 2048], P('band', 'tp'), may hold values from -0.125 to 0.125
- w_key: bfloat16 [2048, 2048], P('band', 'tp'), may hold values from -0.125 to 0.125
- w_value: bfloat16 [2048, 2048], P('band', 'tp'), may hold values from -0.125 to 0.125
- w_out: bfloat16 [2048, 2048], P('tp', 'band'), may hold values from -1 to 1
- w_up: bfloat16 [2048, 8192], P('band', 'tp'), may hold values from -0.125 to 0.125
- w_down: bfloat16 [8192, 2048], P('tp', 'band'), may hold values from -0.0625 to 0.0625
- b_query: float32 [2048], P('tp'), may hold values from -3 to 3
- b_value: float32 [2048], P('tp'), may hold values from -3 to 3
- b_out: float32 [2048], replicated, may hold values from -3 to 3
- b_up: float32 [8192], P('tp'), may hold values from -3 to 3
- b_down: float32 [2048], replicated, may hold values from -3 to 3
- attn_gain: float32 [2048], replicated, may hold values from 0.1 to 1.9
- attn_bias: float32 [2048], replicated, may hold values from -2 to 2
- ffn_gain: float32 [2048], replicated, may hold values from 0.1 to 1.9
- ffn_bias: float32 [2048], replicated, may hold values from -2 to 2
- cotangent: bfloat16 [4, 2048, 2048], P(None, 'band'), may hold values from -6 to 6
Outputs:
- output: bfloat16 [4, 2048, 2048], P(None, 'band')
- token_grad: float32 [4, 2048, 2048], P(None, 'band')
- grad_w_query: float32 [2048, 2048], P('band', 'tp')
- grad_w_key: float32 [2048, 2048], P('band', 'tp')
- grad_w_value: float32 [2048, 2048], P('band', 'tp')
- grad_w_out: float32 [2048, 2048], P('tp', 'band')
- grad_w_up: float32 [2048, 8192], P('band', 'tp')
- grad_w_down: float32 [8192, 2048], P('tp', 'band')
- grad_b_query: float32 [2048], P('tp')
- grad_b_value: float32 [2048], P('tp')
- grad_b_out: float32 [2048], replicated
- grad_b_up: float32 [8192], P('tp')
- grad_b_down: float32 [2048], replicated
- grad_attn_gain: float32 [2048], replicated
- grad_attn_bias: float32 [2048], replicated
- grad_ffn_gain: float32 [2048], replicated
- grad_ffn_bias: float32 [2048], replicated
The draws below stay inside these ranges and needn't reach their ends.
Inputs may be any that keep to these rules, and one draw needn't show every extreme that they name: `positions`: each sequence's row holds every position 0 to 2047 once. `doc_lengths`: each row sums to 2048, and its largest entry is 1024. `exit_depth`: along a row (by position) the depths never rise, and position 0 has 24.
All inputs are finite; a program needn't handle non-finite values.
Results may differ from the reference program's by a relative error of at most 0.02.
Values may be sent and summed in bfloat16 or wider, within the bound.
A program may use at most 256 MiB of HBM per device.

```python
import math
import jax
import jax.numpy as jnp
import numpy as np
from jax import lax

D = 2048
HEADS = 32
HEAD_DIM = 64
FF = 8192
DEPTH = 24
LAYER = 12
LEN = 2048
NDOC = 4
SEQS = 4


def draw_positions(key, part):
    key = jax.random.fold_in(key, 1)
    several = jax.random.split(key, SEQS)
    return jax.vmap(lambda single: jax.random.permutation(single, LEN))(several).astype(jnp.int32)


def draw_exit_depth(key, part):
    key = jax.random.fold_in(key, 2)
    slopes = jax.random.randint(key, (SEQS, 1), LAYER, DEPTH + 1)
    places = jnp.arange(LEN, dtype=jnp.int32)[None, :]
    return (DEPTH - places * slopes // LEN).astype(jnp.int32)


def level_of(key, dims, cuts, low, largest):
    loudness = 1.0
    for axis_at, shards_of in cuts:
        draws = jax.random.uniform(jax.random.fold_in(jax.random.fold_in(key, 6), axis_at), (shards_of,), jnp.float32, low / len(cuts), largest / len(cuts))
        loudness = loudness * jnp.repeat(jnp.exp(draws), dims[axis_at] // shards_of).reshape((-1,) + (1,) * (len(dims) - 1 - axis_at))
    return loudness


def profile(number_of, total, reach, lean):
    weights = [(1 << 20) // math.isqrt(grade ** lean) + 1 for grade in range(2, number_of + 1)]
    rest, holding = total - reach - (number_of - 1), [1] * (number_of - 1)
    while rest > 0:
        movable = [i for i in range(number_of - 1) if holding[i] < reach]
        mass, remaining = sum([weights[i] for i in movable]), rest
        for i in movable:
            more = min(reach - holding[i], max(1, remaining * weights[i] // mass), rest)
            holding[i] = holding[i] + more
            rest = rest - more
    return np.array([reach] + holding)


def ragged_sizes(own_key, amount, total, bound, slope):
    if amount == 2:
        one = jax.random.randint(own_key, (), max(1, total - bound), min(bound, total - 1) + 1)
        return jnp.stack([one, total - one])
    tallies = jnp.asarray(profile(amount, total, bound, slope), jnp.int32)
    twos = (amount - 1) // 2
    source_of, sink = tallies[1:1 + 2 * twos:2], tallies[2:2 + 2 * twos:2]
    margin = jnp.minimum(source_of - 1, bound - sink)
    moved = jax.random.randint(jax.random.fold_in(own_key, 1), (twos,), 0, 1 << 20) % (margin + 1)
    tallies = tallies.at[1:1 + 2 * twos:2].set(source_of - moved).at[2:2 + 2 * twos:2].set(sink + moved)
    return tallies[jax.random.permutation(jax.random.fold_in(own_key, 2), amount)]


def scatter_about(key, shape, width, limit, pieces=(), held_as=jnp.bfloat16):
    entries = jax.random.normal(key, shape, jnp.float32) * width
    if len(pieces) > 0:
        entries = level_of(key, shape, pieces, -0.22, 0.18) * entries
    return jnp.clip(entries, min=-limit, max=limit).astype(held_as)


def setup_inputs(seed: int = 0) -> dict:
    splits = jax.random.split(jax.random.key(seed), 21)
    tokens = scatter_about(splits[0], (SEQS, LEN, D), 1.0, 6.0, ((1, 8),))
    positions = draw_positions(jax.random.fold_in(splits[20], 71), 0)
    doc_lengths = jax.vmap(lambda own: ragged_sizes(own, NDOC, LEN, LEN // 2, 2))(jax.random.split(splits[2], SEQS)).reshape((SEQS, NDOC)).astype(jnp.int32)
    exit_depth = draw_exit_depth(jax.random.fold_in(splits[20], 71), 0)
    w_query = scatter_about(splits[4], (D, D), D ** -0.5, 0.125, ((0, 8), (1, 4)))
    w_key = scatter_about(splits[5], (D, D), D ** -0.5, 0.125, ((0, 8), (1, 4)))
    w_value = scatter_about(splits[6], (D, D), D ** -0.5, 0.125, ((0, 8), (1, 4)))
    w_out = scatter_about(splits[7], (D, D), (D // 64) ** -0.5, 1.0, ((0, 4), (1, 8)))
    w_up = scatter_about(splits[8], (D, FF), D ** -0.5, 0.125, ((0, 8), (1, 4)))
    w_down = scatter_about(splits[9], (FF, D), FF ** -0.5, 0.0625, ((0, 4), (1, 8)))
    b_query = scatter_about(splits[10], (D,), 0.5, 3.0, ((0, 4),), jnp.float32)
    b_value = scatter_about(splits[11], (D,), 0.5, 3.0, ((0, 4),), jnp.float32)
    b_out = scatter_about(splits[12], (D,), 0.5, 3.0, (), jnp.float32)
    b_up = scatter_about(splits[13], (FF,), 0.5, 3.0, ((0, 4),), jnp.float32)
    b_down = scatter_about(splits[14], (D,), 0.5, 3.0, (), jnp.float32)
    attn_gain = jnp.clip(1.0 + 0.18 * jax.random.normal(splits[15], (D,), jnp.float32), 0.1, 1.9)
    attn_bias = scatter_about(splits[16], (D,), 0.3, 2.0, (), jnp.float32)
    ffn_gain = jnp.clip(1.0 + 0.18 * jax.random.normal(splits[17], (D,), jnp.float32), 0.1, 1.9)
    ffn_bias = scatter_about(splits[18], (D,), 0.3, 2.0, (), jnp.float32)
    cotangent = scatter_about(splits[19], (SEQS, LEN, D), 1.0, 6.0, ((1, 8),))
    return {"tokens": tokens, "positions": positions, "doc_lengths": doc_lengths, "exit_depth": exit_depth, "w_query": w_query, "w_key": w_key, "w_value": w_value, "w_out": w_out, "w_up": w_up, "w_down": w_down, "b_query": b_query, "b_value": b_value, "b_out": b_out, "b_up": b_up, "b_down": b_down, "attn_gain": attn_gain, "attn_bias": attn_bias, "ffn_gain": ffn_gain, "ffn_bias": ffn_bias, "cotangent": cotangent}


epsilon = 1e-05
masked_score = -1e+30

@jax.custom_vjp
def low(v):
    return lax.optimization_barrier(v.astype(jnp.bfloat16)).astype(jnp.float32)

@jax.custom_vjp
def low_back(v):
    return v

def low_keep(v):
    return (low(v), None)

def low_pass(kept, grad):
    return (grad,)

def back_keep(v):
    return (v, None)

def back_low(kept, grad):
    return (low(grad),)
low.defvjp(low_keep, low_pass)
low_back.defvjp(back_keep, back_low)

def layer_norm(values, gain, shift):
    center = values - lax.optimization_barrier(jnp.mean(values, axis=-1, keepdims=True))
    inverse = lax.rsqrt(lax.optimization_barrier(jnp.mean(center * center, axis=-1, keepdims=True)) + epsilon)
    return center * inverse * gain + shift

def product(left, right):
    return jnp.dot(left, right, preferred_element_type=jnp.float32, precision=lax.Precision.HIGHEST)

def sequence_forward(inputs, params, places, doc_ids, live_rows):
    w_query, w_key, w_value, w_out, w_up, w_down, b_query, b_value, b_out, b_up, b_down, attn_gain, attn_bias, ffn_gain, ffn_bias = params
    normed = low(layer_norm(inputs, attn_gain, attn_bias))
    queries = low(low_back(product(normed, w_query) + b_query))
    keys_all = low(low_back(product(normed, w_key)))
    values_all = low(low_back(product(normed, w_value) + b_value))
    query_heads = queries.reshape(LEN, HEADS, HEAD_DIM)
    key_heads = keys_all.reshape(LEN, HEADS, HEAD_DIM)
    value_heads = values_all.reshape(LEN, HEADS, HEAD_DIM)
    block = min(512, LEN)
    factor = HEAD_DIM ** (-0.5)

    def attend(start):
        block_query = lax.dynamic_slice_in_dim(query_heads, start, block, 0)
        block_pos = lax.dynamic_slice_in_dim(places, start, block, 0)
        block_doc = lax.dynamic_slice_in_dim(doc_ids, start, block, 0)
        scores = jnp.einsum('qhd,khd->hqk', block_query, key_heads, precision=lax.Precision.HIGHEST) * factor
        scores = low_back(scores)
        allowed = (block_doc[:, None] == doc_ids[None, :]) & (places[None, :] <= block_pos[:, None])
        allowed = allowed & (live_rows[None, :] | (places[None, :] == block_pos[:, None]))
        scores = jnp.where(allowed[None], scores, masked_score)
        shifted = jnp.exp(scores - lax.optimization_barrier(jnp.max(scores, axis=2, keepdims=True)))
        probs = low(shifted / lax.optimization_barrier(jnp.sum(shifted, axis=2, keepdims=True)))
        return jnp.einsum('hqk,khd->qhd', probs, value_heads, precision=lax.Precision.HIGHEST)
    starts = jnp.arange(0, LEN, block, dtype=jnp.int32)
    mixed = lax.map(jax.checkpoint(attend), starts).reshape(LEN, HEADS * HEAD_DIM)
    mixed = low(low_back(mixed))
    attn_out = low_back(product(mixed, w_out) + b_out)
    residual = inputs + attn_out
    normed_mid = low(layer_norm(residual, ffn_gain, ffn_bias))
    pre_act = low_back(product(normed_mid, w_up) + b_up)
    hidden = low(jax.nn.gelu(pre_act, approximate=False))
    ffn_out = low_back(product(hidden, w_down) + b_down)
    return inputs + live_rows.astype(jnp.float32)[:, None] * (attn_out + ffn_out)

def reference(tokens, positions, doc_lengths, exit_depth, w_query, w_key, w_value, w_out, w_up, w_down, b_query, b_value, b_out, b_up, b_down, attn_gain, attn_bias, ffn_gain, ffn_bias, cotangent):
    params = tuple((item.astype(jnp.float32) for item in (w_query, w_key, w_value, w_out, w_up, w_down, b_query, b_value, b_out, b_up, b_down, attn_gain, attn_bias, ffn_gain, ffn_bias)))
    ends = jnp.cumsum(doc_lengths, axis=1).astype(jnp.int32)
    doc_ids = lax.optimization_barrier(jnp.sum((positions[:, :, None] >= ends[:, None, :]).astype(jnp.int32), axis=2)).astype(jnp.int32)
    live = jnp.take_along_axis(exit_depth, positions, axis=1) > LAYER

    def one_sequence(totals, item):
        inputs, places, docs_here, live_here, grad_out = item

        def forward(values, weights):
            return sequence_forward(values, weights, places, docs_here, live_here)
        result, pull = jax.vjp(forward, inputs.astype(jnp.float32), params)
        input_grad, weight_grads = pull(grad_out.astype(jnp.float32))
        totals = jax.tree.map(lambda left, right: left + right, totals, weight_grads)
        return (totals, (result.astype(jnp.bfloat16), input_grad))
    zeros = jax.tree.map(jnp.zeros_like, params)
    totals, (output, token_grad) = lax.scan(one_sequence, zeros, (tokens, positions, doc_ids, live, cotangent))
    return (output, token_grad, totals[0], totals[1], totals[2], totals[3], totals[4], totals[5], totals[6], totals[7], totals[8], totals[9], totals[10], totals[11], totals[12], totals[13], totals[14])
```

```python
import functools
import math

import jax
import jax.numpy as jnp
from jax import lax
from jax.experimental import pallas as pl
from jax.experimental.pallas import tpu as pltpu
from jax.sharding import PartitionSpec as P

HEAD_DIM = 64
LAYER = 12
MESH = pl.DeviceIdType.MESH

epsilon = 1e-05
masked_score = -1e30
bf16 = jnp.bfloat16
f32 = jnp.float32


def layer_norm(values, gain, shift):
    center = values - jnp.mean(values, axis=-1, keepdims=True)
    inverse = lax.rsqrt(jnp.mean(center * center, axis=-1, keepdims=True) + epsilon)
    normed = center * inverse
    return (normed * gain + shift, normed, inverse)


def norm_back(grad_out, normed, inverse, gain):
    scaled = grad_out * gain
    return inverse * (
        scaled
        - jnp.mean(scaled, axis=-1, keepdims=True)
        - normed * jnp.mean(scaled * normed, axis=-1, keepdims=True)
    )


def nn(left, right):
    return jnp.dot(left, right, preferred_element_type=f32)


def nt(left, right):
    return lax.dot_general(left, right, (((1,), (1,)), ((), ())), preferred_element_type=f32)


def tn(left, right):
    return lax.dot_general(left, right, (((0,), (0,)), ((), ())), preferred_element_type=f32)


def gelu_exact(values):
    return jax.nn.gelu(values, approximate=False)


def halves(count):
    return (count // 2, 2) if count % 2 == 0 else (count, 1)


def greet(devices):
    barrier = pltpu.get_barrier_semaphore()
    for device in devices:
        pl.semaphore_signal(barrier, inc=1, device_id=device, device_id_type=MESH)
    pl.semaphore_wait(barrier, len(devices))


def takes(microseconds):
    return pl.CostEstimate(
        flops=int(microseconds * 1e9), bytes_accessed=int(microseconds * 2e6), transcendentals=0
    )


def keep(source, target, through, sem, k=0):
    first = pltpu.make_async_copy(source, through, sem.at[k])
    first.start()

    def second():
        first.wait()
        copy = pltpu.make_async_copy(through, target, sem.at[k + 1])
        copy.start()
        return copy

    return second


def grid_peers(count):
    na, nb = halves(count)
    me, band = lax.axis_index("tp"), lax.axis_index("band")
    a, b = me // nb, lax.rem(me, nb)
    along_b = [(band, a * nb + lax.rem(b + d, nb)) for d in range(1, nb)]
    along_a = [(band, lax.rem(a + d, na) * nb + b) for d in range(1, na)]
    from_b = [a * nb + lax.rem(b + nb - d, nb) for d in range(1, nb)]
    from_a = [lax.rem(a + na - d, na) * nb + b for d in range(1, na)]
    return me, a, b, along_a, along_b, from_a, from_b


def gather_kernel(count, inner_slot, with_extra, *refs):
    if with_extra:
        x_ref, e_ref, o_ref, t_ref, through, local_sem, send_sem, recv_sem, part_ref, in_b, in_a = refs
    else:
        x_ref, o_ref, through, local_sem, send_sem, recv_sem = refs
    me, a, b, along_a, along_b, from_a, from_b = grid_peers(count)
    half = x_ref.shape[0] // 2
    part = (pl.ds(0, half), pl.ds(half, half))

    def slot(index, which):
        return o_ref.at[part[which], index] if inner_slot else o_ref.at[index, part[which]]

    greet(along_a + along_b)
    whole = o_ref.at[:, me] if inner_slot else o_ref.at[me]
    local = keep(x_ref, whole, through, local_sem)
    used = []

    def move(source, target, device):
        k = len(used)
        copy = pltpu.make_async_remote_copy(
            source, target, send_sem.at[k], recv_sem.at[k],
            device_id=device, device_id_type=MESH,
        )
        copy.start()
        used.append(copy)
        return copy

    def send(source, index, which, device):
        return move(source, slot(index, which), device)

    if with_extra:
        extra_b = [move(e_ref, in_b.at[k], device) for k, device in enumerate(along_b)]
    first_b = [send(x_ref.at[part[0]], me, 0, device) for device in along_b]
    first_a = [send(x_ref.at[part[1]], me, 1, device) for device in along_a]
    second = [send(x_ref.at[part[0]], me, 0, device) for device in along_a]
    second += [send(x_ref.at[part[1]], me, 1, device) for device in along_b]
    local = local()
    if with_extra:
        total = e_ref[...]
        for k, copy in enumerate(extra_b):
            copy.wait_recv()
            total = total + in_b[k]
        part_ref[...] = total
        extra_a = [move(part_ref, in_a.at[k], device) for k, device in enumerate(along_a)]
    for copy, source in zip(first_b, from_b):
        copy.wait_recv()
        second += [send(slot(source, 0), source, 0, device) for device in along_a]
    for copy, source in zip(first_a, from_a):
        copy.wait_recv()
        second += [send(slot(source, 1), source, 1, device) for device in along_b]
    if with_extra:
        total = part_ref[...]
        for k, copy in enumerate(extra_a):
            copy.wait_recv()
            total = total + in_a[k]
        t_ref[...] = total
        for copy in extra_a + extra_b:
            copy.wait_send()
    for copy in first_a + first_b:
        copy.wait_send()
    for copy in second:
        copy.wait()
    local.wait()


def gather_tp(x, cid, inner_slot=False, extra=None):
    count = lax.axis_size("tp")
    na, nb = halves(count)
    copies = 2 * (na - 1 + nb - 1) + 2 * (na - 1) * (nb - 1)
    shape = (x.shape[0], count) + x.shape[1:] if inner_slot else (count,) + x.shape
    operands, shapes = [x], [jax.ShapeDtypeStruct(shape, x.dtype)]
    specs = [pl.BlockSpec(memory_space=pl.ANY)]
    more = []
    if extra is not None:
        operands.append(extra)
        shapes.append(jax.ShapeDtypeStruct(extra.shape, extra.dtype))
        specs.append(pl.BlockSpec(memory_space=pltpu.VMEM))
        copies += na - 1 + nb - 1
        more = [
            pltpu.VMEM(extra.shape, extra.dtype),
            pltpu.VMEM((max(nb - 1, 1),) + extra.shape, extra.dtype),
            pltpu.VMEM((max(na - 1, 1),) + extra.shape, extra.dtype),
        ]
    out = pl.pallas_call(
        functools.partial(gather_kernel, count, inner_slot, extra is not None),
        out_shape=tuple(shapes),
        in_specs=specs,
        out_specs=tuple(specs),
        scratch_shapes=[
            pltpu.VMEM(x.shape, x.dtype),
            pltpu.SemaphoreType.DMA((2,)),
            pltpu.SemaphoreType.DMA((copies,)),
            pltpu.SemaphoreType.DMA((copies,)),
            *more,
        ],
        compiler_params=pltpu.CompilerParams(collective_id=cid, has_side_effects=True),
        cost_estimate=takes(36),
        name="gather_tp",
    )(*operands)
    return out if extra is not None else out[0]


def scatter_kernel(
    count, p_ref, o_ref, own_a, own_b, one_a, one_b, out_a, out_b, two_a, two_b,
    local_sem, send_sem, recv_sem,
):
    na, nb = halves(count)
    me, a, b, along_a, along_b, from_a, from_b = grid_peers(count)
    half = p_ref.shape[1] // 2
    top, low = pl.ds(0, half), pl.ds(half, half)
    greet(along_a + along_b)
    used = []

    def send(source, target, device):
        k = len(used)
        copy = pltpu.make_async_remote_copy(
            source, target, send_sem.at[k], recv_sem.at[k],
            device_id=device, device_id_type=MESH,
        )
        copy.start()
        used.append(copy)
        return copy

    order_a = list(range(1, na)) + [0]
    order_b = list(range(1, nb)) + [0]
    first_a, first_b = {}, {}
    for step in range(max(na, nb)):
        if step < na:
            e = order_a[step]
            row = lax.rem(a + e, na) * nb
            for d in range(1, nb):
                source = p_ref.at[row + lax.rem(b + d, nb), top]
                first_b[d, e] = send(source, one_a.at[d - 1, e], along_b[d - 1])
        if step < nb:
            e = order_b[step]
            column = lax.rem(b + e, nb)
            for d in range(1, na):
                source = p_ref.at[lax.rem(a + d, na) * nb + column, low]
                first_a[d, e] = send(source, one_b.at[d - 1, e], along_a[d - 1])
    local_a, local_b = {}, {}
    for e in order_a:
        local_a[e] = pltpu.make_async_copy(
            p_ref.at[lax.rem(a + e, na) * nb + b, top], own_a.at[e], local_sem.at[e]
        )
        local_a[e].start()
    for e in order_b:
        local_b[e] = pltpu.make_async_copy(
            p_ref.at[a * nb + lax.rem(b + e, nb), low], own_b.at[e], local_sem.at[na + e]
        )
        local_b[e].start()
    second_a, second_b = {}, {}
    for e in order_a[:-1]:
        local_a[e].wait()
        total = own_a[e].astype(f32)
        for d in range(1, nb):
            first_b[d, e].wait_recv()
            total = total + one_a[d - 1, e].astype(f32)
        out_a[e - 1] = total.astype(out_a.dtype)
        second_a[e] = send(out_a.at[e - 1], two_a.at[e - 1], along_a[e - 1])
    for e in order_b[:-1]:
        local_b[e].wait()
        total = own_b[e].astype(f32)
        for d in range(1, na):
            first_a[d, e].wait_recv()
            total = total + one_b[d - 1, e].astype(f32)
        out_b[e - 1] = total.astype(out_b.dtype)
        second_b[e] = send(out_b.at[e - 1], two_b.at[e - 1], along_b[e - 1])
    local_a[0].wait()
    total = own_a[0].astype(f32)
    for d in range(1, nb):
        first_b[d, 0].wait_recv()
        total = total + one_a[d - 1, 0].astype(f32)
    for e in order_a[:-1]:
        second_a[e].wait_recv()
        total = total + two_a[e - 1].astype(f32)
    o_ref[top] = total
    local_b[0].wait()
    total = own_b[0].astype(f32)
    for d in range(1, na):
        first_a[d, 0].wait_recv()
        total = total + one_b[d - 1, 0].astype(f32)
    for e in order_b[:-1]:
        second_b[e].wait_recv()
        total = total + two_b[e - 1].astype(f32)
    o_ref[low] = total
    for copy in used:
        copy.wait_send()


def scatter_tp(partial, cid):
    count, rows, width = partial.shape
    na, nb = halves(count)
    half = rows // 2
    copies = 2 * (na - 1) * (nb - 1) + 2 * (na - 1 + nb - 1)
    block = (half, width)

    def buffer(*lead):
        return pltpu.VMEM(tuple(max(n, 1) for n in lead) + block, partial.dtype)

    return pl.pallas_call(
        functools.partial(scatter_kernel, count),
        out_shape=jax.ShapeDtypeStruct((rows, width), f32),
        in_specs=[pl.BlockSpec(memory_space=pl.ANY)],
        out_specs=pl.BlockSpec(memory_space=pltpu.VMEM),
        scratch_shapes=[
            buffer(na), buffer(nb),
            buffer(nb - 1, na), buffer(na - 1, nb),
            buffer(na - 1), buffer(nb - 1),
            buffer(na - 1), buffer(nb - 1),
            pltpu.SemaphoreType.DMA((na + nb,)),
            pltpu.SemaphoreType.DMA((copies,)),
            pltpu.SemaphoreType.DMA((copies,)),
        ],
        compiler_params=pltpu.CompilerParams(
            collective_id=cid, has_side_effects=True, vmem_limit_bytes=40 * 2**20
        ),
        cost_estimate=takes(36),
        name="scatter_tp",
    )(partial)


def gather_later(x):
    count = lax.axis_size("tp")
    return lax.all_to_all(jnp.broadcast_to(x[None], (count,) + x.shape), "tp", 0, 0)


def swap_kernel(size, with_positions, *refs):
    if with_positions:
        x_ref, p_ref, o_ref, q_ref, through, p_through, local_sem, send_sem, recv_sem = refs
    else:
        x_ref, o_ref, through, local_sem, send_sem, recv_sem = refs
    me, tp = lax.axis_index("band"), lax.axis_index("tp")
    others = [lax.rem(me + d, size) for d in range(1, size)]
    greet([(other, tp) for other in others])
    local = [keep(x_ref.at[me], o_ref.at[me], through, local_sem)]
    if with_positions:
        local.append(keep(p_ref, q_ref.at[me], p_through, local_sem, 2))
    copies = []
    for k, other in enumerate(others):
        if with_positions:
            copies.append(
                pltpu.make_async_remote_copy(
                    p_ref, q_ref.at[me], send_sem.at[size - 1 + k], recv_sem.at[size - 1 + k],
                    device_id=(other, tp), device_id_type=MESH,
                )
            )
        copies.append(
            pltpu.make_async_remote_copy(
                x_ref.at[other], o_ref.at[me], send_sem.at[k], recv_sem.at[k],
                device_id=(other, tp), device_id_type=MESH,
            )
        )
    for copy in copies:
        copy.start()
    local = [rest() for rest in local]
    for copy in copies + local:
        copy.wait()


def swap_band(x, cid, positions=None):
    size = lax.axis_size("band")
    operands, shapes = [x], [jax.ShapeDtypeStruct(x.shape, x.dtype)]
    if positions is not None:
        operands.append(positions)
        shapes.append(jax.ShapeDtypeStruct((size,) + positions.shape, positions.dtype))
    lanes = (size - 1) * len(operands)
    out = pl.pallas_call(
        functools.partial(swap_kernel, size, positions is not None),
        out_shape=tuple(shapes),
        in_specs=[pl.BlockSpec(memory_space=pl.ANY)] * len(operands),
        out_specs=tuple([pl.BlockSpec(memory_space=pl.ANY)] * len(operands)),
        scratch_shapes=[
            pltpu.VMEM(x.shape[1:], x.dtype),
            *(pltpu.VMEM(extra.shape, extra.dtype) for extra in operands[1:]),
            pltpu.SemaphoreType.DMA((4,)),
            pltpu.SemaphoreType.DMA((lanes,)),
            pltpu.SemaphoreType.DMA((lanes,)),
        ],
        compiler_params=pltpu.CompilerParams(collective_id=cid, has_side_effects=True),
        cost_estimate=takes(30),
        name="swap_band",
    )(*operands)
    return out if positions is not None else out[0]


def heads_kernel(group, x_ref, o_ref, through, local_sem, send_sem, recv_sem):
    band, tp = lax.axis_index("band"), lax.axis_index("tp")
    mine = lax.rem(band, group)
    base = band - mine
    others = [lax.rem(mine + d, group) for d in range(1, group)]
    greet([(base + other, tp) for other in others])
    local = keep(x_ref.at[mine], o_ref.at[mine], through, local_sem)
    copies = [
        pltpu.make_async_remote_copy(
            x_ref.at[other], o_ref.at[mine], send_sem.at[k], recv_sem.at[k],
            device_id=(base + other, tp), device_id_type=MESH,
        )
        for k, other in enumerate(others)
    ]
    for copy in copies:
        copy.start()
    for copy in [local(), *copies]:
        copy.wait()


def swap_heads(x, group, cid):
    return pl.pallas_call(
        functools.partial(heads_kernel, group),
        out_shape=jax.ShapeDtypeStruct(x.shape, x.dtype),
        in_specs=[pl.BlockSpec(memory_space=pl.ANY)],
        out_specs=pl.BlockSpec(memory_space=pl.ANY),
        scratch_shapes=[
            pltpu.VMEM(x.shape[1:], x.dtype),
            pltpu.SemaphoreType.DMA((2,)),
            pltpu.SemaphoreType.DMA((group - 1,)),
            pltpu.SemaphoreType.DMA((group - 1,)),
        ],
        compiler_params=pltpu.CompilerParams(collective_id=cid, has_side_effects=True),
        cost_estimate=takes(4),
        name="swap_heads",
    )(x)


def project_kernel(x_ref, w_ref, bias_ref, scale_ref, o_ref):
    total = nn(x_ref[...], w_ref[...]) + bias_ref[...]
    o_ref[0] = total.astype(bf16) * scale_ref[...].astype(bf16)


def project(x, weight, bias, scale, group):
    rows, depth = x.shape
    width = weight.shape[1] // group
    if width % 128:
        total = (nn(x, weight) + bias).astype(bf16) * scale.astype(bf16)
        return total.reshape(rows, group, width).transpose(1, 0, 2)
    block = min(256, rows)
    return pl.pallas_call(
        project_kernel,
        out_shape=jax.ShapeDtypeStruct((group, rows, width), bf16),
        grid=(group, rows // block),
        in_specs=[
            pl.BlockSpec((block, depth), lambda g, i: (i, 0)),
            pl.BlockSpec((depth, width), lambda g, i: (0, g)),
            pl.BlockSpec((1, width), lambda g, i: (0, g)),
            pl.BlockSpec((1, width), lambda g, i: (0, g)),
        ],
        out_specs=pl.BlockSpec((1, block, width), lambda g, i: (g, i, 0)),
        compiler_params=pltpu.CompilerParams(vmem_limit_bytes=40 * 2**20),
        cost_estimate=pl.CostEstimate(
            flops=2 * rows * depth * width * group, bytes_accessed=12 * 2**20, transcendentals=0
        ),
        name="project",
    )(x, weight, bias[None], scale[None])


def permitted(first, row, column, live_end):
    return (column >= first) & (column <= row) & ((column < live_end) | (column == row))


def head_mask(width, head, shape):
    lane = lax.broadcasted_iota(jnp.int32, shape, 1)
    return (lane >= head * HEAD_DIM) & (lane < (head + 1) * HEAD_DIM)


def attend_kernel(block, info_ref, first_ref, q_ref, k_ref, v_ref, o_ref, log_ref, vt_ref):
    length, width = q_ref.shape
    heads = width // HEAD_DIM
    live_end = info_ref[0]
    count = lax.div(live_end + block - 1, block)
    vt_ref[...] = v_ref[...].T
    o_ref[...] = jnp.zeros_like(o_ref)
    log_ref[...] = jnp.zeros_like(log_ref)

    def queries(i, _):
        rows = pl.ds(pl.multiple_of(i * block, block), block)
        q = q_ref[rows, :]
        first = first_ref[0:1, rows]
        row = i * block + lax.broadcasted_iota(jnp.int32, (1, block), 1)
        q_heads = [
            jnp.where(head_mask(width, h, (block, width)), q, jnp.zeros_like(q)) for h in range(heads)
        ]

        def keys(j, carry):
            columns = pl.ds(pl.multiple_of(j * block, block), block)
            k = k_ref[columns, :]
            column = j * block + lax.broadcasted_iota(jnp.int32, (block, 1), 0)
            allowed = permitted(first, row, column, live_end)
            out = []
            for h in range(heads):
                top, total, summed = carry[h]
                scores = jnp.where(allowed, nt(k, q_heads[h]), masked_score)
                new_top = jnp.maximum(top, jnp.max(scores, axis=0, keepdims=True))
                weights = jnp.exp(scores - new_top)
                scale = jnp.exp(top - new_top)
                total = total * scale + jnp.sum(weights, axis=0, keepdims=True)
                vt = vt_ref[h * HEAD_DIM : (h + 1) * HEAD_DIM, columns]
                summed = summed * scale + nn(vt, weights.astype(bf16))
                out.append((new_top, total, summed))
            return tuple(out)

        start = tuple(
            (
                jnp.full((1, block), masked_score, f32),
                jnp.zeros((1, block), f32),
                jnp.zeros((HEAD_DIM, block), f32),
            )
            for _ in range(heads)
        )
        done = lax.fori_loop(info_ref[1 + i], i + 1, keys, start)
        mixed = jnp.concatenate([summed / total for _, total, summed in done], axis=0)
        o_ref[rows, :] = mixed.T.astype(o_ref.dtype)
        for h, (top, total, _) in enumerate(done):
            log_ref[0, h : h + 1, rows] = top + jnp.log(total)
        return 0

    lax.fori_loop(0, count, queries, 0)


def attend_back_kernel(
    block, info_ref, first_ref, q_ref, k_ref, v_ref, o_ref, do_ref, log_ref, out_ref, dk_acc, dv_acc
):
    length, width = q_ref.shape
    heads = width // HEAD_DIM
    features = out_ref.shape[1] // 3
    slab = pl.program_id(0)
    factor = HEAD_DIM ** (-0.5)
    live_end = info_ref[0]
    count = lax.div(live_end + block - 1, block)

    def lanes(which):
        if features == width:
            return pl.ds(which * features, width)
        return pl.ds(pl.multiple_of(which * features + slab * width, width), width)

    dk_acc[...] = jnp.zeros_like(dk_acc)
    dv_acc[...] = jnp.zeros_like(dv_acc)
    out_ref[:, lanes(0)] = jnp.zeros((length, width), out_ref.dtype)

    def queries(i, _):
        rows = pl.ds(pl.multiple_of(i * block, block), block)
        q, do = q_ref[rows, :], do_ref[rows, :]
        first = first_ref[0:1, rows]
        row = i * block + lax.broadcasted_iota(jnp.int32, (1, block), 1)
        dots = (do.astype(f32) * o_ref[rows, :].astype(f32)).T
        masks = [head_mask(width, h, (block, width)) for h in range(heads)]
        zero = jnp.zeros_like(q)
        q_heads = [jnp.where(mask, q, zero) for mask in masks]
        do_heads = [jnp.where(mask, do, zero) for mask in masks]
        logs = [log_ref[0, h : h + 1, rows] for h in range(heads)]
        deltas = [
            jnp.sum(dots[h * HEAD_DIM : (h + 1) * HEAD_DIM], axis=0, keepdims=True)
            for h in range(heads)
        ]

        def keys(j, dq):
            columns = pl.ds(pl.multiple_of(j * block, block), block)
            k, v = k_ref[columns, :], v_ref[columns, :]
            column = j * block + lax.broadcasted_iota(jnp.int32, (block, 1), 0)
            allowed = permitted(first, row, column, live_end)
            dk, dv = dk_acc[columns, :], dv_acc[columns, :]
            for h in range(heads):
                scores = jnp.where(allowed, nt(k, q_heads[h]) - logs[h], masked_score)
                probs = jnp.exp(scores)
                prob_grad = nt(v, do_heads[h])
                score_grad = (probs * (prob_grad - deltas[h])).astype(bf16)
                dv = dv + nn(probs.astype(bf16), do_heads[h])
                dk = dk + nn(score_grad, q_heads[h])
                dq = dq + tn(score_grad, jnp.where(masks[h], k, zero))
            dk_acc[columns, :] = dk
            dv_acc[columns, :] = dv
            return dq

        dq = lax.fori_loop(info_ref[1 + i], i + 1, keys, jnp.zeros((block, width), f32))
        out_ref[rows, lanes(0)] = (dq * factor).astype(out_ref.dtype)
        return 0

    lax.fori_loop(0, count, queries, 0)
    out_ref[:, lanes(1)] = dk_acc[...].astype(out_ref.dtype)
    out_ref[:, lanes(2)] = dv_acc[...].astype(out_ref.dtype)


def attention_specs(length, features):
    width = min(128, features)
    slabs = features // width

    plain = pl.BlockSpec((length, width), lambda i, info: (0, i))

    def piece(which):
        if features % 128:
            return plain
        return pl.BlockSpec((length, width), lambda i, info, w=which: (0, w * slabs + i))

    logs = pl.BlockSpec((1, 8, length), lambda i, info: (i, 0, 0))
    first = pl.BlockSpec((1, length), lambda i, info: (0, 0))
    return width, slabs, piece, plain, logs, first


def three(qkv, features):
    if features % 128:
        return [qkv[:, w * features : (w + 1) * features] for w in range(3)]
    return [qkv] * 3


def attend(qkv, info, first, block):
    length, features = qkv.shape[0], qkv.shape[1] // 3
    width, slabs, piece, plain, logs, first_spec = attention_specs(length, features)
    return pl.pallas_call(
        functools.partial(attend_kernel, block),
        out_shape=(
            jax.ShapeDtypeStruct((length, features), bf16),
            jax.ShapeDtypeStruct((slabs, 8, length), f32),
        ),
        grid_spec=pltpu.PrefetchScalarGridSpec(
            num_scalar_prefetch=1,
            grid=(slabs,),
            in_specs=[first_spec, piece(0), piece(1), piece(2)],
            out_specs=(plain, logs),
            scratch_shapes=[pltpu.VMEM((width, length), bf16)],
        ),
        compiler_params=pltpu.CompilerParams(vmem_limit_bytes=40 * 2**20),
        cost_estimate=takes(36),
        name="attend",
    )(info, first, *three(qkv, features))


def attend_back(qkv, mixed, grad, log_total, info, first, block):
    length, features = qkv.shape[0], qkv.shape[1] // 3
    width, slabs, piece, plain, logs, first_spec = attention_specs(length, features)
    return pl.pallas_call(
        functools.partial(attend_back_kernel, block),
        out_shape=jax.ShapeDtypeStruct((length, 3 * features), bf16),
        grid_spec=pltpu.PrefetchScalarGridSpec(
            num_scalar_prefetch=1,
            grid=(slabs,),
            in_specs=[first_spec, piece(0), piece(1), piece(2), plain, plain, logs],
            out_specs=pl.BlockSpec((length, 3 * features), lambda i, info: (0, 0)),
            scratch_shapes=[pltpu.VMEM((length, width), f32), pltpu.VMEM((length, width), f32)],
        ),
        compiler_params=pltpu.CompilerParams(vmem_limit_bytes=40 * 2**20),
        cost_estimate=takes(40),
        name="attend_back",
    )(info, first, *three(qkv, features), mixed, grad, log_total)


def body(
    tokens,
    positions,
    doc_lengths,
    exit_depth,
    w_query,
    w_key,
    w_value,
    w_out,
    w_up,
    w_down,
    b_query,
    b_value,
    b_out,
    b_up,
    b_down,
    attn_gain,
    attn_bias,
    ffn_gain,
    ffn_bias,
    cotangent,
):
    seqs, local_rows, width = tokens.shape
    inner = b_query.shape[0]
    bands, tps = lax.axis_size("band"), lax.axis_size("tp")
    group = bands // seqs
    piece = local_rows // (group * tps)
    band, tp = lax.axis_index("band"), lax.axis_index("tp")
    seq, member = band // group, lax.rem(band, group)
    features = inner // group
    length = exit_depth.shape[1]
    own = bands * piece
    rows = tps * own
    block = min(256, length)

    def by_group(*parts):
        split = [p.reshape(p.shape[:-1] + (group, features)) for p in parts]
        return jnp.stack(split, axis=-2).reshape(parts[0].shape[:-1] + (-1,))

    def share(grad):
        return lax.psum_scatter(grad, "band", scatter_dimension=0, tiled=True)

    w_in = lax.all_gather(by_group(w_query, w_key, w_value), "band", axis=0, tiled=True)
    w_out_t = lax.all_gather(w_out.T, "band", axis=0, tiled=True)
    w_up_all = lax.all_gather(w_up, "band", axis=0, tiled=True)
    w_down_t = lax.all_gather(w_down.T, "band", axis=0, tiled=True)

    def my_share(array):
        split = array.reshape(seqs, group, tps, piece, width)
        return lax.dynamic_index_in_dim(split, tp, 2, keepdims=False).reshape(bands, piece, width)

    token_own, all_pos = swap_band(my_share(tokens), 0, positions)
    token_own, grad_own = lax.optimization_barrier((token_own, my_share(cotangent)))
    grad_own = lax.all_to_all(grad_own, "band", 0, 0)
    seq_pos = lax.dynamic_index_in_dim(all_pos, seq, 1, keepdims=False)
    seq_pos = seq_pos.reshape(bands, group, tps, piece).transpose(1, 2, 0, 3)
    row_pos = seq_pos.reshape(length)
    member_pos = lax.dynamic_index_in_dim(seq_pos, member, 0, keepdims=False)
    own_pos = lax.dynamic_index_in_dim(member_pos, tp, 0, keepdims=False).reshape(own)
    depths = lax.dynamic_index_in_dim(exit_depth, seq, 0, keepdims=False)
    live_end = jnp.sum((depths > LAYER).astype(jnp.int32))
    live_own = (own_pos < live_end).astype(f32)[:, None]
    ends = jnp.cumsum(lax.dynamic_index_in_dim(doc_lengths, seq, 0, keepdims=False))
    places = jnp.arange(length, dtype=jnp.int32)
    first = jnp.max(jnp.where(ends[:, None] <= places[None, :], ends[:, None], 0), axis=0)
    info = jnp.concatenate([live_end[None], first[::block] // block]).astype(jnp.int32)
    first = first[None, :].astype(jnp.int32)
    to_sorted = (row_pos[None, :] == places[:, None]).astype(bf16)
    to_rows = (row_pos[:, None] == places[None, :]).astype(bf16)

    inputs = token_own.reshape(own, width).astype(f32)
    normed_in, unit_in, inverse_in = layer_norm(inputs, attn_gain, attn_bias)
    z1 = gather_tp(normed_in.astype(bf16), 1).reshape(rows, width)


    bias_in = by_group(b_query, jnp.zeros_like(b_query), b_value)
    scale_in = by_group(
        jnp.full_like(b_query, HEAD_DIM ** (-0.5)), jnp.ones_like(b_query), jnp.ones_like(b_query)
    )
    qkv = project(z1, w_in, bias_in, scale_in, group)
    qkv = swap_heads(qkv, group, 4).reshape(length, 3 * features)
    qkv = nn(to_sorted, qkv).astype(bf16)
    qkv, grad_own = lax.optimization_barrier((qkv, grad_own))
    grad_own = grad_own.reshape(own, width).astype(f32)
    down_grad_own = (live_own * grad_own).astype(bf16)
    down_grad = gather_later(down_grad_own)
    mixed_sorted, log_total = attend(qkv, info, first, block)
    mixed_sorted, down_grad = lax.optimization_barrier((mixed_sorted, down_grad))
    down_grad = down_grad.reshape(rows, width)
    mixed = nn(to_rows, mixed_sorted).astype(bf16).reshape(group, rows, features)
    mixed = swap_heads(mixed, group, 5).transpose(1, 0, 2).reshape(rows, inner)

    attn_part = nt(mixed, w_out_t).astype(bf16).reshape(tps, own, width)
    attn_out = scatter_tp(attn_part, 6) + b_out
    residual = inputs + attn_out
    normed_mid, unit_mid, inverse_mid = layer_norm(residual, ffn_gain, ffn_bias)
    z2 = gather_tp(normed_mid.astype(bf16), 7).reshape(rows, width)
    pre_act = nn(z2, w_up_all) + b_up
    below = 0.5 * (1.0 + lax.erf(pre_act * 0.5**0.5))
    act = (pre_act * below).astype(bf16)
    slope = (below + pre_act * jnp.exp(-0.5 * pre_act * pre_act) * (2 * math.pi) ** -0.5).astype(bf16)

    ffn_part = nt(act, w_down_t).astype(bf16).reshape(tps, own, width)
    act, ffn_part = lax.optimization_barrier((act, ffn_part))
    ffn_part = lax.all_to_all(ffn_part, "tp", 0, 0)
    grad_w_down_t = tn(down_grad, act).astype(bf16)
    up_grad = (nn(down_grad, w_down_t) * slope.astype(f32)).astype(bf16)
    up_grad, grad_w_down_t = lax.optimization_barrier((up_grad, grad_w_down_t))
    shared_down = share(grad_w_down_t)
    grad_w_up = tn(z2, up_grad).astype(bf16)
    mid_part = nt(up_grad, w_up_all).astype(bf16).reshape(tps, own, width)
    mid_part, ffn_part = lax.optimization_barrier((mid_part, ffn_part))
    ffn_out = jnp.sum(ffn_part.astype(f32), axis=0) + b_down
    output_own = (inputs + live_own * (attn_out + ffn_out)).astype(bf16)
    output = lax.all_to_all(output_own.reshape(bands, piece, width), "band", 0, 0)
    mid_grad = scatter_tp(mid_part, 8)
    resid_grad = norm_back(mid_grad, unit_mid, inverse_mid, ffn_gain)
    attn_grad_own = (live_own * grad_own + resid_grad).astype(bf16)
    attn_grad = gather_tp(attn_grad_own, 9).reshape(rows, width)
    attn_grad, grad_w_up, output = lax.optimization_barrier((attn_grad, grad_w_up, output))
    output = gather_later(output)


    grad_w_out_t = tn(attn_grad, mixed).astype(bf16)
    mixed_grad = nn(attn_grad, w_out_t).astype(bf16)
    mixed_grad = mixed_grad.reshape(rows, group, features).transpose(1, 0, 2)
    mixed_grad = swap_heads(mixed_grad, group, 13).reshape(length, features)
    mixed_grad = nn(to_sorted, mixed_grad).astype(bf16)
    grad_w_up, shared_down = lax.optimization_barrier((grad_w_up, shared_down))
    shared_up = share(grad_w_up)
    mixed_grad, grad_w_out_t = lax.optimization_barrier((mixed_grad, grad_w_out_t))
    in_grad = attend_back(qkv, mixed_sorted, mixed_grad, log_total, info, first, block)
    shared_up, grad_w_out_t = lax.optimization_barrier((shared_up, grad_w_out_t))
    shared_out = share(grad_w_out_t)
    in_grad, output = lax.optimization_barrier((in_grad, output))
    output = output.transpose(1, 0, 2, 3).reshape(tokens.shape)
    in_grad = nn(to_rows, in_grad).astype(bf16).reshape(group, rows, 3 * features)
    in_grad = swap_heads(in_grad, group, 14).transpose(1, 0, 2).reshape(rows, 3 * inner)
    grad_w_in = tn(z1, in_grad).astype(bf16)
    in_part = nt(in_grad, w_in).astype(bf16).reshape(tps, own, width)
    input_grad = scatter_tp(in_part, 15)
    token_grad = grad_own + resid_grad + norm_back(input_grad, unit_in, inverse_in, attn_gain)

    def over_rows(array):
        return jnp.sum(array.astype(f32), axis=0)

    wide = [
        over_rows(attn_grad_own),
        over_rows(down_grad_own),
        over_rows(input_grad * unit_in),
        over_rows(input_grad),
        over_rows(mid_grad * unit_mid),
        over_rows(mid_grad),
    ]
    in_sums = over_rows(in_grad).reshape(group, 3, features)
    narrow = [in_sums[:, 0].reshape(-1), in_sums[:, 2].reshape(-1), over_rows(up_grad)]
    small = jnp.concatenate(wide + narrow)
    count = small.shape[0]
    small = jnp.pad(small, (0, -count % 2048)).astype(bf16).reshape(16, -1)
    token_grad, small = swap_band(token_grad.astype(bf16).reshape(bands, piece, width), 16, small)
    small = jnp.sum(small.astype(f32), axis=0).reshape(-1)
    narrow = small[6 * width : count]
    token_grad, wide = gather_tp(token_grad, 17, True, small[: 6 * width].reshape(-1, width))
    token_grad = token_grad.reshape(tokens.shape).astype(f32)
    grad_w_in, shared_out = lax.optimization_barrier((grad_w_in, shared_out))
    shared_in = share(grad_w_in).astype(f32).reshape(-1, group, 3, features)
    shared_down, shared_out = shared_down.astype(f32).T, shared_out.astype(f32).T
    shared_up = shared_up.astype(f32)
    shared_q, shared_k, shared_v = (
        shared_in[:, :, which].reshape(-1, inner) for which in range(3)
    )

    return (
        output,
        token_grad,
        shared_q,
        shared_k,
        shared_v,
        shared_out,
        shared_up,
        shared_down,
        narrow[:inner],
        narrow[inner : 2 * inner],
        wide[0],
        narrow[2 * inner :],
        wide[1],
        wide[2],
        wide[3],
        wide[4],
        wide[5],
    )


def solution(mesh):
    return jax.shard_map(
        body,
        mesh=mesh,
        in_specs=(
            P(None, "band", None),
            P(None, "band"),
            P(),
            P(),
            P("band", "tp"),
            P("band", "tp"),
            P("band", "tp"),
            P("tp", "band"),
            P("band", "tp"),
            P("tp", "band"),
            P("tp"),
            P("tp"),
            P(),
            P("tp"),
            P(),
            P(),
            P(),
            P(),
            P(),
            P(None, "band", None),
        ),
        out_specs=(
            P(None, "band", None),
            P(None, "band", None),
            P("band", "tp"),
            P("band", "tp"),
            P("band", "tp"),
            P("tp", "band"),
            P("band", "tp"),
            P("tp", "band"),
            P("tp"),
            P("tp"),
            P(),
            P("tp"),
            P(),
            P(),
            P(),
            P(),
            P(),
        ),
        check_vma=False,
    )
```

```python
import functools
import math

import jax
import jax.numpy as jnp
from jax import lax
from jax.experimental import pallas as pl
from jax.experimental.pallas import tpu as pltpu
from jax.sharding import PartitionSpec as P

HEAD_DIM = 64
LAYER = 12
MESH = pl.DeviceIdType.MESH

epsilon = 1e-05
masked_score = -1e30
bf16 = jnp.bfloat16
f32 = jnp.float32


def layer_norm(values, gain, shift):
    center = values - jnp.mean(values, axis=-1, keepdims=True)
    inverse = lax.rsqrt(jnp.mean(center * center, axis=-1, keepdims=True) + epsilon)
    normed = center * inverse
    return (normed * gain + shift, normed, inverse)


def norm_back(grad_out, normed, inverse, gain):
    scaled = grad_out * gain
    return inverse * (
        scaled
        - jnp.mean(scaled, axis=-1, keepdims=True)
        - normed * jnp.mean(scaled * normed, axis=-1, keepdims=True)
    )


def nn(left, right):
    return jnp.dot(left, right, preferred_element_type=f32)


def nt(left, right):
    return lax.dot_general(left, right, (((1,), (1,)), ((), ())), preferred_element_type=f32)


def tn(left, right):
    return lax.dot_general(left, right, (((0,), (0,)), ((), ())), preferred_element_type=f32)


def gelu_exact(values):
    return jax.nn.gelu(values, approximate=False)


def halves(count):
    return (count // 2, 2) if count % 2 == 0 else (count, 1)


def takes(microseconds):
    return pl.CostEstimate(
        flops=int(microseconds * 1e9), bytes_accessed=int(microseconds * 2e6), transcendentals=0
    )


class Sems:
    def __init__(self, send_sem, recv_sem, local_sem):
        self.send_sem, self.recv_sem, self.local_sem = send_sem, recv_sem, local_sem
        self.sent = self.local = 0

    def send(self, source, target, device):
        k = self.sent
        self.sent += 1
        copy = pltpu.make_async_remote_copy(
            source, target, self.send_sem.at[k], self.recv_sem.at[k],
            device_id=device, device_id_type=MESH,
        )
        copy.start()
        return copy

    def copy(self, source, target):
        k = self.local
        self.local += 1
        copy = pltpu.make_async_copy(source, target, self.local_sem.at[k])
        copy.start()
        return copy


class Grid:
    def __init__(self, count):
        self.na, self.nb = na, nb = halves(count)
        self.me, band = lax.axis_index("tp"), lax.axis_index("band")
        self.a, self.b = a, b = self.me // nb, lax.rem(self.me, nb)
        self.along_b = [(band, a * nb + lax.rem(b + d, nb)) for d in range(1, nb)]
        self.along_a = [(band, lax.rem(a + d, na) * nb + b) for d in range(1, na)]
        self.from_b = [a * nb + lax.rem(b + nb - d, nb) for d in range(1, nb)]
        self.from_a = [lax.rem(a + na - d, na) * nb + b for d in range(1, na)]


def tp_peers():
    grid = Grid(lax.axis_size("tp"))
    return grid.along_a + grid.along_b


def band_peers():
    size = lax.axis_size("band")
    me, tp = lax.axis_index("band"), lax.axis_index("tp")
    return [(lax.rem(me + d, size), tp) for d in range(1, size)]


anywhere = pl.BlockSpec(memory_space=pl.ANY)
vmem = pl.BlockSpec(memory_space=pltpu.VMEM)


class Gather:
    peers = "tp"

    def __init__(self, x, inner_slot=False, extra=None):
        self.count = count = lax.axis_size("tp")
        na, nb = halves(count)
        self.inner_slot, self.extra = inner_slot, extra is not None
        self.sends = 2 * (na - 1 + nb - 1) + 2 * (na - 1) * (nb - 1)
        self.locals = 2
        shape = (x.shape[0], count) + x.shape[1:] if inner_slot else (count,) + x.shape
        self.operands, self.in_specs = [x], [anywhere]
        self.shapes, self.out_specs = [jax.ShapeDtypeStruct(shape, x.dtype)], [anywhere]
        self.scratch = [pltpu.VMEM(x.shape, x.dtype)]
        if self.extra:
            self.operands.append(extra)
            self.in_specs.append(vmem)
            self.shapes.append(jax.ShapeDtypeStruct(extra.shape, extra.dtype))
            self.out_specs.append(vmem)
            self.sends += na - 1 + nb - 1
            self.scratch += [
                pltpu.VMEM(extra.shape, extra.dtype),
                pltpu.VMEM((max(nb - 1, 1),) + extra.shape, extra.dtype),
                pltpu.VMEM((max(na - 1, 1),) + extra.shape, extra.dtype),
            ]

    def slot(self, index, which):
        part = self.part[which]
        return self.out.at[part, index] if self.inner_slot else self.out.at[index, part]

    def begin(self, ins, outs, scratch, sems):
        self.grid = grid = Grid(self.count)
        self.sems = sems
        x, self.out = ins[0], outs[0]
        half = x.shape[0] // 2
        self.part = part = (pl.ds(0, half), pl.ds(half, half))
        self.through = scratch[0]
        self.load = sems.copy(x, self.through)
        me = grid.me
        if self.extra:
            self.more = (ins[1], outs[1], *scratch[1:])
            self.extra_b = [
                sems.send(ins[1], scratch[2].at[k], device) for k, device in enumerate(grid.along_b)
            ]
        top, low = x.at[part[0]], x.at[part[1]]
        self.first_b = [sems.send(top, self.slot(me, 0), device) for device in grid.along_b]
        self.first_a = [sems.send(low, self.slot(me, 1), device) for device in grid.along_a]
        self.second = [sems.send(top, self.slot(me, 0), device) for device in grid.along_a]
        self.second += [sems.send(low, self.slot(me, 1), device) for device in grid.along_b]

    def middle(self):
        grid, sems = self.grid, self.sems
        self.load.wait()
        whole = self.out.at[:, grid.me] if self.inner_slot else self.out.at[grid.me]
        self.store = sems.copy(self.through, whole)
        if self.extra:
            own, _, part_ref, in_b, in_a = self.more
            total = own[...]
            for k, copy in enumerate(self.extra_b):
                copy.wait_recv()
                total = total + in_b[k]
            part_ref[...] = total
            self.extra_a = [
                sems.send(part_ref, in_a.at[k], device) for k, device in enumerate(grid.along_a)
            ]
        for copy, source in zip(self.first_b, grid.from_b):
            copy.wait_recv()
            held = self.slot(source, 0)
            self.second += [sems.send(held, held, device) for device in grid.along_a]
        for copy, source in zip(self.first_a, grid.from_a):
            copy.wait_recv()
            held = self.slot(source, 1)
            self.second += [sems.send(held, held, device) for device in grid.along_b]

    def end(self):
        if self.extra:
            _, total_ref, part_ref, _, in_a = self.more
            total = part_ref[...]
            for k, copy in enumerate(self.extra_a):
                copy.wait_recv()
                total = total + in_a[k]
            total_ref[...] = total
            for copy in self.extra_a + self.extra_b:
                copy.wait_send()
        for copy in self.first_a + self.first_b:
            copy.wait_send()
        for copy in self.second:
            copy.wait()
        self.store.wait()


class Scatter:
    peers = "tp"

    def __init__(self, partial):
        self.count, rows, width = partial.shape
        na, nb = halves(self.count)
        block = (rows // 2, width)
        self.sends = 2 * (na - 1) * (nb - 1) + 2 * (na - 1 + nb - 1)
        self.locals = na + nb
        self.operands, self.in_specs = [partial], [anywhere]
        self.shapes, self.out_specs = [jax.ShapeDtypeStruct((rows, width), f32)], [vmem]

        def buffer(*lead):
            return pltpu.VMEM(tuple(max(n, 1) for n in lead) + block, partial.dtype)

        self.scratch = [
            buffer(na), buffer(nb), buffer(nb - 1, na), buffer(na - 1, nb),
            buffer(na - 1), buffer(nb - 1), buffer(na - 1), buffer(nb - 1),
        ]

    def begin(self, ins, outs, scratch, sems):
        self.grid = grid = Grid(self.count)
        self.sems, self.out, self.scratch_refs = sems, outs[0], scratch
        own_a, own_b, one_a, one_b = scratch[:4]
        part = ins[0]
        na, nb, a, b = grid.na, grid.nb, grid.a, grid.b
        half = part.shape[1] // 2
        self.top, self.low = top, low = pl.ds(0, half), pl.ds(half, half)
        self.order_a = order_a = list(range(1, na)) + [0]
        self.order_b = order_b = list(range(1, nb)) + [0]
        self.first_a, self.first_b = {}, {}
        for step in range(max(na, nb)):
            if step < na:
                e = order_a[step]
                row = lax.rem(a + e, na) * nb
                for d in range(1, nb):
                    source = part.at[row + lax.rem(b + d, nb), top]
                    self.first_b[d, e] = sems.send(source, one_a.at[d - 1, e], grid.along_b[d - 1])
            if step < nb:
                e = order_b[step]
                column = lax.rem(b + e, nb)
                for d in range(1, na):
                    source = part.at[lax.rem(a + d, na) * nb + column, low]
                    self.first_a[d, e] = sems.send(source, one_b.at[d - 1, e], grid.along_a[d - 1])
        self.local_a = {
            e: sems.copy(part.at[lax.rem(a + e, na) * nb + b, top], own_a.at[e]) for e in order_a
        }
        self.local_b = {
            e: sems.copy(part.at[a * nb + lax.rem(b + e, nb), low], own_b.at[e]) for e in order_b
        }

    def sum_a(self, e):
        own_a, _, one_a = self.scratch_refs[:3]
        self.local_a[e].wait()
        total = own_a[e].astype(f32)
        for d in range(1, self.grid.nb):
            self.first_b[d, e].wait_recv()
            total = total + one_a[d - 1, e].astype(f32)
        return total

    def sum_b(self, e):
        _, own_b, _, one_b = self.scratch_refs[:4]
        self.local_b[e].wait()
        total = own_b[e].astype(f32)
        for d in range(1, self.grid.na):
            self.first_a[d, e].wait_recv()
            total = total + one_b[d - 1, e].astype(f32)
        return total

    def middle(self):
        grid, sems = self.grid, self.sems
        out_a, out_b, two_a, two_b = self.scratch_refs[4:]
        self.second_a, self.second_b = {}, {}
        for e in self.order_a[:-1]:
            out_a[e - 1] = self.sum_a(e).astype(out_a.dtype)
            self.second_a[e] = sems.send(out_a.at[e - 1], two_a.at[e - 1], grid.along_a[e - 1])
        for e in self.order_b[:-1]:
            out_b[e - 1] = self.sum_b(e).astype(out_b.dtype)
            self.second_b[e] = sems.send(out_b.at[e - 1], two_b.at[e - 1], grid.along_b[e - 1])

    def end(self):
        _, _, two_a, two_b = self.scratch_refs[4:]
        total = self.sum_a(0)
        for e in self.order_a[:-1]:
            self.second_a[e].wait_recv()
            total = total + two_a[e - 1].astype(f32)
        self.out[self.top] = total
        total = self.sum_b(0)
        for e in self.order_b[:-1]:
            self.second_b[e].wait_recv()
            total = total + two_b[e - 1].astype(f32)
        self.out[self.low] = total
        for group in (self.first_a, self.first_b, self.second_a, self.second_b):
            for copy in group.values():
                copy.wait_send()


class Swap:
    peers = "band"

    def __init__(self, x, extra=None):
        size = lax.axis_size("band")
        arrays = [x] if extra is None else [x, extra]
        self.operands, self.in_specs = arrays, [anywhere] * len(arrays)
        self.shapes = [jax.ShapeDtypeStruct(x.shape, x.dtype)]
        self.scratch = [pltpu.VMEM(x.shape[1:], x.dtype)]
        if extra is not None:
            self.shapes.append(jax.ShapeDtypeStruct((size,) + extra.shape, extra.dtype))
            self.scratch.append(pltpu.VMEM(extra.shape, extra.dtype))
        self.out_specs = [anywhere] * len(arrays)
        self.sends = (size - 1) * len(arrays)
        self.locals = 2 * len(arrays)

    def begin(self, ins, outs, scratch, sems):
        me = lax.axis_index("band")
        self.sems, self.scratch_refs = sems, scratch
        self.slots = [out.at[me] for out in outs]
        self.loads = [sems.copy(ins[0].at[me], scratch[0])]
        if len(ins) > 1:
            self.loads.append(sems.copy(ins[1], scratch[1]))
        self.copies = []
        for peer in band_peers():
            if len(ins) > 1:
                self.copies.append(sems.send(ins[1], self.slots[1], peer))
            self.copies.append(sems.send(ins[0].at[peer[0]], self.slots[0], peer))

    def middle(self):
        self.stores = []
        for load, through, slot in zip(self.loads, self.scratch_refs, self.slots):
            load.wait()
            self.stores.append(self.sems.copy(through, slot))

    def end(self):
        for copy in self.copies + self.stores:
            copy.wait()


class Work:
    def __init__(self, operands, tasks, early):
        self.tasks, self.early = tasks, early
        self.operands = operands
        self.shapes = []
        for kind, left, right, _, _ in tasks:
            if kind == "sum":
                self.shapes.append(jax.ShapeDtypeStruct((1, operands[left].shape[1]), f32))
                continue
            rows = operands[left].shape[1 if kind == "tn" else 0]
            self.shapes.append(jax.ShapeDtypeStruct((rows, operands[right].shape[1]), bf16))
        self.scratch = [pltpu.VMEM(x.shape, x.dtype) for x in [*operands, *self.shapes]]
        self.locals = len(operands) + len(tasks)

    def begin(self, ins, outs, scratch, sems):
        self.sems, self.outs = sems, outs
        self.held, self.made = scratch[: len(ins)], scratch[len(ins) :]
        self.loads = [sems.copy(source, target) for source, target in zip(ins, self.held)]
        self.stores = []

    def ready(self, k):
        if self.loads[k] is not None:
            self.loads[k].wait()
            self.loads[k] = None

    def run(self, tasks):
        for kind, left, right, scale, out in tasks:
            for k in (left, right, scale):
                if k is not None:
                    self.ready(k)
            x, made = self.held[left], self.made[out]
            if kind == "sum":
                rows = min(128, x.shape[0])
                made[...] = jnp.zeros_like(made)

                def add(k, _, x=x, made=made, rows=rows):
                    r = pl.ds(pl.multiple_of(k * rows, rows), rows)
                    made[...] += jnp.sum(x[r, :].astype(f32), axis=0, keepdims=True)
                    return 0

                lax.fori_loop(0, x.shape[0] // rows, add, 0)
                self.stores.append(self.sems.copy(made, self.outs[out]))
                continue
            y = self.held[right]
            factor = None if scale is None else self.held[scale]
            tile_r, tile_c = min(512, made.shape[0]), min(512, made.shape[1])
            columns = made.shape[1] // tile_c

            def tile(k, _, kind=kind, x=x, y=y, made=made, factor=factor):
                i, j = k // columns, lax.rem(k, columns)
                r = pl.ds(pl.multiple_of(i * tile_r, tile_r), tile_r)
                c = pl.ds(pl.multiple_of(j * tile_c, tile_c), tile_c)
                total = tn(x[:, r], y[:, c]) if kind == "tn" else nn(x[r, :], y[:, c])
                if factor is not None:
                    total = total * factor[r, c].astype(f32)
                made[r, c] = total.astype(made.dtype)
                return 0

            lax.fori_loop(0, (made.shape[0] // tile_r) * columns, tile, 0)
            self.stores.append(self.sems.copy(made, self.outs[out]))

    def end(self):
        for store in self.stores:
            store.wait()


def transfer(parts, cid, work=None, name="transfer", time=36):
    items = list(parts) + ([work] if work is not None else [])
    sends = sum(part.sends for part in parts)
    locals_ = sum(item.locals for item in items)

    def kernel(*refs):
        refs = list(refs)

        def take(number):
            taken = refs[:number]
            del refs[:number]
            return taken

        ins = [take(len(item.operands)) for item in items]
        outs = [take(len(item.shapes)) for item in items]
        scratch = [take(len(item.scratch)) for item in items]
        sems = Sems(*refs)
        devices = []
        if any(part.peers == "tp" for part in parts):
            devices += tp_peers()
        if any(part.peers == "band" for part in parts):
            devices += band_peers()
        barrier = pltpu.get_barrier_semaphore()
        for device in devices:
            pl.semaphore_signal(barrier, inc=1, device_id=device, device_id_type=MESH)
        if work is not None:
            work.begin(ins[-1], outs[-1], scratch[-1], sems)
        pl.semaphore_wait(barrier, len(devices))
        for part, i, o, t in zip(parts, ins, outs, scratch):
            part.begin(i, o, t, sems)
        if work is not None:
            work.run(work.tasks[: work.early])
        for part in parts:
            part.middle()
        if work is not None:
            work.run(work.tasks[work.early :])
        for part in parts:
            part.end()
        if work is not None:
            work.end()

    in_specs = [spec for part in parts for spec in part.in_specs]
    out_specs = [spec for part in parts for spec in part.out_specs]
    if work is not None:
        in_specs += [anywhere] * len(work.operands)
        out_specs += [anywhere] * len(work.shapes)
    return pl.pallas_call(
        kernel,
        out_shape=tuple(shape for item in items for shape in item.shapes),
        in_specs=in_specs,
        out_specs=tuple(out_specs),
        scratch_shapes=[
            *(scratch for item in items for scratch in item.scratch),
            pltpu.SemaphoreType.DMA((sends,)),
            pltpu.SemaphoreType.DMA((sends,)),
            pltpu.SemaphoreType.DMA((locals_,)),
        ],
        compiler_params=pltpu.CompilerParams(
            collective_id=cid, has_side_effects=True, vmem_limit_bytes=(56 if work else 32) * 2**20
        ),
        cost_estimate=takes(time),
        name=name,
    )(*(operand for item in items for operand in item.operands))


def gather_later(x):
    count = lax.axis_size("tp")
    return lax.all_to_all(jnp.broadcast_to(x[None], (count,) + x.shape), "tp", 0, 0)


class Block:
    def __init__(self, order, shift, grid, size):
        band = lax.axis_index("band")
        self.order, self.shift = order, shift
        self.to, self.source = lax.rem(band + shift, size), lax.rem(band + size - shift, size)
        if order % 2 == 0:
            self.n1, self.n2 = grid.nb, grid.na
            self.first, self.second, self.origin = grid.along_b, grid.along_a, grid.from_b
            self.index = lambda d, e: lax.rem(grid.a + e, grid.na) * grid.nb + lax.rem(
                grid.b + d, grid.nb
            )
        else:
            self.n1, self.n2 = grid.na, grid.nb
            self.first, self.second, self.origin = grid.along_a, grid.along_b, grid.from_a
            self.index = lambda d, e: lax.rem(grid.a + d, grid.na) * grid.nb + lax.rem(
                grid.b + e, grid.nb
            )


def finish_kernel(
    count, size, part, unit, above, resid, inverse, gain, wide, narrow,
    out, wide_out, narrow_out,
    own, one, two_out, two, made, arrived, late, late_in, wide_in, narrow_in, pair, pair_b, pair_a,
    send_sem, recv_sem, local_sem,
):
    grid = Grid(count)
    sems = Sems(send_sem, recv_sem, local_sem)
    band = lax.axis_index("band")
    peers = band_peers()
    devices = grid.along_a + grid.along_b + peers
    barrier = pltpu.get_barrier_semaphore()
    for device in devices:
        pl.semaphore_signal(barrier, inc=1, device_id=device, device_id_type=MESH)
    shifts = list(range(1, size)) + [0]
    blocks = [Block(k, shift, grid, size) for k, shift in enumerate(shifts)]
    late[...] = jnp.zeros_like(late)
    pl.semaphore_wait(barrier, len(devices))
    done = []

    for blk in blocks:
        k = blk.order
        seconds = list(range(1, blk.n2)) + [0]
        blk.one = {
            (d, e): sems.send(
                part.at[blk.index(d, e), blk.to], one.at[k, d - 1, e], blk.first[d - 1]
            )
            for e in seconds
            for d in range(1, blk.n1)
        }
        blk.own = {e: sems.copy(part.at[blk.index(0, e), blk.to], own.at[k, e]) for e in seconds}
    early = []
    for peer in peers:
        early.append(sems.send(wide, wide_in.at[band], peer))
        early.append(sems.send(narrow, narrow_in.at[band], peer))

    def first_sum(blk, e):
        k = blk.order
        blk.own[e].wait()
        total = own[k, e].astype(f32)
        for d in range(1, blk.n1):
            blk.one[d, e].wait_recv()
            total = total + one[k, d - 1, e].astype(f32)
        return total

    def pass_on(blk):
        k = blk.order
        blk.two = []
        for e in range(1, blk.n2):
            two_out[k, e - 1] = first_sum(blk, e).astype(bf16)
            blk.two.append(sems.send(two_out.at[k, e - 1], two.at[k, e - 1], blk.second[e - 1]))

    def complete(blk):
        k = blk.order
        grad = first_sum(blk, 0)
        for e, copy in enumerate(blk.two):
            copy.wait_recv()
            grad = grad + two[k, e].astype(f32)
        normed = unit[blk.to]
        scaled = grad * gain[...]
        mean = jnp.mean(scaled, axis=-1, keepdims=True)
        along = jnp.mean(scaled * normed, axis=-1, keepdims=True)
        base = above[blk.to].astype(f32) + resid[blk.to]
        token = base + inverse[blk.to] * (scaled - mean - normed * along)
        made[k] = token.astype(bf16)
        sums = (jnp.sum(grad * normed, axis=0, keepdims=True), jnp.sum(grad, axis=0, keepdims=True))
        quarter = late.shape[1]
        for which, total in enumerate(sums):
            for i in range(4):
                row = slice(4 * which + i, 4 * which + i + 1)
                late[row, :] = late[row, :] + total[:, i * quarter : (i + 1) * quarter]
        if blk.shift:
            blk.swap = sems.send(made.at[k], arrived.at[k], (blk.to, lax.axis_index("tp")))

    def relay(blk):
        k = blk.order
        if blk.shift:
            blk.swap.wait_recv()
            held = arrived.at[k]
        else:
            held = made.at[k]
        slot = out.at[blk.source, grid.me]
        blk.near = [sems.send(held, slot, device) for device in blk.first]
        blk.far = [sems.send(held, slot, device) for device in blk.second]
        done.append(sems.copy(held, slot))

    def forward(blk):
        for copy, source in zip(blk.near, blk.origin):
            copy.wait_recv()
            held = out.at[blk.source, source]
            blk.far += [sems.send(held, held, device) for device in blk.second]

    pairs = [blocks[k : k + 2] for k in range(0, size, 2)]
    stages = (pass_on, complete, relay, forward)
    for step in range(len(pairs) + len(stages) - 1):
        for behind, stage in enumerate(stages):
            if 0 <= step - behind < len(pairs):
                for blk in pairs[step - behind]:
                    stage(blk)
        if step == len(pairs):
            last = [sems.send(late, late_in.at[band], peer) for peer in peers]

    for copy in early + last:
        copy.wait_recv()
    wide_in[band] = wide[...]
    narrow_in[band] = narrow[...]
    late_in[band] = late[...]
    total, narrow_total, late_total = (
        sum(array[k].astype(f32) for k in range(size)) for array in (wide_in, narrow_in, late_in)
    )
    narrow_out[...] = narrow_total
    pair[0:16, :] = total
    pair[16:24, :] = late_total
    near = [sems.send(pair, pair_b.at[k], device) for k, device in enumerate(grid.along_b)]
    total = pair[...]
    for k, copy in enumerate(near):
        copy.wait_recv()
        total = total + pair_b[k]
    for copy in near:
        copy.wait_send()
    pair[...] = total
    far = [sems.send(pair, pair_a.at[k], device) for k, device in enumerate(grid.along_a)]
    for k, copy in enumerate(far):
        copy.wait_recv()
        total = total + pair_a[k]
    wide_out[...] = total

    for copy in early + last + far:
        copy.wait_send()
    for blk in blocks:
        for copy in [*blk.one.values(), *blk.two, *blk.near]:
            copy.wait_send()
        if blk.shift:
            blk.swap.wait_send()
        for copy in blk.far:
            copy.wait()
    for copy in done:
        copy.wait()


def finish(part, unit, above, resid, inverse, gain, wide, narrow, cid):
    count, size, rows, width = part.shape
    na, nb = halves(count)
    most = max(na, nb)
    sends = locals_ = 0
    for k in range(size):
        n1, n2 = (nb, na) if k % 2 == 0 else (na, nb)
        sends += (n1 - 1) * n2 + 2 * (n2 - 1) + (n1 - 1) + (n1 - 1) * (n2 - 1)
        locals_ += n2 + 1
    sends += 4 * (size - 1) + na - 1 + nb - 1
    lanes = wide.shape[1]

    def blocks(*lead):
        return pltpu.VMEM(tuple(max(n, 1) for n in lead) + (rows, width), bf16)

    return pl.pallas_call(
        functools.partial(finish_kernel, count, size),
        out_shape=(
            jax.ShapeDtypeStruct((size, count, rows, width), bf16),
            jax.ShapeDtypeStruct((24, lanes), f32),
            jax.ShapeDtypeStruct(narrow.shape, f32),
        ),
        in_specs=[anywhere] + [vmem] * 7,
        out_specs=(anywhere, vmem, vmem),
        scratch_shapes=[
            blocks(size, most), blocks(size, most - 1, most),
            blocks(size, most - 1), blocks(size, most - 1),
            blocks(size), blocks(size),
            pltpu.VMEM((8, lanes), f32),
            pltpu.VMEM((size, 8, lanes), f32),
            pltpu.VMEM((size,) + wide.shape, bf16),
            pltpu.VMEM((size,) + narrow.shape, bf16),
            pltpu.VMEM((24, lanes), f32),
            pltpu.VMEM((max(nb - 1, 1), 24, lanes), f32),
            pltpu.VMEM((max(na - 1, 1), 24, lanes), f32),
            pltpu.SemaphoreType.DMA((sends,)),
            pltpu.SemaphoreType.DMA((sends,)),
            pltpu.SemaphoreType.DMA((locals_,)),
        ],
        compiler_params=pltpu.CompilerParams(
            collective_id=cid, has_side_effects=True, vmem_limit_bytes=48 * 2**20
        ),
        cost_estimate=takes(90),
        name="finish",
    )(part, unit, above, resid, inverse, gain, wide, narrow)


def heads_kernel(group, kind, x_ref, o_ref, through, local_sem, send_sem, recv_sem):
    band, tp = lax.axis_index("band"), lax.axis_index("tp")
    mine = lax.rem(band, group)
    base = band - mine
    others = [lax.rem(mine + d, group) for d in range(1, group)]
    sems = Sems(send_sem, recv_sem, local_sem)
    width = through.shape[1]

    def columns(index):
        return pl.ds(pl.multiple_of(index * width, width), width)

    def source(index):
        return x_ref.at[:, columns(index)] if kind == "cut" else x_ref.at[index]

    target = o_ref.at[:, columns(mine)] if kind == "join" else o_ref.at[mine]
    barrier = pltpu.get_barrier_semaphore()
    for other in others:
        pl.semaphore_signal(barrier, inc=1, device_id=(base + other, tp), device_id_type=MESH)
    load = sems.copy(source(mine), through)
    pl.semaphore_wait(barrier, group - 1)
    copies = [sems.send(source(other), target, (base + other, tp)) for other in others]
    load.wait()
    for copy in [sems.copy(through, target), *copies]:
        copy.wait()


def swap_heads(x, group, cid, kind):
    if kind == "cut":
        rows, width = x.shape[0], x.shape[1] // group
    else:
        rows, width = x.shape[1:]
    if width % 128 and kind == "cut":
        x = x.reshape(rows, group, width).transpose(1, 0, 2)
        return swap_heads(x, group, cid, "plain")
    if width % 128 and kind == "join":
        x = swap_heads(x, group, cid, "plain")
        return x.transpose(1, 0, 2).reshape(rows, group * width)
    shape = (rows, group * width) if kind == "join" else (group, rows, width)
    return pl.pallas_call(
        functools.partial(heads_kernel, group, kind),
        out_shape=jax.ShapeDtypeStruct(shape, x.dtype),
        in_specs=[anywhere],
        out_specs=anywhere,
        scratch_shapes=[
            pltpu.VMEM((rows, width), x.dtype),
            pltpu.SemaphoreType.DMA((2,)),
            pltpu.SemaphoreType.DMA((group - 1,)),
            pltpu.SemaphoreType.DMA((group - 1,)),
        ],
        compiler_params=pltpu.CompilerParams(collective_id=cid, has_side_effects=True),
        cost_estimate=takes(4),
        name="swap_heads",
    )(x)


def project_kernel(x_ref, w_ref, bias_ref, scale_ref, o_ref):
    total = nn(x_ref[...], w_ref[...]) + bias_ref[...]
    o_ref[0] = total.astype(bf16) * scale_ref[...].astype(bf16)


def project(x, weight, bias, scale, group):
    rows, depth = x.shape
    total_width = bias.shape[0]
    width = total_width // group
    if width % 128:
        total = (nn(x, weight[:, :total_width]) + bias).astype(bf16) * scale.astype(bf16)
        return total.reshape(rows, group, width).transpose(1, 0, 2)
    block = min(256, rows)
    return pl.pallas_call(
        project_kernel,
        out_shape=jax.ShapeDtypeStruct((group, rows, width), bf16),
        grid=(group, rows // block),
        in_specs=[
            pl.BlockSpec((block, depth), lambda g, i: (i, 0)),
            pl.BlockSpec((depth, width), lambda g, i: (0, g)),
            pl.BlockSpec((1, width), lambda g, i: (0, g)),
            pl.BlockSpec((1, width), lambda g, i: (0, g)),
        ],
        out_specs=pl.BlockSpec((1, block, width), lambda g, i: (g, i, 0)),
        compiler_params=pltpu.CompilerParams(vmem_limit_bytes=40 * 2**20),
        cost_estimate=pl.CostEstimate(
            flops=2 * rows * depth * width * group, bytes_accessed=12 * 2**20, transcendentals=0
        ),
        name="project",
    )(x, weight, bias[None], scale[None])


def permitted(first, limit, row, column):
    return ((column >= first) & (column <= limit)) | (column == row)


def head_mask(head, shape):
    lane = lax.broadcasted_iota(jnp.int32, shape, 1)
    return (lane >= head * HEAD_DIM) & (lane < (head + 1) * HEAD_DIM)


def attend_kernel(qb, kb, info_ref, first_ref, q_ref, k_ref, v_ref, o_ref, log_ref, vt_ref):
    length, width = q_ref.shape
    heads = width // HEAD_DIM
    live_end = info_ref[0]
    count = lax.div(live_end + qb - 1, qb)
    vt_ref[...] = v_ref[...].T
    o_ref[...] = jnp.zeros_like(o_ref)
    log_ref[...] = jnp.zeros_like(log_ref)

    def queries(i, _):
        rows = pl.ds(pl.multiple_of(i * qb, qb), qb)
        q = q_ref[rows, :]
        first = first_ref[0:1, rows]
        row = i * qb + lax.broadcasted_iota(jnp.int32, (1, qb), 1)
        limit = jnp.minimum(row, live_end - 1)
        q_heads = [
            jnp.where(head_mask(h, (qb, width)), q, jnp.zeros_like(q)) for h in range(heads)
        ]
        def keys(j, carry):
            columns = pl.ds(pl.multiple_of(j * kb, kb), kb)
            k = k_ref[columns, :]
            column = j * kb + lax.broadcasted_iota(jnp.int32, (kb, 1), 0)
            allowed = permitted(first, limit, row, column)
            out = []
            for h in range(heads):
                top, total, summed = carry[h]
                scores = jnp.where(allowed, nt(k, q_heads[h]), masked_score)
                new_top = jnp.maximum(top, jnp.max(scores, axis=0, keepdims=True))
                weights = jnp.exp(scores - new_top)
                scale = jnp.exp(top - new_top)
                total = total * scale + jnp.sum(weights, axis=0, keepdims=True)
                vt = vt_ref[h * HEAD_DIM : (h + 1) * HEAD_DIM, columns]
                summed = summed * scale + nn(vt, weights.astype(bf16))
                out.append((new_top, total, summed))
            return tuple(out)
        start = tuple(
            (
                jnp.full((1, qb), masked_score, f32),
                jnp.zeros((1, qb), f32),
                jnp.zeros((HEAD_DIM, qb), f32),
            )
            for _ in range(heads)
        )
        lo = lax.div(info_ref[1 + i], kb)
        hi = lax.div(i * qb + qb - 1, kb) + 1
        done = lax.fori_loop(lo, hi, keys, start)
        mixed = jnp.concatenate([summed / total for _, total, summed in done], axis=0)
        o_ref[rows, :] = mixed.T.astype(o_ref.dtype)
        for h, (top, total, _) in enumerate(done):
            log_ref[0, h : h + 1, rows] = top + jnp.log(total)
        return 0
    lax.fori_loop(0, count, queries, 0)


def attend_back_kernel(
    qb, kb, info_ref, first_ref, q_ref, k_ref, v_ref, o_ref, do_ref, log_ref, out_ref, sum_ref,
    dk_acc, dv_acc,
):
    length, width = q_ref.shape
    heads = width // HEAD_DIM
    features = out_ref.shape[1] // 3
    slab = pl.program_id(0)
    factor = HEAD_DIM ** (-0.5)
    live_end = info_ref[0]
    count = lax.div(live_end + qb - 1, qb)

    def lanes(which):
        if features == width:
            return pl.ds(which * features, width)
        return pl.ds(pl.multiple_of(which * features + slab * width, width), width)
    dk_acc[...] = jnp.zeros_like(dk_acc)
    dv_acc[...] = jnp.zeros_like(dv_acc)
    out_ref[:, lanes(0)] = jnp.zeros((length, width), out_ref.dtype)

    def queries(i, _):
        rows = pl.ds(pl.multiple_of(i * qb, qb), qb)
        q, do = q_ref[rows, :], do_ref[rows, :]
        first = first_ref[0:1, rows]
        row = i * qb + lax.broadcasted_iota(jnp.int32, (1, qb), 1)
        limit = jnp.minimum(row, live_end - 1)
        dots = (do.astype(f32) * o_ref[rows, :].astype(f32)).T
        masks = [head_mask(h, (qb, width)) for h in range(heads)]
        kmasks = [head_mask(h, (kb, width)) for h in range(heads)]
        zero = jnp.zeros_like(q)
        q_heads = [jnp.where(mask, q, zero) for mask in masks]
        do_heads = [jnp.where(mask, do, zero) for mask in masks]
        logs = [log_ref[0, h : h + 1, rows] for h in range(heads)]
        deltas = [
            jnp.sum(dots[h * HEAD_DIM : (h + 1) * HEAD_DIM], axis=0, keepdims=True)
            for h in range(heads)
        ]
        def keys(j, dq):
            columns = pl.ds(pl.multiple_of(j * kb, kb), kb)
            k, v = k_ref[columns, :], v_ref[columns, :]
            column = j * kb + lax.broadcasted_iota(jnp.int32, (kb, 1), 0)
            allowed = permitted(first, limit, row, column)
            dk, dv = dk_acc[columns, :], dv_acc[columns, :]
            for h in range(heads):
                scores = jnp.where(allowed, nt(k, q_heads[h]) - logs[h], masked_score)
                probs = jnp.exp(scores)
                prob_grad = nt(v, do_heads[h])
                score_grad = (probs * (prob_grad - deltas[h])).astype(bf16)
                dv = dv + nn(probs.astype(bf16), do_heads[h])
                dk = dk + nn(score_grad, q_heads[h])
                dq = dq + tn(score_grad, jnp.where(kmasks[h], k, jnp.zeros_like(k)))
            dk_acc[columns, :] = dk
            dv_acc[columns, :] = dv
            return dq
        lo = lax.div(info_ref[1 + i], kb)
        hi = lax.div(i * qb + qb - 1, kb) + 1
        dq = lax.fori_loop(lo, hi, keys, jnp.zeros((qb, width), f32))
        out_ref[rows, lanes(0)] = (dq * factor).astype(out_ref.dtype)
        return 0
    lax.fori_loop(0, count, queries, 0)
    sum_ref[...] = jnp.zeros_like(sum_ref)

    def store(i, _):
        rows = pl.ds(pl.multiple_of(i * kb, kb), kb)
        dv = dv_acc[rows, :].astype(out_ref.dtype)
        out_ref[rows, lanes(1)] = dk_acc[rows, :].astype(out_ref.dtype)
        out_ref[rows, lanes(2)] = dv
        dq = out_ref[rows, lanes(0)].astype(f32)
        sum_ref[0, 0:1, :] += jnp.sum(dq, axis=0, keepdims=True)
        sum_ref[0, 1:2, :] += jnp.sum(dv.astype(f32), axis=0, keepdims=True)
        return 0
    lax.fori_loop(0, length // kb, store, 0)


def attention_specs(length, features):
    width = min(256, features)
    slabs = features // width

    plain = pl.BlockSpec((length, width), lambda i, info: (0, i))

    def piece(which):
        if features % 128:
            return plain
        return pl.BlockSpec((length, width), lambda i, info, w=which: (0, w * slabs + i))

    logs = pl.BlockSpec((1, 8, length), lambda i, info: (i, 0, 0))
    first = pl.BlockSpec((1, length), lambda i, info: (0, 0))
    return width, slabs, piece, plain, logs, first


def three(qkv, features):
    if features % 128:
        return [qkv[:, w * features : (w + 1) * features] for w in range(3)]
    return [qkv] * 3


def attend(qkv, info, first, qb, kb):
    length, features = qkv.shape[0], qkv.shape[1] // 3
    width, slabs, piece, plain, logs, first_spec = attention_specs(length, features)
    return pl.pallas_call(
        functools.partial(attend_kernel, qb, kb),
        out_shape=(
            jax.ShapeDtypeStruct((length, features), bf16),
            jax.ShapeDtypeStruct((slabs, 8, length), f32),
        ),
        grid_spec=pltpu.PrefetchScalarGridSpec(
            num_scalar_prefetch=1,
            grid=(slabs,),
            in_specs=[first_spec, piece(0), piece(1), piece(2)],
            out_specs=(plain, logs),
            scratch_shapes=[pltpu.VMEM((width, length), bf16)],
        ),
        compiler_params=pltpu.CompilerParams(vmem_limit_bytes=48 * 2**20),
        cost_estimate=takes(30),
        name="attend",
    )(info, first, *three(qkv, features))


def attend_back(qkv, mixed, grad, log_total, info, first, qb, kb):
    length, features = qkv.shape[0], qkv.shape[1] // 3
    width, slabs, piece, plain, logs, first_spec = attention_specs(length, features)
    return pl.pallas_call(
        functools.partial(attend_back_kernel, qb, kb),
        out_shape=(
            jax.ShapeDtypeStruct((length, 3 * features), bf16),
            jax.ShapeDtypeStruct((slabs, 8, width), f32),
        ),
        grid_spec=pltpu.PrefetchScalarGridSpec(
            num_scalar_prefetch=1,
            grid=(slabs,),
            in_specs=[first_spec, piece(0), piece(1), piece(2), plain, plain, logs],
            out_specs=(
                pl.BlockSpec((length, 3 * features), lambda i, info: (0, 0)),
                pl.BlockSpec((1, 8, width), lambda i, info: (i, 0, 0)),
            ),
            scratch_shapes=[pltpu.VMEM((length, width), f32), pltpu.VMEM((length, width), f32)],
        ),
        compiler_params=pltpu.CompilerParams(vmem_limit_bytes=48 * 2**20),
        cost_estimate=takes(34),
        name="attend_back",
    )(info, first, *three(qkv, features), mixed, grad, log_total)


def body(
    tokens,
    positions,
    doc_lengths,
    exit_depth,
    w_query,
    w_key,
    w_value,
    w_out,
    w_up,
    w_down,
    b_query,
    b_value,
    b_out,
    b_up,
    b_down,
    attn_gain,
    attn_bias,
    ffn_gain,
    ffn_bias,
    cotangent,
):
    seqs, local_rows, width = tokens.shape
    inner = b_query.shape[0]
    bands, tps = lax.axis_size("band"), lax.axis_size("tp")
    group = bands // seqs
    piece = local_rows // (group * tps)
    band, tp = lax.axis_index("band"), lax.axis_index("tp")
    seq, member = band // group, lax.rem(band, group)
    features = inner // group
    length = exit_depth.shape[1]
    own = bands * piece
    rows = tps * own
    block, half_block = min(512, length), min(256, length)

    def by_group(*parts):
        split = [p.reshape(p.shape[:-1] + (group, features)) for p in parts]
        return jnp.stack(split, axis=-2).reshape(parts[0].shape[:-1] + (-1,))

    def share(grad):
        return lax.psum_scatter(grad, "band", scatter_dimension=0, tiled=True)

    w_in_out = jnp.concatenate([by_group(w_query, w_key, w_value), w_out.T], axis=1)
    w_in_out = lax.all_gather(w_in_out, "band", axis=0, tiled=True)
    w_in, w_out_t = w_in_out[:, : 3 * inner], w_in_out[:, 3 * inner :]
    w_up_all = lax.all_gather(w_up, "band", axis=0, tiled=True)
    w_down_t = lax.all_gather(w_down.T, "band", axis=0, tiled=True)

    def my_share(array):
        split = array.reshape(seqs, group, tps, piece, width)
        return lax.dynamic_index_in_dim(split, tp, 2, keepdims=False).reshape(bands, piece, width)

    token_own, all_pos = transfer([Swap(my_share(tokens), positions)], 0, name="swap_in")
    seq_pos = lax.dynamic_index_in_dim(all_pos, seq, 1, keepdims=False)
    seq_pos = seq_pos.reshape(bands, group, tps, piece).transpose(1, 2, 0, 3)
    row_pos = seq_pos.reshape(length)
    member_pos = lax.dynamic_index_in_dim(seq_pos, member, 0, keepdims=False)
    own_pos = lax.dynamic_index_in_dim(member_pos, tp, 0, keepdims=False).reshape(own)
    depths = lax.dynamic_index_in_dim(exit_depth, seq, 0, keepdims=False)
    live_end = jnp.sum((depths > LAYER).astype(jnp.int32))
    live_own = (own_pos < live_end).astype(f32)[:, None]
    ends = jnp.cumsum(lax.dynamic_index_in_dim(doc_lengths, seq, 0, keepdims=False))
    places = jnp.arange(length, dtype=jnp.int32)
    first = jnp.max(jnp.where(ends[:, None] <= places[None, :], ends[:, None], 0), axis=0)
    info = jnp.concatenate([live_end[None], first[::block]]).astype(jnp.int32)
    first = first[None, :].astype(jnp.int32)
    to_sorted = (row_pos[None, :] == places[:, None]).astype(bf16)
    to_rows = (row_pos[:, None] == places[None, :]).astype(bf16)

    inputs = token_own.reshape(own, width).astype(f32)
    normed_in, unit_in, inverse_in = layer_norm(inputs, attn_gain, attn_bias)
    z1, grad_low = transfer([Gather(normed_in.astype(bf16)), Swap(my_share(cotangent))], 1, name="gather_in")
    z1 = z1.reshape(rows, width)
    grad_own = grad_low.reshape(own, width).astype(f32)
    down_grad_own = (live_own * grad_own).astype(bf16)
    down_grad = gather_later(down_grad_own)

    bias_in = by_group(b_query, jnp.zeros_like(b_query), b_value)
    scale_in = by_group(
        jnp.full_like(b_query, HEAD_DIM ** (-0.5)), jnp.ones_like(b_query), jnp.ones_like(b_query)
    )
    qkv = project(z1, w_in_out, bias_in, scale_in, group)
    qkv = swap_heads(qkv, group, 4, "plain").reshape(length, 3 * features)
    qkv = nn(to_sorted, qkv).astype(bf16)
    mixed_sorted, log_total = attend(qkv, info, first, block, block)
    mixed_sorted, down_grad = lax.optimization_barrier((mixed_sorted, down_grad))
    down_grad = down_grad.reshape(rows, width)
    mixed = nn(to_rows, mixed_sorted).astype(bf16).reshape(group, rows, features)
    mixed = swap_heads(mixed, group, 5, "join")

    attn_part = nt(mixed, w_out_t).astype(bf16).reshape(tps, own, width)
    (attn_out,) = transfer([Scatter(attn_part)], 6, name="scatter_attn")
    attn_out = attn_out + b_out
    residual = inputs + attn_out
    normed_mid, unit_mid, inverse_mid = layer_norm(residual, ffn_gain, ffn_bias)
    (z2,) = transfer([Gather(normed_mid.astype(bf16))], 7, name="gather_mid")
    z2 = z2.reshape(rows, width)
    pre_act = nn(z2, w_up_all) + b_up
    below = 0.5 * (1.0 + lax.erf(pre_act * 0.5**0.5))
    act = (pre_act * below).astype(bf16)
    slope = (below + pre_act * jnp.exp(-0.5 * pre_act * pre_act) * (2 * math.pi) ** -0.5).astype(bf16)

    grad_w_down_t = tn(down_grad, act).astype(bf16)
    grad_w_down_t, act, w_down_t = lax.optimization_barrier((grad_w_down_t, act, w_down_t))
    shared_down = share(grad_w_down_t)
    ffn_part = nt(act, w_down_t).astype(bf16).reshape(tps, own, width)
    ffn_out, up_grad = transfer(
        [Scatter(ffn_part)],
        8,
        Work([down_grad, w_down_t, slope], [("nn", 0, 1, 2, 0)], 1),
        name="scatter_ffn",
    )
    output = (inputs + live_own * (attn_out + ffn_out + b_down)).astype(bf16)
    output = output.reshape(bands, piece, width)

    mid_part = nt(up_grad, w_up_all).astype(bf16).reshape(tps, own, width)
    mid_grad, output, grad_w_up, up_sums = transfer(
        [Scatter(mid_part), Swap(output)],
        9,
        Work([z2, up_grad], [("tn", 0, 1, None, 0), ("sum", 1, None, None, 1)], 1),
        name="scatter_mid",
    )
    resid_grad = norm_back(mid_grad, unit_mid, inverse_mid, ffn_gain)
    attn_grad_own = (live_own * grad_own + resid_grad).astype(bf16)
    (attn_grad,) = transfer([Gather(attn_grad_own)], 10, name="gather_back")
    attn_grad = attn_grad.reshape(rows, width)
    attn_grad, output = lax.optimization_barrier((attn_grad, output))
    output = gather_later(output)

    grad_w_out_t = tn(attn_grad, mixed).astype(bf16)
    mixed_grad = nn(attn_grad, w_out_t).astype(bf16)
    mixed_grad = swap_heads(mixed_grad, group, 13, "cut").reshape(length, features)
    mixed_grad = nn(to_sorted, mixed_grad).astype(bf16)
    grad_w_up, shared_down = lax.optimization_barrier((grad_w_up, shared_down))
    shared_up = share(grad_w_up)
    mixed_grad, grad_w_out_t = lax.optimization_barrier((mixed_grad, grad_w_out_t))
    in_grad, in_sums = attend_back(
        qkv, mixed_sorted, mixed_grad, log_total, info, first, block, half_block
    )
    in_sums = in_sums.transpose(1, 0, 2).reshape(8, features)
    mine = (jnp.arange(group) == member).astype(f32)[:, None]
    in_grad, output = lax.optimization_barrier((in_grad, output))
    output = output.transpose(1, 0, 2, 3).reshape(tokens.shape)
    in_grad = nn(to_rows, in_grad).astype(bf16).reshape(group, rows, 3 * features)
    in_grad = swap_heads(in_grad, group, 14, "join")
    in_part = nt(in_grad, w_in).astype(bf16).reshape(tps, bands, piece, width)
    in_part, in_grad = lax.optimization_barrier((in_part, in_grad))
    grad_w_in = tn(z1, in_grad).astype(bf16)
    grad_w_in_out = jnp.concatenate([grad_w_in, grad_w_out_t], axis=1)
    grad_w_in_out, shared_up, in_part = lax.optimization_barrier((grad_w_in_out, shared_up, in_part))
    shared_in_out = share(grad_w_in_out)

    def over_rows(array):
        return jnp.sum(array.astype(f32), axis=0)

    wide = [
        over_rows(attn_grad_own),
        over_rows(down_grad_own),
        over_rows(mid_grad * unit_mid),
        over_rows(mid_grad),
    ]
    wide = jnp.concatenate(wide).astype(bf16).reshape(16, width // 4)
    narrow = jnp.concatenate(
        [(mine * in_sums[0]).reshape(-1), (mine * in_sums[1]).reshape(-1), up_sums[0]]
    )
    count = narrow.shape[0]
    narrow = jnp.pad(narrow, (0, -count % 2048)).astype(bf16).reshape(16, -1)
    token_grad, wide, narrow = finish(
        in_part,
        unit_in.reshape(bands, piece, width),
        grad_low,
        resid_grad.reshape(bands, piece, width),
        inverse_in.reshape(bands, piece, 1),
        attn_gain[None],
        wide,
        narrow,
        15,
    )
    token_grad = token_grad.reshape(tokens.shape).astype(f32)
    wide, late = wide[:16].reshape(4, width), wide[16:].reshape(2, width)
    narrow = narrow.reshape(-1)[:count]
    shared_in = shared_in_out[:, : 3 * inner].astype(f32).reshape(-1, group, 3, features)
    shared_down, shared_out = shared_down.astype(f32).T, shared_in_out[:, 3 * inner :].astype(f32).T
    shared_up = shared_up.astype(f32)
    shared_q, shared_k, shared_v = (
        shared_in[:, :, which].reshape(-1, inner) for which in range(3)
    )

    return (
        output,
        token_grad,
        shared_q,
        shared_k,
        shared_v,
        shared_out,
        shared_up,
        shared_down,
        narrow[:inner],
        narrow[inner : 2 * inner],
        wide[0],
        narrow[2 * inner :],
        wide[1],
        late[0],
        late[1],
        wide[2],
        wide[3],
    )


def solution(mesh):
    return jax.shard_map(
        body,
        mesh=mesh,
        in_specs=(
            P(None, "band", None),
            P(None, "band"),
            P(),
            P(),
            P("band", "tp"),
            P("band", "tp"),
            P("band", "tp"),
            P("tp", "band"),
            P("band", "tp"),
            P("tp", "band"),
            P("tp"),
            P("tp"),
            P(),
            P("tp"),
            P(),
            P(),
            P(),
            P(),
            P(),
            P(None, "band", None),
        ),
        out_specs=(
            P(None, "band", None),
            P(None, "band", None),
            P("band", "tp"),
            P("band", "tp"),
            P("band", "tp"),
            P("tp", "band"),
            P("band", "tp"),
            P("tp", "band"),
            P("tp"),
            P("tp"),
            P(),
            P("tp"),
            P(),
            P(),
            P(),
            P(),
            P(),
        ),
        check_vma=False,
    )
```

```python
import functools
import math

import jax
import jax.numpy as jnp
from jax import lax
from jax.experimental import pallas as pl
from jax.experimental.pallas import tpu as pltpu
from jax.sharding import PartitionSpec as P

HEAD_DIM = 64
LAYER = 12
MESH = pl.DeviceIdType.MESH

epsilon = 1e-05
masked_score = -1e30
bf16 = jnp.bfloat16
f32 = jnp.float32


def layer_norm(values, gain, shift):
    center = values - jnp.mean(values, axis=-1, keepdims=True)
    inverse = lax.rsqrt(jnp.mean(center * center, axis=-1, keepdims=True) + epsilon)
    normed = center * inverse
    return (normed * gain + shift, normed, inverse)


def norm_back(grad_out, normed, inverse, gain):
    scaled = grad_out * gain
    return inverse * (
        scaled
        - jnp.mean(scaled, axis=-1, keepdims=True)
        - normed * jnp.mean(scaled * normed, axis=-1, keepdims=True)
    )


def nn(left, right):
    return jnp.dot(left, right, preferred_element_type=f32)


def nt(left, right):
    return lax.dot_general(left, right, (((1,), (1,)), ((), ())), preferred_element_type=f32)


def tn(left, right):
    return lax.dot_general(left, right, (((0,), (0,)), ((), ())), preferred_element_type=f32)


def gelu_exact(values):
    return jax.nn.gelu(values, approximate=False)


def halves(count):
    return (count // 2, 2) if count % 2 == 0 else (count, 1)


def takes(microseconds):
    return pl.CostEstimate(
        flops=int(microseconds * 1e9), bytes_accessed=int(microseconds * 2e6), transcendentals=0
    )


class Sems:
    def __init__(self, send_sem, recv_sem, local_sem):
        self.send_sem, self.recv_sem, self.local_sem = send_sem, recv_sem, local_sem
        self.sent = self.local = 0

    def send(self, source, target, device):
        k = self.sent
        self.sent += 1
        copy = pltpu.make_async_remote_copy(
            source, target, self.send_sem.at[k], self.recv_sem.at[k],
            device_id=device, device_id_type=MESH,
        )
        copy.start()
        return copy

    def copy(self, source, target):
        k = self.local
        self.local += 1
        copy = pltpu.make_async_copy(source, target, self.local_sem.at[k])
        copy.start()
        return copy


class Grid:
    def __init__(self, count):
        self.na, self.nb = na, nb = halves(count)
        self.me, band = lax.axis_index("tp"), lax.axis_index("band")
        self.a, self.b = a, b = self.me // nb, lax.rem(self.me, nb)
        self.along_b = [(band, a * nb + lax.rem(b + d, nb)) for d in range(1, nb)]
        self.along_a = [(band, lax.rem(a + d, na) * nb + b) for d in range(1, na)]
        self.from_b = [a * nb + lax.rem(b + nb - d, nb) for d in range(1, nb)]
        self.from_a = [lax.rem(a + na - d, na) * nb + b for d in range(1, na)]


def tp_peers():
    grid = Grid(lax.axis_size("tp"))
    return grid.along_a + grid.along_b


def band_peers():
    size = lax.axis_size("band")
    me, tp = lax.axis_index("band"), lax.axis_index("tp")
    return [(lax.rem(me + d, size), tp) for d in range(1, size)]


anywhere = pl.BlockSpec(memory_space=pl.ANY)
vmem = pl.BlockSpec(memory_space=pltpu.VMEM)


class Gather:
    peers = "tp"

    def __init__(self, x, inner_slot=False, extra=None):
        self.count = count = lax.axis_size("tp")
        na, nb = halves(count)
        self.inner_slot, self.extra = inner_slot, extra is not None
        self.sends = 2 * (na - 1 + nb - 1) + 2 * (na - 1) * (nb - 1)
        self.locals = 2
        shape = (x.shape[0], count) + x.shape[1:] if inner_slot else (count,) + x.shape
        self.operands, self.in_specs = [x], [anywhere]
        self.shapes, self.out_specs = [jax.ShapeDtypeStruct(shape, x.dtype)], [anywhere]
        self.scratch = [pltpu.VMEM(x.shape, x.dtype)]
        if self.extra:
            self.operands.append(extra)
            self.in_specs.append(vmem)
            self.shapes.append(jax.ShapeDtypeStruct(extra.shape, extra.dtype))
            self.out_specs.append(vmem)
            self.sends += na - 1 + nb - 1
            self.scratch += [
                pltpu.VMEM(extra.shape, extra.dtype),
                pltpu.VMEM((max(nb - 1, 1),) + extra.shape, extra.dtype),
                pltpu.VMEM((max(na - 1, 1),) + extra.shape, extra.dtype),
            ]

    def slot(self, index, which):
        part = self.part[which]
        return self.out.at[part, index] if self.inner_slot else self.out.at[index, part]

    def begin(self, ins, outs, scratch, sems):
        self.grid = grid = Grid(self.count)
        self.sems = sems
        x, self.out = ins[0], outs[0]
        half = x.shape[0] // 2
        self.part = part = (pl.ds(0, half), pl.ds(half, half))
        self.through = scratch[0]
        self.load = sems.copy(x, self.through)
        me = grid.me
        if self.extra:
            self.more = (ins[1], outs[1], *scratch[1:])
            self.extra_b = [
                sems.send(ins[1], scratch[2].at[k], device) for k, device in enumerate(grid.along_b)
            ]
        top, low = x.at[part[0]], x.at[part[1]]
        self.first_b = [sems.send(top, self.slot(me, 0), device) for device in grid.along_b]
        self.first_a = [sems.send(low, self.slot(me, 1), device) for device in grid.along_a]
        self.second = [sems.send(top, self.slot(me, 0), device) for device in grid.along_a]
        self.second += [sems.send(low, self.slot(me, 1), device) for device in grid.along_b]

    def middle(self):
        grid, sems = self.grid, self.sems
        self.load.wait()
        whole = self.out.at[:, grid.me] if self.inner_slot else self.out.at[grid.me]
        self.store = sems.copy(self.through, whole)
        if self.extra:
            own, _, part_ref, in_b, in_a = self.more
            total = own[...]
            for k, copy in enumerate(self.extra_b):
                copy.wait_recv()
                total = total + in_b[k]
            part_ref[...] = total
            self.extra_a = [
                sems.send(part_ref, in_a.at[k], device) for k, device in enumerate(grid.along_a)
            ]
        for copy, source in zip(self.first_b, grid.from_b):
            copy.wait_recv()
            held = self.slot(source, 0)
            self.second += [sems.send(held, held, device) for device in grid.along_a]
        for copy, source in zip(self.first_a, grid.from_a):
            copy.wait_recv()
            held = self.slot(source, 1)
            self.second += [sems.send(held, held, device) for device in grid.along_b]

    def end(self):
        if self.extra:
            _, total_ref, part_ref, _, in_a = self.more
            total = part_ref[...]
            for k, copy in enumerate(self.extra_a):
                copy.wait_recv()
                total = total + in_a[k]
            total_ref[...] = total
            for copy in self.extra_a + self.extra_b:
                copy.wait_send()
        for copy in self.first_a + self.first_b:
            copy.wait_send()
        for copy in self.second:
            copy.wait()
        self.store.wait()


class Scatter:
    peers = "tp"

    def __init__(self, partial):
        self.count, rows, width = partial.shape
        na, nb = halves(self.count)
        block = (rows // 2, width)
        self.sends = 2 * (na - 1) * (nb - 1) + 2 * (na - 1 + nb - 1)
        self.locals = na + nb
        self.operands, self.in_specs = [partial], [anywhere]
        self.shapes, self.out_specs = [jax.ShapeDtypeStruct((rows, width), f32)], [vmem]

        def buffer(*lead):
            return pltpu.VMEM(tuple(max(n, 1) for n in lead) + block, partial.dtype)

        self.scratch = [
            buffer(na), buffer(nb), buffer(nb - 1, na), buffer(na - 1, nb),
            buffer(na - 1), buffer(nb - 1), buffer(na - 1), buffer(nb - 1),
        ]

    def begin(self, ins, outs, scratch, sems):
        self.grid = grid = Grid(self.count)
        self.sems, self.out, self.scratch_refs = sems, outs[0], scratch
        own_a, own_b, one_a, one_b = scratch[:4]
        part = ins[0]
        na, nb, a, b = grid.na, grid.nb, grid.a, grid.b
        half = part.shape[1] // 2
        self.top, self.low = top, low = pl.ds(0, half), pl.ds(half, half)
        self.order_a = order_a = list(range(1, na)) + [0]
        self.order_b = order_b = list(range(1, nb)) + [0]
        self.first_a, self.first_b = {}, {}
        for step in range(max(na, nb)):
            if step < na:
                e = order_a[step]
                row = lax.rem(a + e, na) * nb
                for d in range(1, nb):
                    source = part.at[row + lax.rem(b + d, nb), top]
                    self.first_b[d, e] = sems.send(source, one_a.at[d - 1, e], grid.along_b[d - 1])
            if step < nb:
                e = order_b[step]
                column = lax.rem(b + e, nb)
                for d in range(1, na):
                    source = part.at[lax.rem(a + d, na) * nb + column, low]
                    self.first_a[d, e] = sems.send(source, one_b.at[d - 1, e], grid.along_a[d - 1])
        self.local_a = {
            e: sems.copy(part.at[lax.rem(a + e, na) * nb + b, top], own_a.at[e]) for e in order_a
        }
        self.local_b = {
            e: sems.copy(part.at[a * nb + lax.rem(b + e, nb), low], own_b.at[e]) for e in order_b
        }

    def sum_a(self, e):
        own_a, _, one_a = self.scratch_refs[:3]
        self.local_a[e].wait()
        total = own_a[e].astype(f32)
        for d in range(1, self.grid.nb):
            self.first_b[d, e].wait_recv()
            total = total + one_a[d - 1, e].astype(f32)
        return total

    def sum_b(self, e):
        _, own_b, _, one_b = self.scratch_refs[:4]
        self.local_b[e].wait()
        total = own_b[e].astype(f32)
        for d in range(1, self.grid.na):
            self.first_a[d, e].wait_recv()
            total = total + one_b[d - 1, e].astype(f32)
        return total

    def middle(self):
        grid, sems = self.grid, self.sems
        out_a, out_b, two_a, two_b = self.scratch_refs[4:]
        self.second_a, self.second_b = {}, {}
        for e in self.order_a[:-1]:
            out_a[e - 1] = self.sum_a(e).astype(out_a.dtype)
            self.second_a[e] = sems.send(out_a.at[e - 1], two_a.at[e - 1], grid.along_a[e - 1])
        for e in self.order_b[:-1]:
            out_b[e - 1] = self.sum_b(e).astype(out_b.dtype)
            self.second_b[e] = sems.send(out_b.at[e - 1], two_b.at[e - 1], grid.along_b[e - 1])

    def end(self):
        _, _, two_a, two_b = self.scratch_refs[4:]
        total = self.sum_a(0)
        for e in self.order_a[:-1]:
            self.second_a[e].wait_recv()
            total = total + two_a[e - 1].astype(f32)
        self.out[self.top] = total
        total = self.sum_b(0)
        for e in self.order_b[:-1]:
            self.second_b[e].wait_recv()
            total = total + two_b[e - 1].astype(f32)
        self.out[self.low] = total
        for group in (self.first_a, self.first_b, self.second_a, self.second_b):
            for copy in group.values():
                copy.wait_send()


class Swap:
    peers = "band"

    def __init__(self, x, extra=None):
        size = lax.axis_size("band")
        arrays = [x] if extra is None else [x, extra]
        self.operands, self.in_specs = arrays, [anywhere] * len(arrays)
        self.shapes = [jax.ShapeDtypeStruct(x.shape, x.dtype)]
        self.scratch = [pltpu.VMEM(x.shape[1:], x.dtype)]
        if extra is not None:
            self.shapes.append(jax.ShapeDtypeStruct((size,) + extra.shape, extra.dtype))
            self.scratch.append(pltpu.VMEM(extra.shape, extra.dtype))
        self.out_specs = [anywhere] * len(arrays)
        self.sends = (size - 1) * len(arrays)
        self.locals = 2 * len(arrays)

    def begin(self, ins, outs, scratch, sems):
        me = lax.axis_index("band")
        self.sems, self.scratch_refs = sems, scratch
        self.slots = [out.at[me] for out in outs]
        self.loads = [sems.copy(ins[0].at[me], scratch[0])]
        if len(ins) > 1:
            self.loads.append(sems.copy(ins[1], scratch[1]))
        self.copies = []
        for peer in band_peers():
            if len(ins) > 1:
                self.copies.append(sems.send(ins[1], self.slots[1], peer))
            self.copies.append(sems.send(ins[0].at[peer[0]], self.slots[0], peer))

    def middle(self):
        self.stores = []
        for load, through, slot in zip(self.loads, self.scratch_refs, self.slots):
            load.wait()
            self.stores.append(self.sems.copy(through, slot))

    def end(self):
        for copy in self.copies + self.stores:
            copy.wait()


class Work:
    def __init__(self, operands, tasks, early):
        self.tasks, self.early = tasks, early
        self.operands = operands
        self.shapes = []
        for kind, left, right, _, _ in tasks:
            known = [*operands, *self.shapes]
            if kind == "sum":
                self.shapes.append(jax.ShapeDtypeStruct((1, known[left].shape[1]), f32))
                continue
            rows = known[left].shape[1 if kind == "tn" else 0]
            columns = known[right].shape[0 if kind == "nt" else 1]
            self.shapes.append(jax.ShapeDtypeStruct((rows, columns), bf16))
        self.scratch = [pltpu.VMEM(x.shape, x.dtype) for x in [*operands, *self.shapes]]
        self.locals = len(operands) + len(tasks)

    def begin(self, ins, outs, scratch, sems):
        self.sems, self.outs = sems, outs
        self.held, self.made = scratch[: len(ins)], scratch[len(ins) :]
        self.loads = [sems.copy(source, target) for source, target in zip(ins, self.held)]
        self.stores = []

    def ready(self, k):
        if k < len(self.loads) and self.loads[k] is not None:
            self.loads[k].wait()
            self.loads[k] = None

    def run(self, tasks):
        for kind, left, right, scale, out in tasks:
            for k in (left, right, scale):
                if k is not None:
                    self.ready(k)
            known = [*self.held, *self.made]
            x, made = known[left], self.made[out]
            if kind == "sum":
                rows = min(128, x.shape[0])
                made[...] = jnp.zeros_like(made)

                def add(k, _, x=x, made=made, rows=rows):
                    r = pl.ds(pl.multiple_of(k * rows, rows), rows)
                    made[...] += jnp.sum(x[r, :].astype(f32), axis=0, keepdims=True)
                    return 0

                lax.fori_loop(0, x.shape[0] // rows, add, 0)
                self.stores.append(self.sems.copy(made, self.outs[out]))
                continue
            y = known[right]
            factor = None if scale is None else self.held[scale]
            tile_r, tile_c = min(512, made.shape[0]), min(512, made.shape[1])
            columns = made.shape[1] // tile_c

            def tile(k, _, kind=kind, x=x, y=y, made=made, factor=factor):
                i, j = k // columns, lax.rem(k, columns)
                r = pl.ds(pl.multiple_of(i * tile_r, tile_r), tile_r)
                c = pl.ds(pl.multiple_of(j * tile_c, tile_c), tile_c)
                if kind == "tn":
                    total = tn(x[:, r], y[:, c])
                elif kind == "nt":
                    total = nt(x[r, :], y[c, :])
                else:
                    total = nn(x[r, :], y[:, c])
                if factor is not None:
                    total = total * factor[r, c].astype(f32)
                made[r, c] = total.astype(made.dtype)
                return 0

            lax.fori_loop(0, (made.shape[0] // tile_r) * columns, tile, 0)
            self.stores.append(self.sems.copy(made, self.outs[out]))

    def end(self):
        for store in self.stores:
            store.wait()


def transfer(parts, cid, work=None, name="transfer", time=36):
    items = list(parts) + ([work] if work is not None else [])
    sends = sum(part.sends for part in parts)
    locals_ = sum(item.locals for item in items)

    def kernel(*refs):
        refs = list(refs)

        def take(number):
            taken = refs[:number]
            del refs[:number]
            return taken

        ins = [take(len(item.operands)) for item in items]
        outs = [take(len(item.shapes)) for item in items]
        scratch = [take(len(item.scratch)) for item in items]
        sems = Sems(*refs)
        devices = []
        if any(part.peers == "tp" for part in parts):
            devices += tp_peers()
        if any(part.peers == "band" for part in parts):
            devices += band_peers()
        barrier = pltpu.get_barrier_semaphore()
        for device in devices:
            pl.semaphore_signal(barrier, inc=1, device_id=device, device_id_type=MESH)
        if work is not None:
            work.begin(ins[-1], outs[-1], scratch[-1], sems)
        pl.semaphore_wait(barrier, len(devices))
        for part, i, o, t in zip(parts, ins, outs, scratch):
            part.begin(i, o, t, sems)
        if work is not None:
            work.run(work.tasks[: work.early])
        for part in parts:
            part.middle()
        if work is not None:
            work.run(work.tasks[work.early :])
        for part in parts:
            part.end()
        if work is not None:
            work.end()

    in_specs = [spec for part in parts for spec in part.in_specs]
    out_specs = [spec for part in parts for spec in part.out_specs]
    if work is not None:
        in_specs += [anywhere] * len(work.operands)
        out_specs += [anywhere] * len(work.shapes)
    return pl.pallas_call(
        kernel,
        out_shape=tuple(shape for item in items for shape in item.shapes),
        in_specs=in_specs,
        out_specs=tuple(out_specs),
        scratch_shapes=[
            *(scratch for item in items for scratch in item.scratch),
            pltpu.SemaphoreType.DMA((sends,)),
            pltpu.SemaphoreType.DMA((sends,)),
            pltpu.SemaphoreType.DMA((locals_,)),
        ],
        compiler_params=pltpu.CompilerParams(
            collective_id=cid, has_side_effects=True, vmem_limit_bytes=(58 if work else 32) * 2**20
        ),
        cost_estimate=takes(time),
        name=name,
    )(*(operand for item in items for operand in item.operands))


def gather_later(x):
    count = lax.axis_size("tp")
    return lax.all_to_all(jnp.broadcast_to(x[None], (count,) + x.shape), "tp", 0, 0)


class Block:
    def __init__(self, order, shift, grid, size):
        band = lax.axis_index("band")
        self.order, self.shift = order, shift
        self.to, self.source = lax.rem(band + shift, size), lax.rem(band + size - shift, size)
        if order % 2 == 0:
            self.n1, self.n2 = grid.nb, grid.na
            self.first, self.second, self.origin = grid.along_b, grid.along_a, grid.from_b
            self.index = lambda d, e: lax.rem(grid.a + e, grid.na) * grid.nb + lax.rem(
                grid.b + d, grid.nb
            )
        else:
            self.n1, self.n2 = grid.na, grid.nb
            self.first, self.second, self.origin = grid.along_a, grid.along_b, grid.from_a
            self.index = lambda d, e: lax.rem(grid.a + d, grid.na) * grid.nb + lax.rem(
                grid.b + e, grid.nb
            )


def finish_kernel(
    count, size, part, unit, above, resid, inverse, gain, wide, narrow,
    out, wide_out, narrow_out,
    own, one, two_out, two, made, arrived, late, late_in, wide_in, narrow_in, pair, pair_b, pair_a,
    send_sem, recv_sem, local_sem,
):
    grid = Grid(count)
    sems = Sems(send_sem, recv_sem, local_sem)
    band = lax.axis_index("band")
    peers = band_peers()
    devices = grid.along_a + grid.along_b + peers
    barrier = pltpu.get_barrier_semaphore()
    for device in devices:
        pl.semaphore_signal(barrier, inc=1, device_id=device, device_id_type=MESH)
    shifts = list(range(1, size)) + [0]
    blocks = [Block(k, shift, grid, size) for k, shift in enumerate(shifts)]
    late[...] = jnp.zeros_like(late)
    pl.semaphore_wait(barrier, len(devices))
    done = []

    for blk in blocks:
        k = blk.order
        seconds = list(range(1, blk.n2)) + [0]
        blk.one = {
            (d, e): sems.send(
                part.at[blk.index(d, e), blk.to], one.at[k, d - 1, e], blk.first[d - 1]
            )
            for e in seconds
            for d in range(1, blk.n1)
        }
        blk.own = {e: sems.copy(part.at[blk.index(0, e), blk.to], own.at[k, e]) for e in seconds}
    early = []
    for peer in peers:
        early.append(sems.send(wide, wide_in.at[band], peer))
        early.append(sems.send(narrow, narrow_in.at[band], peer))

    def first_sum(blk, e):
        k = blk.order
        blk.own[e].wait()
        total = own[k, e].astype(f32)
        for d in range(1, blk.n1):
            blk.one[d, e].wait_recv()
            total = total + one[k, d - 1, e].astype(f32)
        return total

    def pass_on(blk):
        k = blk.order
        blk.two = []
        for e in range(1, blk.n2):
            two_out[k, e - 1] = first_sum(blk, e).astype(bf16)
            blk.two.append(sems.send(two_out.at[k, e - 1], two.at[k, e - 1], blk.second[e - 1]))

    def complete(blk):
        k = blk.order
        grad = first_sum(blk, 0)
        for e, copy in enumerate(blk.two):
            copy.wait_recv()
            grad = grad + two[k, e].astype(f32)
        normed = unit[blk.to]
        scaled = grad * gain[...]
        mean = jnp.mean(scaled, axis=-1, keepdims=True)
        along = jnp.mean(scaled * normed, axis=-1, keepdims=True)
        base = above[blk.to].astype(f32) + resid[blk.to]
        token = base + inverse[blk.to] * (scaled - mean - normed * along)
        made[k] = token.astype(bf16)
        sums = (jnp.sum(grad * normed, axis=0, keepdims=True), jnp.sum(grad, axis=0, keepdims=True))
        quarter = late.shape[1]
        for which, total in enumerate(sums):
            for i in range(4):
                row = slice(4 * which + i, 4 * which + i + 1)
                late[row, :] = late[row, :] + total[:, i * quarter : (i + 1) * quarter]
        if blk.shift:
            blk.swap = sems.send(made.at[k], arrived.at[k], (blk.to, lax.axis_index("tp")))

    def relay(blk):
        k = blk.order
        if blk.shift:
            blk.swap.wait_recv()
            held = arrived.at[k]
        else:
            held = made.at[k]
        slot = out.at[blk.source, grid.me]
        blk.near = [sems.send(held, slot, device) for device in blk.first]
        blk.far = [sems.send(held, slot, device) for device in blk.second]
        done.append(sems.copy(held, slot))

    def forward(blk):
        for copy, source in zip(blk.near, blk.origin):
            copy.wait_recv()
            held = out.at[blk.source, source]
            blk.far += [sems.send(held, held, device) for device in blk.second]

    pairs = [blocks[k : k + 2] for k in range(0, size, 2)]
    stages = (pass_on, complete, relay, forward)
    for step in range(len(pairs) + len(stages) - 1):
        for behind, stage in enumerate(stages):
            if 0 <= step - behind < len(pairs):
                for blk in pairs[step - behind]:
                    stage(blk)
        if step == len(pairs):
            last = [sems.send(late, late_in.at[band], peer) for peer in peers]

    for copy in early + last:
        copy.wait_recv()
    wide_in[band] = wide[...]
    narrow_in[band] = narrow[...]
    late_in[band] = late[...]
    total, narrow_total, late_total = (
        sum(array[k].astype(f32) for k in range(size)) for array in (wide_in, narrow_in, late_in)
    )
    narrow_out[...] = narrow_total
    pair[0:16, :] = total
    pair[16:24, :] = late_total
    near = [sems.send(pair, pair_b.at[k], device) for k, device in enumerate(grid.along_b)]
    total = pair[...]
    for k, copy in enumerate(near):
        copy.wait_recv()
        total = total + pair_b[k]
    for copy in near:
        copy.wait_send()
    pair[...] = total
    far = [sems.send(pair, pair_a.at[k], device) for k, device in enumerate(grid.along_a)]
    for k, copy in enumerate(far):
        copy.wait_recv()
        total = total + pair_a[k]
    wide_out[...] = total

    for copy in early + last + far:
        copy.wait_send()
    for blk in blocks:
        for copy in [*blk.one.values(), *blk.two, *blk.near]:
            copy.wait_send()
        if blk.shift:
            blk.swap.wait_send()
        for copy in blk.far:
            copy.wait()
    for copy in done:
        copy.wait()


def finish(part, unit, above, resid, inverse, gain, wide, narrow, cid):
    count, size, rows, width = part.shape
    na, nb = halves(count)
    most = max(na, nb)
    sends = locals_ = 0
    for k in range(size):
        n1, n2 = (nb, na) if k % 2 == 0 else (na, nb)
        sends += (n1 - 1) * n2 + 2 * (n2 - 1) + (n1 - 1) + (n1 - 1) * (n2 - 1)
        locals_ += n2 + 1
    sends += 4 * (size - 1) + na - 1 + nb - 1
    lanes = wide.shape[1]

    def blocks(*lead):
        return pltpu.VMEM(tuple(max(n, 1) for n in lead) + (rows, width), bf16)

    return pl.pallas_call(
        functools.partial(finish_kernel, count, size),
        out_shape=(
            jax.ShapeDtypeStruct((size, count, rows, width), bf16),
            jax.ShapeDtypeStruct((24, lanes), f32),
            jax.ShapeDtypeStruct(narrow.shape, f32),
        ),
        in_specs=[anywhere] + [vmem] * 7,
        out_specs=(anywhere, vmem, vmem),
        scratch_shapes=[
            blocks(size, most), blocks(size, most - 1, most),
            blocks(size, most - 1), blocks(size, most - 1),
            blocks(size), blocks(size),
            pltpu.VMEM((8, lanes), f32),
            pltpu.VMEM((size, 8, lanes), f32),
            pltpu.VMEM((size,) + wide.shape, bf16),
            pltpu.VMEM((size,) + narrow.shape, bf16),
            pltpu.VMEM((24, lanes), f32),
            pltpu.VMEM((max(nb - 1, 1), 24, lanes), f32),
            pltpu.VMEM((max(na - 1, 1), 24, lanes), f32),
            pltpu.SemaphoreType.DMA((sends,)),
            pltpu.SemaphoreType.DMA((sends,)),
            pltpu.SemaphoreType.DMA((locals_,)),
        ],
        compiler_params=pltpu.CompilerParams(
            collective_id=cid, has_side_effects=True, vmem_limit_bytes=48 * 2**20
        ),
        cost_estimate=takes(90),
        name="finish",
    )(part, unit, above, resid, inverse, gain, wide, narrow)


def heads_kernel(group, kind, x_ref, o_ref, through, local_sem, send_sem, recv_sem):
    band, tp = lax.axis_index("band"), lax.axis_index("tp")
    mine = lax.rem(band, group)
    base = band - mine
    others = [lax.rem(mine + d, group) for d in range(1, group)]
    sems = Sems(send_sem, recv_sem, local_sem)
    width = through.shape[1]

    def columns(index):
        return pl.ds(pl.multiple_of(index * width, width), width)

    def source(index):
        return x_ref.at[:, columns(index)] if kind == "cut" else x_ref.at[index]

    target = o_ref.at[:, columns(mine)] if kind == "join" else o_ref.at[mine]
    barrier = pltpu.get_barrier_semaphore()
    for other in others:
        pl.semaphore_signal(barrier, inc=1, device_id=(base + other, tp), device_id_type=MESH)
    load = sems.copy(source(mine), through)
    pl.semaphore_wait(barrier, group - 1)
    copies = [sems.send(source(other), target, (base + other, tp)) for other in others]
    load.wait()
    for copy in [sems.copy(through, target), *copies]:
        copy.wait()


def swap_heads(x, group, cid, kind):
    if kind == "cut":
        rows, width = x.shape[0], x.shape[1] // group
    else:
        rows, width = x.shape[1:]
    if width % 128 and kind == "cut":
        x = x.reshape(rows, group, width).transpose(1, 0, 2)
        return swap_heads(x, group, cid, "plain")
    if width % 128 and kind == "join":
        x = swap_heads(x, group, cid, "plain")
        return x.transpose(1, 0, 2).reshape(rows, group * width)
    shape = (rows, group * width) if kind == "join" else (group, rows, width)
    return pl.pallas_call(
        functools.partial(heads_kernel, group, kind),
        out_shape=jax.ShapeDtypeStruct(shape, x.dtype),
        in_specs=[anywhere],
        out_specs=anywhere,
        scratch_shapes=[
            pltpu.VMEM((rows, width), x.dtype),
            pltpu.SemaphoreType.DMA((2,)),
            pltpu.SemaphoreType.DMA((group - 1,)),
            pltpu.SemaphoreType.DMA((group - 1,)),
        ],
        compiler_params=pltpu.CompilerParams(collective_id=cid, has_side_effects=True),
        cost_estimate=takes(4),
        name="swap_heads",
    )(x)


def project_kernel(x_ref, w_ref, bias_ref, scale_ref, o_ref):
    total = nn(x_ref[...], w_ref[...]) + bias_ref[...]
    o_ref[0] = total.astype(bf16) * scale_ref[...].astype(bf16)


def project(x, weight, bias, scale, group):
    rows, depth = x.shape
    total_width = bias.shape[0]
    width = total_width // group
    if width % 128:
        total = (nn(x, weight[:, :total_width]) + bias).astype(bf16) * scale.astype(bf16)
        return total.reshape(rows, group, width).transpose(1, 0, 2)
    block = min(256, rows)
    return pl.pallas_call(
        project_kernel,
        out_shape=jax.ShapeDtypeStruct((group, rows, width), bf16),
        grid=(group, rows // block),
        in_specs=[
            pl.BlockSpec((block, depth), lambda g, i: (i, 0)),
            pl.BlockSpec((depth, width), lambda g, i: (0, g)),
            pl.BlockSpec((1, width), lambda g, i: (0, g)),
            pl.BlockSpec((1, width), lambda g, i: (0, g)),
        ],
        out_specs=pl.BlockSpec((1, block, width), lambda g, i: (g, i, 0)),
        compiler_params=pltpu.CompilerParams(vmem_limit_bytes=40 * 2**20),
        cost_estimate=pl.CostEstimate(
            flops=2 * rows * depth * width * group, bytes_accessed=12 * 2**20, transcendentals=0
        ),
        name="project",
    )(x, weight, bias[None], scale[None])


def products_kernel(split, left_ref, right_ref, other_ref, last_ref, o_ref):
    tile = min(512, o_ref.shape[0])

    def fill(x_ref, y_ref):
        def step(k, _):
            rows = pl.ds(pl.multiple_of(k * tile, tile), tile)
            o_ref[rows, :] = tn(x_ref[:, rows], y_ref[...]).astype(o_ref.dtype)
            return 0

        lax.fori_loop(0, o_ref.shape[0] // tile, step, 0)

    @pl.when(pl.program_id(0) < split)
    def _():
        fill(left_ref, right_ref)

    @pl.when(pl.program_id(0) >= split)
    def _():
        fill(other_ref, last_ref)


def two_products(left, right, other, last):
    rows, depth = left.shape
    width = last.shape[1]
    split = right.shape[1] // width
    whole = pl.BlockSpec((rows, depth), lambda j: (0, 0))
    return pl.pallas_call(
        functools.partial(products_kernel, split),
        out_shape=jax.ShapeDtypeStruct((depth, right.shape[1] + width), bf16),
        grid=(split + 1,),
        in_specs=[
            whole,
            pl.BlockSpec((rows, width), lambda j: (0, jnp.minimum(j, split - 1))),
            whole,
            pl.BlockSpec((rows, width), lambda j: (0, 0)),
        ],
        out_specs=pl.BlockSpec((depth, width), lambda j: (0, j)),
        compiler_params=pltpu.CompilerParams(vmem_limit_bytes=48 * 2**20),
        cost_estimate=takes(12),
        name="two_products",
    )(left, right, other, last)


def permitted(first, limit, row, column):
    return ((column >= first) & (column <= limit)) | (column == row)


def head_mask(head, shape):
    lane = lax.broadcasted_iota(jnp.int32, shape, 1)
    return (lane >= head * HEAD_DIM) & (lane < (head + 1) * HEAD_DIM)


def attend_kernel(qb, kb, info_ref, first_ref, q_ref, k_ref, v_ref, o_ref, log_ref, vt_ref):
    length, width = q_ref.shape
    heads = width // HEAD_DIM
    live_end = info_ref[0]
    count = lax.div(live_end + qb - 1, qb)
    vt_ref[...] = v_ref[...].T
    o_ref[...] = jnp.zeros_like(o_ref)
    log_ref[...] = jnp.zeros_like(log_ref)

    def queries(i, _):
        rows = pl.ds(pl.multiple_of(i * qb, qb), qb)
        q = q_ref[rows, :]
        first = first_ref[0:1, rows]
        row = i * qb + lax.broadcasted_iota(jnp.int32, (1, qb), 1)
        limit = jnp.minimum(row, live_end - 1)
        q_heads = [
            jnp.where(head_mask(h, (qb, width)), q, jnp.zeros_like(q)) for h in range(heads)
        ]
        def keys(j, carry):
            columns = pl.ds(pl.multiple_of(j * kb, kb), kb)
            k = k_ref[columns, :]
            column = j * kb + lax.broadcasted_iota(jnp.int32, (kb, 1), 0)
            allowed = permitted(first, limit, row, column)
            out = []
            for h in range(heads):
                top, total, summed = carry[h]
                scores = jnp.where(allowed, nt(k, q_heads[h]), masked_score)
                new_top = jnp.maximum(top, jnp.max(scores, axis=0, keepdims=True))
                weights = jnp.exp(scores - new_top)
                scale = jnp.exp(top - new_top)
                total = total * scale + jnp.sum(weights, axis=0, keepdims=True)
                vt = vt_ref[h * HEAD_DIM : (h + 1) * HEAD_DIM, columns]
                summed = summed * scale + nn(vt, weights.astype(bf16))
                out.append((new_top, total, summed))
            return tuple(out)
        start = tuple(
            (
                jnp.full((1, qb), masked_score, f32),
                jnp.zeros((1, qb), f32),
                jnp.zeros((HEAD_DIM, qb), f32),
            )
            for _ in range(heads)
        )
        lo = lax.div(info_ref[1 + i], kb)
        hi = lax.div(i * qb + qb - 1, kb) + 1
        done = lax.fori_loop(lo, hi, keys, start)
        mixed = jnp.concatenate([summed / total for _, total, summed in done], axis=0)
        o_ref[rows, :] = mixed.T.astype(o_ref.dtype)
        for h, (top, total, _) in enumerate(done):
            log_ref[0, h : h + 1, rows] = top + jnp.log(total)
        return 0
    lax.fori_loop(0, count, queries, 0)


def attend_back_kernel(
    qb, kb, info_ref, first_ref, q_ref, k_ref, v_ref, o_ref, do_ref, log_ref, out_ref, sum_ref,
    dk_acc, dv_acc,
):
    length, width = q_ref.shape
    heads = width // HEAD_DIM
    features = out_ref.shape[1] // 3
    slab = pl.program_id(0)
    factor = HEAD_DIM ** (-0.5)
    live_end = info_ref[0]
    count = lax.div(live_end + qb - 1, qb)

    def lanes(which):
        if features == width:
            return pl.ds(which * features, width)
        return pl.ds(pl.multiple_of(which * features + slab * width, width), width)
    dk_acc[...] = jnp.zeros_like(dk_acc)
    dv_acc[...] = jnp.zeros_like(dv_acc)
    out_ref[:, lanes(0)] = jnp.zeros((length, width), out_ref.dtype)

    def queries(i, _):
        rows = pl.ds(pl.multiple_of(i * qb, qb), qb)
        q, do = q_ref[rows, :], do_ref[rows, :]
        first = first_ref[0:1, rows]
        row = i * qb + lax.broadcasted_iota(jnp.int32, (1, qb), 1)
        limit = jnp.minimum(row, live_end - 1)
        dots = (do.astype(f32) * o_ref[rows, :].astype(f32)).T
        masks = [head_mask(h, (qb, width)) for h in range(heads)]
        kmasks = [head_mask(h, (kb, width)) for h in range(heads)]
        zero = jnp.zeros_like(q)
        q_heads = [jnp.where(mask, q, zero) for mask in masks]
        do_heads = [jnp.where(mask, do, zero) for mask in masks]
        logs = [log_ref[0, h : h + 1, rows] for h in range(heads)]
        deltas = [
            jnp.sum(dots[h * HEAD_DIM : (h + 1) * HEAD_DIM], axis=0, keepdims=True)
            for h in range(heads)
        ]
        def keys(j, dq):
            columns = pl.ds(pl.multiple_of(j * kb, kb), kb)
            k, v = k_ref[columns, :], v_ref[columns, :]
            column = j * kb + lax.broadcasted_iota(jnp.int32, (kb, 1), 0)
            allowed = permitted(first, limit, row, column)
            dk, dv = dk_acc[columns, :], dv_acc[columns, :]
            for h in range(heads):
                scores = jnp.where(allowed, nt(k, q_heads[h]) - logs[h], masked_score)
                probs = jnp.exp(scores)
                prob_grad = nt(v, do_heads[h])
                score_grad = (probs * (prob_grad - deltas[h])).astype(bf16)
                dv = dv + nn(probs.astype(bf16), do_heads[h])
                dk = dk + nn(score_grad, q_heads[h])
                dq = dq + tn(score_grad, jnp.where(kmasks[h], k, jnp.zeros_like(k)))
            dk_acc[columns, :] = dk
            dv_acc[columns, :] = dv
            return dq
        lo = lax.div(info_ref[1 + i], kb)
        hi = lax.div(i * qb + qb - 1, kb) + 1
        dq = lax.fori_loop(lo, hi, keys, jnp.zeros((qb, width), f32))
        out_ref[rows, lanes(0)] = (dq * factor).astype(out_ref.dtype)
        return 0
    lax.fori_loop(0, count, queries, 0)
    sum_ref[...] = jnp.zeros_like(sum_ref)

    def store(i, _):
        rows = pl.ds(pl.multiple_of(i * kb, kb), kb)
        dv = dv_acc[rows, :].astype(out_ref.dtype)
        out_ref[rows, lanes(1)] = dk_acc[rows, :].astype(out_ref.dtype)
        out_ref[rows, lanes(2)] = dv
        dq = out_ref[rows, lanes(0)].astype(f32)
        sum_ref[0, 0:1, :] += jnp.sum(dq, axis=0, keepdims=True)
        sum_ref[0, 1:2, :] += jnp.sum(dv.astype(f32), axis=0, keepdims=True)
        return 0
    lax.fori_loop(0, length // kb, store, 0)


def attention_specs(length, features):
    width = min(256, features)
    slabs = features // width

    plain = pl.BlockSpec((length, width), lambda i, info: (0, i))

    def piece(which):
        if features % 128:
            return plain
        return pl.BlockSpec((length, width), lambda i, info, w=which: (0, w * slabs + i))

    logs = pl.BlockSpec((1, 8, length), lambda i, info: (i, 0, 0))
    first = pl.BlockSpec((1, length), lambda i, info: (0, 0))
    return width, slabs, piece, plain, logs, first


def three(qkv, features):
    if features % 128:
        return [qkv[:, w * features : (w + 1) * features] for w in range(3)]
    return [qkv] * 3


def attend(qkv, info, first, qb, kb):
    length, features = qkv.shape[0], qkv.shape[1] // 3
    width, slabs, piece, plain, logs, first_spec = attention_specs(length, features)
    return pl.pallas_call(
        functools.partial(attend_kernel, qb, kb),
        out_shape=(
            jax.ShapeDtypeStruct((length, features), bf16),
            jax.ShapeDtypeStruct((slabs, 8, length), f32),
        ),
        grid_spec=pltpu.PrefetchScalarGridSpec(
            num_scalar_prefetch=1,
            grid=(slabs,),
            in_specs=[first_spec, piece(0), piece(1), piece(2)],
            out_specs=(plain, logs),
            scratch_shapes=[pltpu.VMEM((width, length), bf16)],
        ),
        compiler_params=pltpu.CompilerParams(vmem_limit_bytes=48 * 2**20),
        cost_estimate=takes(30),
        name="attend",
    )(info, first, *three(qkv, features))


def attend_back(qkv, mixed, grad, log_total, info, first, qb, kb):
    length, features = qkv.shape[0], qkv.shape[1] // 3
    width, slabs, piece, plain, logs, first_spec = attention_specs(length, features)
    return pl.pallas_call(
        functools.partial(attend_back_kernel, qb, kb),
        out_shape=(
            jax.ShapeDtypeStruct((length, 3 * features), bf16),
            jax.ShapeDtypeStruct((slabs, 8, width), f32),
        ),
        grid_spec=pltpu.PrefetchScalarGridSpec(
            num_scalar_prefetch=1,
            grid=(slabs,),
            in_specs=[first_spec, piece(0), piece(1), piece(2), plain, plain, logs],
            out_specs=(
                pl.BlockSpec((length, 3 * features), lambda i, info: (0, 0)),
                pl.BlockSpec((1, 8, width), lambda i, info: (i, 0, 0)),
            ),
            scratch_shapes=[pltpu.VMEM((length, width), f32), pltpu.VMEM((length, width), f32)],
        ),
        compiler_params=pltpu.CompilerParams(vmem_limit_bytes=48 * 2**20),
        cost_estimate=takes(34),
        name="attend_back",
    )(info, first, *three(qkv, features), mixed, grad, log_total)


def body(
    tokens,
    positions,
    doc_lengths,
    exit_depth,
    w_query,
    w_key,
    w_value,
    w_out,
    w_up,
    w_down,
    b_query,
    b_value,
    b_out,
    b_up,
    b_down,
    attn_gain,
    attn_bias,
    ffn_gain,
    ffn_bias,
    cotangent,
):
    seqs, local_rows, width = tokens.shape
    inner = b_query.shape[0]
    bands, tps = lax.axis_size("band"), lax.axis_size("tp")
    group = bands // seqs
    piece = local_rows // (group * tps)
    band, tp = lax.axis_index("band"), lax.axis_index("tp")
    seq, member = band // group, lax.rem(band, group)
    features = inner // group
    length = exit_depth.shape[1]
    own = bands * piece
    rows = tps * own
    block, half_block = min(512, length), min(256, length)

    def by_group(*parts):
        split = [p.reshape(p.shape[:-1] + (group, features)) for p in parts]
        return jnp.stack(split, axis=-2).reshape(parts[0].shape[:-1] + (-1,))

    def share(grad):
        return lax.psum_scatter(grad, "band", scatter_dimension=0, tiled=True)

    w_in_out = jnp.concatenate([by_group(w_query, w_key, w_value), w_out.T], axis=1)
    w_in_out = lax.all_gather(w_in_out, "band", axis=0, tiled=True)
    w_in, w_out_t = w_in_out[:, : 3 * inner], w_in_out[:, 3 * inner :]
    w_up_all = lax.all_gather(w_up, "band", axis=0, tiled=True)
    w_down_t = lax.all_gather(w_down.T, "band", axis=0, tiled=True)

    def my_share(array):
        split = array.reshape(seqs, group, tps, piece, width)
        return lax.dynamic_index_in_dim(split, tp, 2, keepdims=False).reshape(bands, piece, width)

    token_own, all_pos = transfer([Swap(my_share(tokens), positions)], 0, name="swap_in")
    seq_pos = lax.dynamic_index_in_dim(all_pos, seq, 1, keepdims=False)
    seq_pos = seq_pos.reshape(bands, group, tps, piece).transpose(1, 2, 0, 3)
    row_pos = seq_pos.reshape(length)
    member_pos = lax.dynamic_index_in_dim(seq_pos, member, 0, keepdims=False)
    own_pos = lax.dynamic_index_in_dim(member_pos, tp, 0, keepdims=False).reshape(own)
    depths = lax.dynamic_index_in_dim(exit_depth, seq, 0, keepdims=False)
    live_end = jnp.sum((depths > LAYER).astype(jnp.int32))
    live_own = (own_pos < live_end).astype(f32)[:, None]
    ends = jnp.cumsum(lax.dynamic_index_in_dim(doc_lengths, seq, 0, keepdims=False))
    places = jnp.arange(length, dtype=jnp.int32)
    first = jnp.max(jnp.where(ends[:, None] <= places[None, :], ends[:, None], 0), axis=0)
    info = jnp.concatenate([live_end[None], first[::block]]).astype(jnp.int32)
    first = first[None, :].astype(jnp.int32)
    to_sorted = (row_pos[None, :] == places[:, None]).astype(bf16)
    to_rows = (row_pos[:, None] == places[None, :]).astype(bf16)

    inputs = token_own.reshape(own, width).astype(f32)
    normed_in, unit_in, inverse_in = layer_norm(inputs, attn_gain, attn_bias)
    z1, grad_low = transfer([Gather(normed_in.astype(bf16)), Swap(my_share(cotangent))], 1, name="gather_in")
    z1 = z1.reshape(rows, width)
    grad_own = grad_low.reshape(own, width).astype(f32)
    down_grad_own = (live_own * grad_own).astype(bf16)
    down_grad = gather_later(down_grad_own)

    bias_in = by_group(b_query, jnp.zeros_like(b_query), b_value)
    scale_in = by_group(
        jnp.full_like(b_query, HEAD_DIM ** (-0.5)), jnp.ones_like(b_query), jnp.ones_like(b_query)
    )
    qkv = project(z1, w_in_out, bias_in, scale_in, group)
    qkv = swap_heads(qkv, group, 4, "plain").reshape(length, 3 * features)
    qkv = nn(to_sorted, qkv).astype(bf16)
    mixed_sorted, log_total = attend(qkv, info, first, block, block)
    mixed_sorted, down_grad = lax.optimization_barrier((mixed_sorted, down_grad))
    down_grad = down_grad.reshape(rows, width)
    mixed = nn(to_rows, mixed_sorted).astype(bf16).reshape(group, rows, features)
    mixed = swap_heads(mixed, group, 5, "join")

    attn_part = nt(mixed, w_out_t).astype(bf16).reshape(tps, own, width)
    (attn_out,) = transfer([Scatter(attn_part)], 6, name="scatter_attn")
    attn_out = attn_out + b_out
    residual = inputs + attn_out
    normed_mid, unit_mid, inverse_mid = layer_norm(residual, ffn_gain, ffn_bias)
    (z2,) = transfer([Gather(normed_mid.astype(bf16))], 7, name="gather_mid")
    z2 = z2.reshape(rows, width)
    pre_act = nn(z2, w_up_all) + b_up
    below = 0.5 * (1.0 + lax.erf(pre_act * 0.5**0.5))
    act = (pre_act * below).astype(bf16)
    slope = (below + pre_act * jnp.exp(-0.5 * pre_act * pre_act) * (2 * math.pi) ** -0.5).astype(bf16)

    ffn_part = nt(act, w_down_t).astype(bf16).reshape(tps, own, width)
    ffn_out, up_grad, mid_part, grad_w_down_t = transfer(
        [Scatter(ffn_part)],
        8,
        Work(
            [down_grad, w_down_t, slope, w_up_all, act],
            [("nn", 0, 1, 2, 0), ("nt", 5, 3, None, 1), ("tn", 0, 4, None, 2)],
            1,
        ),
        name="scatter_ffn",
    )
    shared_down = share(grad_w_down_t)
    output = (inputs + live_own * (attn_out + ffn_out + b_down)).astype(bf16)
    output = output.reshape(bands, piece, width)

    mid_part = mid_part.reshape(tps, own, width)
    mid_grad, output, grad_w_up, up_sums = transfer(
        [Scatter(mid_part), Swap(output)],
        9,
        Work([z2, up_grad], [("tn", 0, 1, None, 0), ("sum", 1, None, None, 1)], 1),
        name="scatter_mid",
    )
    resid_grad = norm_back(mid_grad, unit_mid, inverse_mid, ffn_gain)
    attn_grad_own = (live_own * grad_own + resid_grad).astype(bf16)
    (attn_grad,) = transfer([Gather(attn_grad_own)], 10, name="gather_back")
    attn_grad = attn_grad.reshape(rows, width)
    attn_grad, output = lax.optimization_barrier((attn_grad, output))
    output = gather_later(output)

    mixed_grad = nn(attn_grad, w_out_t).astype(bf16)
    mixed_grad = swap_heads(mixed_grad, group, 13, "cut").reshape(length, features)
    mixed_grad = nn(to_sorted, mixed_grad).astype(bf16)
    mixed_grad, grad_w_up = lax.optimization_barrier((mixed_grad, grad_w_up))
    grad_w_up, shared_down = lax.optimization_barrier((grad_w_up, shared_down))
    shared_up = share(grad_w_up)
    in_grad, in_sums = attend_back(
        qkv, mixed_sorted, mixed_grad, log_total, info, first, block, half_block
    )
    in_sums = in_sums.transpose(1, 0, 2).reshape(8, features)
    mine = (jnp.arange(group) == member).astype(f32)[:, None]
    in_grad = nn(to_rows, in_grad).astype(bf16).reshape(group, rows, 3 * features)
    in_grad = swap_heads(in_grad, group, 14, "join")
    in_part = nt(in_grad, w_in).astype(bf16).reshape(tps, bands, piece, width)
    in_part, in_grad = lax.optimization_barrier((in_part, in_grad))
    grad_w_in_out = two_products(z1, in_grad, attn_grad, mixed)
    grad_w_in_out, shared_up, in_part, output = lax.optimization_barrier(
        (grad_w_in_out, shared_up, in_part, output)
    )
    output = output.transpose(1, 0, 2, 3).reshape(tokens.shape)
    shared_in_out = share(grad_w_in_out)

    def over_rows(array):
        return jnp.sum(array.astype(f32), axis=0)

    wide = [
        over_rows(attn_grad_own),
        over_rows(down_grad_own),
        over_rows(mid_grad * unit_mid),
        over_rows(mid_grad),
    ]
    wide = jnp.concatenate(wide).astype(bf16).reshape(16, width // 4)
    narrow = jnp.concatenate(
        [(mine * in_sums[0]).reshape(-1), (mine * in_sums[1]).reshape(-1), up_sums[0]]
    )
    count = narrow.shape[0]
    narrow = jnp.pad(narrow, (0, -count % 2048)).astype(bf16).reshape(16, -1)
    token_grad, wide, narrow = finish(
        in_part,
        unit_in.reshape(bands, piece, width),
        grad_low,
        resid_grad.reshape(bands, piece, width),
        inverse_in.reshape(bands, piece, 1),
        attn_gain[None],
        wide,
        narrow,
        15,
    )
    token_grad = token_grad.reshape(tokens.shape).astype(f32)
    wide, late = wide[:16].reshape(4, width), wide[16:].reshape(2, width)
    narrow = narrow.reshape(-1)[:count]
    shared_in = shared_in_out[:, : 3 * inner].astype(f32).reshape(-1, group, 3, features)
    shared_down, shared_out = shared_down.astype(f32).T, shared_in_out[:, 3 * inner :].astype(f32).T
    shared_up = shared_up.astype(f32)
    shared_q, shared_k, shared_v = (
        shared_in[:, :, which].reshape(-1, inner) for which in range(3)
    )

    return (
        output,
        token_grad,
        shared_q,
        shared_k,
        shared_v,
        shared_out,
        shared_up,
        shared_down,
        narrow[:inner],
        narrow[inner : 2 * inner],
        wide[0],
        narrow[2 * inner :],
        wide[1],
        late[0],
        late[1],
        wide[2],
        wide[3],
    )


def solution(mesh):
    return jax.shard_map(
        body,
        mesh=mesh,
        in_specs=(
            P(None, "band", None),
            P(None, "band"),
            P(),
            P(),
            P("band", "tp"),
            P("band", "tp"),
            P("band", "tp"),
            P("tp", "band"),
            P("band", "tp"),
            P("tp", "band"),
            P("tp"),
            P("tp"),
            P(),
            P("tp"),
            P(),
            P(),
            P(),
            P(),
            P(),
            P(None, "band", None),
        ),
        out_specs=(
            P(None, "band", None),
            P(None, "band", None),
            P("band", "tp"),
            P("band", "tp"),
            P("band", "tp"),
            P("tp", "band"),
            P("band", "tp"),
            P("tp", "band"),
            P("tp"),
            P("tp"),
            P(),
            P("tp"),
            P(),
            P(),
            P(),
            P(),
            P(),
        ),
        check_vma=False,
    )
```

```python
import functools
import math

import jax
import jax.numpy as jnp
from jax import lax
from jax.experimental import pallas as pl
from jax.experimental.pallas import tpu as pltpu
from jax.sharding import PartitionSpec as P

HEAD_DIM = 64
LAYER = 12
MESH = pl.DeviceIdType.MESH

epsilon = 1e-05
masked_score = -1e30
bf16 = jnp.bfloat16
f32 = jnp.float32


def layer_norm(values, gain, shift):
    center = values - jnp.mean(values, axis=-1, keepdims=True)
    inverse = lax.rsqrt(jnp.mean(center * center, axis=-1, keepdims=True) + epsilon)
    normed = center * inverse
    return (normed * gain + shift, normed, inverse)


def norm_back(grad_out, normed, inverse, gain):
    scaled = grad_out * gain
    return inverse * (
        scaled
        - jnp.mean(scaled, axis=-1, keepdims=True)
        - normed * jnp.mean(scaled * normed, axis=-1, keepdims=True)
    )


def nn(left, right):
    return jnp.dot(left, right, preferred_element_type=f32)


def nt(left, right):
    return lax.dot_general(left, right, (((1,), (1,)), ((), ())), preferred_element_type=f32)


def tn(left, right):
    return lax.dot_general(left, right, (((0,), (0,)), ((), ())), preferred_element_type=f32)


def gelu_exact(values):
    return jax.nn.gelu(values, approximate=False)


def halves(count):
    return (count // 2, 2) if count % 2 == 0 else (count, 1)


def takes(microseconds):
    return pl.CostEstimate(
        flops=int(microseconds * 1e9), bytes_accessed=int(microseconds * 2e6), transcendentals=0
    )


class Sems:
    def __init__(self, send_sem, recv_sem, local_sem):
        self.send_sem, self.recv_sem, self.local_sem = send_sem, recv_sem, local_sem
        self.sent = self.local = 0

    def send(self, source, target, device):
        k = self.sent
        self.sent += 1
        copy = pltpu.make_async_remote_copy(
            source, target, self.send_sem.at[k], self.recv_sem.at[k],
            device_id=device, device_id_type=MESH,
        )
        copy.start()
        return copy

    def copy(self, source, target):
        k = self.local
        self.local += 1
        copy = pltpu.make_async_copy(source, target, self.local_sem.at[k])
        copy.start()
        return copy


class Grid:
    def __init__(self, count):
        self.na, self.nb = na, nb = halves(count)
        self.me, band = lax.axis_index("tp"), lax.axis_index("band")
        self.a, self.b = a, b = self.me // nb, lax.rem(self.me, nb)
        self.along_b = [(band, a * nb + lax.rem(b + d, nb)) for d in range(1, nb)]
        self.along_a = [(band, lax.rem(a + d, na) * nb + b) for d in range(1, na)]
        self.from_b = [a * nb + lax.rem(b + nb - d, nb) for d in range(1, nb)]
        self.from_a = [lax.rem(a + na - d, na) * nb + b for d in range(1, na)]


def tp_peers():
    grid = Grid(lax.axis_size("tp"))
    return grid.along_a + grid.along_b


def band_peers():
    size = lax.axis_size("band")
    me, tp = lax.axis_index("band"), lax.axis_index("tp")
    return [(lax.rem(me + d, size), tp) for d in range(1, size)]


anywhere = pl.BlockSpec(memory_space=pl.ANY)
vmem = pl.BlockSpec(memory_space=pltpu.VMEM)


class Gather:
    peers = "tp"

    def __init__(self, x, inner_slot=False, extra=None):
        self.count = count = lax.axis_size("tp")
        na, nb = halves(count)
        self.inner_slot, self.extra = inner_slot, extra is not None
        self.sends = 2 * (na - 1 + nb - 1) + 2 * (na - 1) * (nb - 1)
        self.locals = 2
        shape = (x.shape[0], count) + x.shape[1:] if inner_slot else (count,) + x.shape
        self.operands, self.in_specs = [x], [anywhere]
        self.shapes, self.out_specs = [jax.ShapeDtypeStruct(shape, x.dtype)], [anywhere]
        self.scratch = [pltpu.VMEM(x.shape, x.dtype)]
        if self.extra:
            self.operands.append(extra)
            self.in_specs.append(vmem)
            self.shapes.append(jax.ShapeDtypeStruct(extra.shape, extra.dtype))
            self.out_specs.append(vmem)
            self.sends += na - 1 + nb - 1
            self.scratch += [
                pltpu.VMEM(extra.shape, extra.dtype),
                pltpu.VMEM((max(nb - 1, 1),) + extra.shape, extra.dtype),
                pltpu.VMEM((max(na - 1, 1),) + extra.shape, extra.dtype),
            ]

    def slot(self, index, which):
        part = self.part[which]
        return self.out.at[part, index] if self.inner_slot else self.out.at[index, part]

    def begin(self, ins, outs, scratch, sems):
        self.grid = grid = Grid(self.count)
        self.sems = sems
        x, self.out = ins[0], outs[0]
        half = x.shape[0] // 2
        self.part = part = (pl.ds(0, half), pl.ds(half, half))
        self.through = scratch[0]
        self.load = sems.copy(x, self.through)
        me = grid.me
        if self.extra:
            self.more = (ins[1], outs[1], *scratch[1:])
            self.extra_b = [
                sems.send(ins[1], scratch[2].at[k], device) for k, device in enumerate(grid.along_b)
            ]
        top, low = x.at[part[0]], x.at[part[1]]
        self.first_b = [sems.send(top, self.slot(me, 0), device) for device in grid.along_b]
        self.first_a = [sems.send(low, self.slot(me, 1), device) for device in grid.along_a]
        self.second = [sems.send(top, self.slot(me, 0), device) for device in grid.along_a]
        self.second += [sems.send(low, self.slot(me, 1), device) for device in grid.along_b]

    def middle(self):
        grid, sems = self.grid, self.sems
        self.load.wait()
        whole = self.out.at[:, grid.me] if self.inner_slot else self.out.at[grid.me]
        self.store = sems.copy(self.through, whole)
        if self.extra:
            own, _, part_ref, in_b, in_a = self.more
            total = own[...]
            for k, copy in enumerate(self.extra_b):
                copy.wait_recv()
                total = total + in_b[k]
            part_ref[...] = total
            self.extra_a = [
                sems.send(part_ref, in_a.at[k], device) for k, device in enumerate(grid.along_a)
            ]
        for copy, source in zip(self.first_b, grid.from_b):
            copy.wait_recv()
            held = self.slot(source, 0)
            self.second += [sems.send(held, held, device) for device in grid.along_a]
        for copy, source in zip(self.first_a, grid.from_a):
            copy.wait_recv()
            held = self.slot(source, 1)
            self.second += [sems.send(held, held, device) for device in grid.along_b]

    def end(self):
        if self.extra:
            _, total_ref, part_ref, _, in_a = self.more
            total = part_ref[...]
            for k, copy in enumerate(self.extra_a):
                copy.wait_recv()
                total = total + in_a[k]
            total_ref[...] = total
            for copy in self.extra_a + self.extra_b:
                copy.wait_send()
        for copy in self.first_a + self.first_b:
            copy.wait_send()
        for copy in self.second:
            copy.wait()
        self.store.wait()


class Scatter:
    peers = "tp"

    def __init__(self, partial):
        self.count, rows, width = partial.shape
        na, nb = halves(self.count)
        block = (rows // 2, width)
        self.sends = 2 * (na - 1) * (nb - 1) + 2 * (na - 1 + nb - 1)
        self.locals = na + nb
        self.operands, self.in_specs = [partial], [anywhere]
        self.shapes, self.out_specs = [jax.ShapeDtypeStruct((rows, width), f32)], [vmem]

        def buffer(*lead):
            return pltpu.VMEM(tuple(max(n, 1) for n in lead) + block, partial.dtype)

        self.scratch = [
            buffer(na), buffer(nb), buffer(nb - 1, na), buffer(na - 1, nb),
            buffer(na - 1), buffer(nb - 1), buffer(na - 1), buffer(nb - 1),
        ]

    def begin(self, ins, outs, scratch, sems):
        self.grid = grid = Grid(self.count)
        self.sems, self.out, self.scratch_refs = sems, outs[0], scratch
        own_a, own_b, one_a, one_b = scratch[:4]
        part = ins[0]
        na, nb, a, b = grid.na, grid.nb, grid.a, grid.b
        half = part.shape[1] // 2
        self.top, self.low = top, low = pl.ds(0, half), pl.ds(half, half)
        self.order_a = order_a = list(range(1, na)) + [0]
        self.order_b = order_b = list(range(1, nb)) + [0]
        self.first_a, self.first_b = {}, {}
        for step in range(max(na, nb)):
            if step < na:
                e = order_a[step]
                row = lax.rem(a + e, na) * nb
                for d in range(1, nb):
                    source = part.at[row + lax.rem(b + d, nb), top]
                    self.first_b[d, e] = sems.send(source, one_a.at[d - 1, e], grid.along_b[d - 1])
            if step < nb:
                e = order_b[step]
                column = lax.rem(b + e, nb)
                for d in range(1, na):
                    source = part.at[lax.rem(a + d, na) * nb + column, low]
                    self.first_a[d, e] = sems.send(source, one_b.at[d - 1, e], grid.along_a[d - 1])
        self.local_a = {
            e: sems.copy(part.at[lax.rem(a + e, na) * nb + b, top], own_a.at[e]) for e in order_a
        }
        self.local_b = {
            e: sems.copy(part.at[a * nb + lax.rem(b + e, nb), low], own_b.at[e]) for e in order_b
        }

    def sum_a(self, e):
        own_a, _, one_a = self.scratch_refs[:3]
        self.local_a[e].wait()
        total = own_a[e].astype(f32)
        for d in range(1, self.grid.nb):
            self.first_b[d, e].wait_recv()
            total = total + one_a[d - 1, e].astype(f32)
        return total

    def sum_b(self, e):
        _, own_b, _, one_b = self.scratch_refs[:4]
        self.local_b[e].wait()
        total = own_b[e].astype(f32)
        for d in range(1, self.grid.na):
            self.first_a[d, e].wait_recv()
            total = total + one_b[d - 1, e].astype(f32)
        return total

    def middle(self):
        grid, sems = self.grid, self.sems
        out_a, out_b, two_a, two_b = self.scratch_refs[4:]
        self.second_a, self.second_b = {}, {}
        for e in self.order_a[:-1]:
            out_a[e - 1] = self.sum_a(e).astype(out_a.dtype)
            self.second_a[e] = sems.send(out_a.at[e - 1], two_a.at[e - 1], grid.along_a[e - 1])
        for e in self.order_b[:-1]:
            out_b[e - 1] = self.sum_b(e).astype(out_b.dtype)
            self.second_b[e] = sems.send(out_b.at[e - 1], two_b.at[e - 1], grid.along_b[e - 1])

    def end(self):
        _, _, two_a, two_b = self.scratch_refs[4:]
        total = self.sum_a(0)
        for e in self.order_a[:-1]:
            self.second_a[e].wait_recv()
            total = total + two_a[e - 1].astype(f32)
        self.out[self.top] = total
        total = self.sum_b(0)
        for e in self.order_b[:-1]:
            self.second_b[e].wait_recv()
            total = total + two_b[e - 1].astype(f32)
        self.out[self.low] = total
        for group in (self.first_a, self.first_b, self.second_a, self.second_b):
            for copy in group.values():
                copy.wait_send()


class Swap:
    peers = "band"

    def __init__(self, x, extra=None):
        size = lax.axis_size("band")
        arrays = [x] if extra is None else [x, extra]
        self.operands, self.in_specs = arrays, [anywhere] * len(arrays)
        self.shapes = [jax.ShapeDtypeStruct(x.shape, x.dtype)]
        self.scratch = [pltpu.VMEM(x.shape[1:], x.dtype)]
        if extra is not None:
            self.shapes.append(jax.ShapeDtypeStruct((size,) + extra.shape, extra.dtype))
            self.scratch.append(pltpu.VMEM(extra.shape, extra.dtype))
        self.out_specs = [anywhere] * len(arrays)
        self.sends = (size - 1) * len(arrays)
        self.locals = 2 * len(arrays)

    def begin(self, ins, outs, scratch, sems):
        me = lax.axis_index("band")
        self.sems, self.scratch_refs = sems, scratch
        self.slots = [out.at[me] for out in outs]
        self.loads = [sems.copy(ins[0].at[me], scratch[0])]
        if len(ins) > 1:
            self.loads.append(sems.copy(ins[1], scratch[1]))
        self.copies = []
        for peer in band_peers():
            if len(ins) > 1:
                self.copies.append(sems.send(ins[1], self.slots[1], peer))
            self.copies.append(sems.send(ins[0].at[peer[0]], self.slots[0], peer))

    def middle(self):
        self.stores = []
        for load, through, slot in zip(self.loads, self.scratch_refs, self.slots):
            load.wait()
            self.stores.append(self.sems.copy(through, slot))

    def end(self):
        for copy in self.copies + self.stores:
            copy.wait()


class Work:
    def __init__(self, operands, tasks, early):
        self.tasks, self.early = tasks, early
        self.operands = operands
        self.shapes = []
        for kind, left, right, _, _ in tasks:
            known = [*operands, *self.shapes]
            if kind == "sum":
                self.shapes.append(jax.ShapeDtypeStruct((1, known[left].shape[1]), f32))
                continue
            rows = known[left].shape[1 if kind == "tn" else 0]
            columns = known[right].shape[0 if kind == "nt" else 1]
            self.shapes.append(jax.ShapeDtypeStruct((rows, columns), bf16))
        self.scratch = [pltpu.VMEM(x.shape, x.dtype) for x in [*operands, *self.shapes]]
        self.locals = len(operands) + len(tasks)

    def begin(self, ins, outs, scratch, sems):
        self.sems, self.outs = sems, outs
        self.held, self.made = scratch[: len(ins)], scratch[len(ins) :]
        self.loads = [sems.copy(source, target) for source, target in zip(ins, self.held)]
        self.stores = []

    def ready(self, k):
        if k < len(self.loads) and self.loads[k] is not None:
            self.loads[k].wait()
            self.loads[k] = None

    def run(self, tasks):
        for kind, left, right, scale, out in tasks:
            for k in (left, right, scale):
                if k is not None:
                    self.ready(k)
            known = [*self.held, *self.made]
            x, made = known[left], self.made[out]
            if kind == "sum":
                rows = min(128, x.shape[0])
                made[...] = jnp.zeros_like(made)

                def add(k, _, x=x, made=made, rows=rows):
                    r = pl.ds(pl.multiple_of(k * rows, rows), rows)
                    made[...] += jnp.sum(x[r, :].astype(f32), axis=0, keepdims=True)
                    return 0

                lax.fori_loop(0, x.shape[0] // rows, add, 0)
                self.stores.append(self.sems.copy(made, self.outs[out]))
                continue
            y = known[right]
            factor = None if scale is None else self.held[scale]
            tile_r, tile_c = min(512, made.shape[0]), min(512, made.shape[1])
            columns = made.shape[1] // tile_c

            def tile(k, _, kind=kind, x=x, y=y, made=made, factor=factor):
                i, j = k // columns, lax.rem(k, columns)
                r = pl.ds(pl.multiple_of(i * tile_r, tile_r), tile_r)
                c = pl.ds(pl.multiple_of(j * tile_c, tile_c), tile_c)
                if kind == "tn":
                    total = tn(x[:, r], y[:, c])
                elif kind == "nt":
                    total = nt(x[r, :], y[c, :])
                else:
                    total = nn(x[r, :], y[:, c])
                if factor is not None:
                    total = total * factor[r, c].astype(f32)
                made[r, c] = total.astype(made.dtype)
                return 0

            lax.fori_loop(0, (made.shape[0] // tile_r) * columns, tile, 0)
            self.stores.append(self.sems.copy(made, self.outs[out]))

    def end(self):
        for store in self.stores:
            store.wait()


def transfer(parts, cid, work=None, name="transfer", time=36):
    items = list(parts) + ([work] if work is not None else [])
    sends = sum(part.sends for part in parts)
    locals_ = sum(item.locals for item in items)

    def kernel(*refs):
        refs = list(refs)

        def take(number):
            taken = refs[:number]
            del refs[:number]
            return taken

        ins = [take(len(item.operands)) for item in items]
        outs = [take(len(item.shapes)) for item in items]
        scratch = [take(len(item.scratch)) for item in items]
        sems = Sems(*refs)
        devices = []
        if any(part.peers == "tp" for part in parts):
            devices += tp_peers()
        if any(part.peers == "band" for part in parts):
            devices += band_peers()
        barrier = pltpu.get_barrier_semaphore()
        for device in devices:
            pl.semaphore_signal(barrier, inc=1, device_id=device, device_id_type=MESH)
        if work is not None:
            work.begin(ins[-1], outs[-1], scratch[-1], sems)
        pl.semaphore_wait(barrier, len(devices))
        for part, i, o, t in zip(parts, ins, outs, scratch):
            part.begin(i, o, t, sems)
        if work is not None:
            work.run(work.tasks[: work.early])
        for part in parts:
            part.middle()
        if work is not None:
            work.run(work.tasks[work.early :])
        for part in parts:
            part.end()
        if work is not None:
            work.end()

    in_specs = [spec for part in parts for spec in part.in_specs]
    out_specs = [spec for part in parts for spec in part.out_specs]
    if work is not None:
        in_specs += [anywhere] * len(work.operands)
        out_specs += [anywhere] * len(work.shapes)
    return pl.pallas_call(
        kernel,
        out_shape=tuple(shape for item in items for shape in item.shapes),
        in_specs=in_specs,
        out_specs=tuple(out_specs),
        scratch_shapes=[
            *(scratch for item in items for scratch in item.scratch),
            pltpu.SemaphoreType.DMA((sends,)),
            pltpu.SemaphoreType.DMA((sends,)),
            pltpu.SemaphoreType.DMA((locals_,)),
        ],
        compiler_params=pltpu.CompilerParams(
            collective_id=cid, has_side_effects=True, vmem_limit_bytes=(58 if work else 32) * 2**20
        ),
        cost_estimate=takes(time),
        name=name,
    )(*(operand for item in items for operand in item.operands))


def gather_later(x, axis=0):
    x = jnp.expand_dims(x, axis)
    copies = jnp.broadcast_to(x, x.shape[:axis] + (lax.axis_size("tp"),) + x.shape[axis + 1 :])
    return lax.all_to_all(copies, "tp", axis, axis)


class Block:
    def __init__(self, order, shift, grid, size):
        band = lax.axis_index("band")
        self.order, self.shift = order, shift
        self.to, self.source = lax.rem(band + shift, size), lax.rem(band + size - shift, size)
        if order % 2 == 0:
            self.n1, self.n2 = grid.nb, grid.na
            self.first, self.second, self.origin = grid.along_b, grid.along_a, grid.from_b
            self.index = lambda d, e: lax.rem(grid.a + e, grid.na) * grid.nb + lax.rem(
                grid.b + d, grid.nb
            )
        else:
            self.n1, self.n2 = grid.na, grid.nb
            self.first, self.second, self.origin = grid.along_a, grid.along_b, grid.from_a
            self.index = lambda d, e: lax.rem(grid.a + d, grid.na) * grid.nb + lax.rem(
                grid.b + e, grid.nb
            )


def finish_kernel(
    count, size, part, unit, above, resid, inverse, gain, wide, narrow,
    out, wide_out, narrow_out,
    own, one, two_out, two, made, arrived, late, late_in, wide_in, narrow_in, pair, pair_b, pair_a,
    send_sem, recv_sem, local_sem,
):
    grid = Grid(count)
    sems = Sems(send_sem, recv_sem, local_sem)
    band = lax.axis_index("band")
    peers = band_peers()
    devices = grid.along_a + grid.along_b + peers
    barrier = pltpu.get_barrier_semaphore()
    for device in devices:
        pl.semaphore_signal(barrier, inc=1, device_id=device, device_id_type=MESH)
    shifts = list(range(1, size)) + [0]
    blocks = [Block(k, shift, grid, size) for k, shift in enumerate(shifts)]
    late[...] = jnp.zeros_like(late)
    pl.semaphore_wait(barrier, len(devices))
    done = []

    for blk in blocks:
        k = blk.order
        seconds = list(range(1, blk.n2)) + [0]
        blk.one = {
            (d, e): sems.send(
                part.at[blk.index(d, e), blk.to], one.at[k, d - 1, e], blk.first[d - 1]
            )
            for e in seconds
            for d in range(1, blk.n1)
        }
        blk.own = {e: sems.copy(part.at[blk.index(0, e), blk.to], own.at[k, e]) for e in seconds}
    early = []
    for peer in peers:
        early.append(sems.send(wide, wide_in.at[band], peer))
        early.append(sems.send(narrow, narrow_in.at[band], peer))

    def first_sum(blk, e):
        k = blk.order
        blk.own[e].wait()
        total = own[k, e].astype(f32)
        for d in range(1, blk.n1):
            blk.one[d, e].wait_recv()
            total = total + one[k, d - 1, e].astype(f32)
        return total

    def pass_on(blk):
        k = blk.order
        blk.two = []
        for e in range(1, blk.n2):
            two_out[k, e - 1] = first_sum(blk, e).astype(bf16)
            blk.two.append(sems.send(two_out.at[k, e - 1], two.at[k, e - 1], blk.second[e - 1]))

    def complete(blk):
        k = blk.order
        grad = first_sum(blk, 0)
        for e, copy in enumerate(blk.two):
            copy.wait_recv()
            grad = grad + two[k, e].astype(f32)
        normed = unit[blk.to]
        scaled = grad * gain[...]
        mean = jnp.mean(scaled, axis=-1, keepdims=True)
        along = jnp.mean(scaled * normed, axis=-1, keepdims=True)
        base = above[blk.to].astype(f32) + resid[blk.to]
        token = base + inverse[blk.to] * (scaled - mean - normed * along)
        made[k] = token.astype(bf16)
        sums = (jnp.sum(grad * normed, axis=0, keepdims=True), jnp.sum(grad, axis=0, keepdims=True))
        quarter = late.shape[1]
        for which, total in enumerate(sums):
            for i in range(4):
                row = slice(4 * which + i, 4 * which + i + 1)
                late[row, :] = late[row, :] + total[:, i * quarter : (i + 1) * quarter]
        if blk.shift:
            blk.swap = sems.send(made.at[k], arrived.at[k], (blk.to, lax.axis_index("tp")))

    def relay(blk):
        k = blk.order
        if blk.shift:
            blk.swap.wait_recv()
            held = arrived.at[k]
        else:
            held = made.at[k]
        slot = out.at[blk.source, grid.me]
        blk.near = [sems.send(held, slot, device) for device in blk.first]
        blk.far = [sems.send(held, slot, device) for device in blk.second]
        done.append(sems.copy(held, slot))

    def forward(blk):
        for copy, source in zip(blk.near, blk.origin):
            copy.wait_recv()
            held = out.at[blk.source, source]
            blk.far += [sems.send(held, held, device) for device in blk.second]

    pairs = [blocks[k : k + 2] for k in range(0, size, 2)]
    stages = (pass_on, complete, relay, forward)
    for step in range(len(pairs) + len(stages) - 1):
        for behind, stage in enumerate(stages):
            if 0 <= step - behind < len(pairs):
                for blk in pairs[step - behind]:
                    stage(blk)
        if step == len(pairs):
            last = [sems.send(late, late_in.at[band], peer) for peer in peers]

    for copy in early + last:
        copy.wait_recv()
    wide_in[band] = wide[...]
    narrow_in[band] = narrow[...]
    late_in[band] = late[...]
    total, narrow_total, late_total = (
        sum(array[k].astype(f32) for k in range(size)) for array in (wide_in, narrow_in, late_in)
    )
    narrow_out[...] = narrow_total
    pair[0:16, :] = total
    pair[16:24, :] = late_total
    near = [sems.send(pair, pair_b.at[k], device) for k, device in enumerate(grid.along_b)]
    total = pair[...]
    for k, copy in enumerate(near):
        copy.wait_recv()
        total = total + pair_b[k]
    for copy in near:
        copy.wait_send()
    pair[...] = total
    far = [sems.send(pair, pair_a.at[k], device) for k, device in enumerate(grid.along_a)]
    for k, copy in enumerate(far):
        copy.wait_recv()
        total = total + pair_a[k]
    wide_out[...] = total

    for copy in early + last + far:
        copy.wait_send()
    for blk in blocks:
        for copy in [*blk.one.values(), *blk.two, *blk.near]:
            copy.wait_send()
        if blk.shift:
            blk.swap.wait_send()
        for copy in blk.far:
            copy.wait()
    for copy in done:
        copy.wait()


def finish(part, unit, above, resid, inverse, gain, wide, narrow, cid):
    count, size, rows, width = part.shape
    na, nb = halves(count)
    most = max(na, nb)
    sends = locals_ = 0
    for k in range(size):
        n1, n2 = (nb, na) if k % 2 == 0 else (na, nb)
        sends += (n1 - 1) * n2 + 2 * (n2 - 1) + (n1 - 1) + (n1 - 1) * (n2 - 1)
        locals_ += n2 + 1
    sends += 4 * (size - 1) + na - 1 + nb - 1
    lanes = wide.shape[1]

    def blocks(*lead):
        return pltpu.VMEM(tuple(max(n, 1) for n in lead) + (rows, width), bf16)

    return pl.pallas_call(
        functools.partial(finish_kernel, count, size),
        out_shape=(
            jax.ShapeDtypeStruct((size, count, rows, width), bf16),
            jax.ShapeDtypeStruct((24, lanes), f32),
            jax.ShapeDtypeStruct(narrow.shape, f32),
        ),
        in_specs=[anywhere] + [vmem] * 7,
        out_specs=(anywhere, vmem, vmem),
        scratch_shapes=[
            blocks(size, most), blocks(size, most - 1, most),
            blocks(size, most - 1), blocks(size, most - 1),
            blocks(size), blocks(size),
            pltpu.VMEM((8, lanes), f32),
            pltpu.VMEM((size, 8, lanes), f32),
            pltpu.VMEM((size,) + wide.shape, bf16),
            pltpu.VMEM((size,) + narrow.shape, bf16),
            pltpu.VMEM((24, lanes), f32),
            pltpu.VMEM((max(nb - 1, 1), 24, lanes), f32),
            pltpu.VMEM((max(na - 1, 1), 24, lanes), f32),
            pltpu.SemaphoreType.DMA((sends,)),
            pltpu.SemaphoreType.DMA((sends,)),
            pltpu.SemaphoreType.DMA((locals_,)),
        ],
        compiler_params=pltpu.CompilerParams(
            collective_id=cid, has_side_effects=True, vmem_limit_bytes=48 * 2**20
        ),
        cost_estimate=takes(90),
        name="finish",
    )(part, unit, above, resid, inverse, gain, wide, narrow)


def heads_kernel(group, kind, x_ref, o_ref, through, local_sem, send_sem, recv_sem):
    band, tp = lax.axis_index("band"), lax.axis_index("tp")
    mine = lax.rem(band, group)
    base = band - mine
    others = [lax.rem(mine + d, group) for d in range(1, group)]
    sems = Sems(send_sem, recv_sem, local_sem)
    width = through.shape[1]

    def columns(index):
        return pl.ds(pl.multiple_of(index * width, width), width)

    def source(index):
        return x_ref.at[:, columns(index)] if kind == "cut" else x_ref.at[index]

    target = o_ref.at[:, columns(mine)] if kind == "join" else o_ref.at[mine]
    barrier = pltpu.get_barrier_semaphore()
    for other in others:
        pl.semaphore_signal(barrier, inc=1, device_id=(base + other, tp), device_id_type=MESH)
    load = sems.copy(source(mine), through)
    pl.semaphore_wait(barrier, group - 1)
    copies = [sems.send(source(other), target, (base + other, tp)) for other in others]
    load.wait()
    for copy in [sems.copy(through, target), *copies]:
        copy.wait()


def swap_heads(x, group, cid, kind):
    if kind == "cut":
        rows, width = x.shape[0], x.shape[1] // group
    else:
        rows, width = x.shape[1:]
    if width % 128 and kind == "cut":
        x = x.reshape(rows, group, width).transpose(1, 0, 2)
        return swap_heads(x, group, cid, "plain")
    if width % 128 and kind == "join":
        x = swap_heads(x, group, cid, "plain")
        return x.transpose(1, 0, 2).reshape(rows, group * width)
    shape = (rows, group * width) if kind == "join" else (group, rows, width)
    return pl.pallas_call(
        functools.partial(heads_kernel, group, kind),
        out_shape=jax.ShapeDtypeStruct(shape, x.dtype),
        in_specs=[anywhere],
        out_specs=anywhere,
        scratch_shapes=[
            pltpu.VMEM((rows, width), x.dtype),
            pltpu.SemaphoreType.DMA((2,)),
            pltpu.SemaphoreType.DMA((group - 1,)),
            pltpu.SemaphoreType.DMA((group - 1,)),
        ],
        compiler_params=pltpu.CompilerParams(collective_id=cid, has_side_effects=True),
        cost_estimate=takes(4),
        name="swap_heads",
    )(x)


def settle_kernel(
    wides, grad_ref, out_ref, up_ref, down_ref, wide_ref, narrow_ref,
    grad_to, out_to, up_to, down_to, *small,
):
    grad_to[...] = grad_ref[...].astype(f32)
    out_to[0] = out_ref[:, 0]
    up_to[...] = up_ref[...].astype(f32)
    down_to[...] = down_ref[...].astype(f32).T

    @pl.when(pl.program_id(0) == 0)
    def _():
        for refs, source in ((small[:wides], wide_ref), (small[wides:], narrow_ref)):
            lanes, row = source.shape[1], 0
            for ref in refs:
                for i in range(ref.shape[1] // lanes):
                    ref[0:1, i * lanes : (i + 1) * lanes] = source[row : row + 1, :]
                    row += 1


def settle(grad, out, up, down, wide, narrow, widths):
    size, count, rows, width = grad.shape
    wides = wide.shape[0] * wide.shape[1] // width
    slab = down.shape[1] // size
    small = [width] * wides + list(widths)
    block = pl.BlockSpec((1, count, rows, width), lambda i: (i, 0, 0, 0))
    across = pl.BlockSpec((up.shape[0] // size, up.shape[1]), lambda i: (i, 0))
    if up.shape[0] // size % 16:
        across = pl.BlockSpec(up.shape, lambda i: (0, 0))
    return pl.pallas_call(
        functools.partial(settle_kernel, wides),
        out_shape=(
            jax.ShapeDtypeStruct(grad.shape, f32),
            jax.ShapeDtypeStruct(grad.shape, out.dtype),
            jax.ShapeDtypeStruct(up.shape, f32),
            jax.ShapeDtypeStruct(down.shape[::-1], f32),
            *(jax.ShapeDtypeStruct((1, n), f32) for n in small),
        ),
        grid=(size,),
        in_specs=[
            block,
            pl.BlockSpec((count, 1, rows, width), lambda i: (0, i, 0, 0)),
            across,
            pl.BlockSpec((down.shape[0], slab), lambda i: (0, i)) if slab % 128 == 0 else vmem,
            pl.BlockSpec(wide.shape, lambda i: (0, 0)),
            pl.BlockSpec(narrow.shape, lambda i: (0, 0)),
        ],
        out_specs=(
            block,
            block,
            across,
            pl.BlockSpec((slab, down.shape[0]), lambda i: (i, 0)) if slab % 128 == 0 else vmem,
            *(pl.BlockSpec((1, n), lambda i: (0, 0)) for n in small),
        ),
        compiler_params=pltpu.CompilerParams(vmem_limit_bytes=40 * 2**20),
        cost_estimate=takes(10),
        name="settle",
    )(grad, out, up, down, wide, narrow)


def split_kernel(group, features, x_ref, q_ref, k_ref, v_ref, out_ref):
    for g in range(group):
        for which, ref in enumerate((q_ref, k_ref, v_ref)):
            start = (3 * g + which) * features
            ref[:, g * features : (g + 1) * features] = x_ref[:, start : start + features].astype(f32)
    out_ref[...] = x_ref[:, 3 * group * features :].astype(f32).T


def split_shared(x, group, features):
    rows, inner = x.shape[0], group * features
    return pl.pallas_call(
        functools.partial(split_kernel, group, features),
        out_shape=(
            *[jax.ShapeDtypeStruct((rows, inner), f32)] * 3,
            jax.ShapeDtypeStruct((x.shape[1] - 3 * inner, rows), f32),
        ),
        in_specs=[vmem],
        out_specs=(vmem,) * 4,
        compiler_params=pltpu.CompilerParams(vmem_limit_bytes=32 * 2**20),
        cost_estimate=takes(2),
        name="split_shared",
    )(x)


def project_kernel(x_ref, w_ref, bias_ref, scale_ref, o_ref):
    total = nn(x_ref[...], w_ref[...]) + bias_ref[...]
    o_ref[0] = total.astype(bf16) * scale_ref[...].astype(bf16)


def project(x, weight, bias, scale, group):
    rows, depth = x.shape
    total_width = bias.shape[0]
    width = total_width // group
    if width % 128:
        total = (nn(x, weight[:, :total_width]) + bias).astype(bf16) * scale.astype(bf16)
        return total.reshape(rows, group, width).transpose(1, 0, 2)
    block = min(256, rows)
    return pl.pallas_call(
        project_kernel,
        out_shape=jax.ShapeDtypeStruct((group, rows, width), bf16),
        grid=(group, rows // block),
        in_specs=[
            pl.BlockSpec((block, depth), lambda g, i: (i, 0)),
            pl.BlockSpec((depth, width), lambda g, i: (0, g)),
            pl.BlockSpec((1, width), lambda g, i: (0, g)),
            pl.BlockSpec((1, width), lambda g, i: (0, g)),
        ],
        out_specs=pl.BlockSpec((1, block, width), lambda g, i: (g, i, 0)),
        compiler_params=pltpu.CompilerParams(vmem_limit_bytes=40 * 2**20),
        cost_estimate=pl.CostEstimate(
            flops=2 * rows * depth * width * group, bytes_accessed=12 * 2**20, transcendentals=0
        ),
        name="project",
    )(x, weight, bias[None], scale[None])


def products_kernel(left_ref, right_ref, other_ref, last_ref, o_ref):
    tile, width = last_ref.shape[1], right_ref.shape[1]

    def step(k, _):
        columns = pl.ds(pl.multiple_of(k * tile, tile), tile)
        o_ref[:, columns] = tn(left_ref[...], right_ref[:, columns]).astype(o_ref.dtype)
        return 0

    lax.fori_loop(0, width // tile, step, 0)
    o_ref[:, width:] = tn(other_ref[...], last_ref[...]).astype(o_ref.dtype)


def two_products(left, right, other, last):
    rows, depth = left.shape
    width, more = right.shape[1], last.shape[1]
    tile = min(512, depth)
    cut = pl.BlockSpec((rows, tile), lambda i: (0, i))
    return pl.pallas_call(
        products_kernel,
        out_shape=jax.ShapeDtypeStruct((depth, width + more), bf16),
        grid=(depth // tile,),
        in_specs=[
            cut,
            pl.BlockSpec((rows, width), lambda i: (0, 0)),
            cut,
            pl.BlockSpec((rows, more), lambda i: (0, 0)),
        ],
        out_specs=pl.BlockSpec((tile, width + more), lambda i: (i, 0)),
        compiler_params=pltpu.CompilerParams(vmem_limit_bytes=48 * 2**20),
        cost_estimate=takes(12),
        name="two_products",
    )(left, right, other, last)


def permitted(first, limit, row, column):
    return ((column >= first) & (column <= limit)) | (column == row)


def head_mask(head, shape):
    lane = lax.broadcasted_iota(jnp.int32, shape, 1)
    return (lane >= head * HEAD_DIM) & (lane < (head + 1) * HEAD_DIM)


def attend_kernel(qb, kb, info_ref, first_ref, q_ref, k_ref, v_ref, o_ref, log_ref, vt_ref):
    length, width = q_ref.shape
    heads = width // HEAD_DIM
    live_end = info_ref[0]
    count = lax.div(live_end + qb - 1, qb)
    vt_ref[...] = v_ref[...].T
    o_ref[...] = jnp.zeros_like(o_ref)
    log_ref[...] = jnp.zeros_like(log_ref)

    def queries(i, _):
        rows = pl.ds(pl.multiple_of(i * qb, qb), qb)
        q = q_ref[rows, :]
        first = first_ref[0:1, rows]
        row = i * qb + lax.broadcasted_iota(jnp.int32, (1, qb), 1)
        limit = jnp.minimum(row, live_end - 1)
        q_heads = [
            jnp.where(head_mask(h, (qb, width)), q, jnp.zeros_like(q)) for h in range(heads)
        ]
        def keys(j, carry):
            columns = pl.ds(pl.multiple_of(j * kb, kb), kb)
            k = k_ref[columns, :]
            column = j * kb + lax.broadcasted_iota(jnp.int32, (kb, 1), 0)
            allowed = permitted(first, limit, row, column)
            out = []
            for h in range(heads):
                top, total, summed = carry[h]
                scores = jnp.where(allowed, nt(k, q_heads[h]), masked_score)
                new_top = jnp.maximum(top, jnp.max(scores, axis=0, keepdims=True))
                weights = jnp.exp(scores - new_top)
                scale = jnp.exp(top - new_top)
                total = total * scale + jnp.sum(weights, axis=0, keepdims=True)
                vt = vt_ref[h * HEAD_DIM : (h + 1) * HEAD_DIM, columns]
                summed = summed * scale + nn(vt, weights.astype(bf16))
                out.append((new_top, total, summed))
            return tuple(out)
        start = tuple(
            (
                jnp.full((1, qb), masked_score, f32),
                jnp.zeros((1, qb), f32),
                jnp.zeros((HEAD_DIM, qb), f32),
            )
            for _ in range(heads)
        )
        lo = lax.div(info_ref[1 + i], kb)
        hi = lax.div(i * qb + qb - 1, kb) + 1
        done = lax.fori_loop(lo, hi, keys, start)
        mixed = jnp.concatenate([summed / total for _, total, summed in done], axis=0)
        o_ref[rows, :] = mixed.T.astype(o_ref.dtype)
        for h, (top, total, _) in enumerate(done):
            log_ref[0, h : h + 1, rows] = top + jnp.log(total)
        return 0
    lax.fori_loop(0, count, queries, 0)


def attend_back_kernel(
    qb, kb, info_ref, first_ref, q_ref, k_ref, v_ref, o_ref, do_ref, log_ref, out_ref, sum_ref,
    dk_acc, dv_acc,
):
    length, width = q_ref.shape
    heads = width // HEAD_DIM
    features = out_ref.shape[1] // 3
    slab = pl.program_id(0)
    factor = HEAD_DIM ** (-0.5)
    live_end = info_ref[0]
    count = lax.div(live_end + qb - 1, qb)

    def lanes(which):
        if features == width:
            return pl.ds(which * features, width)
        return pl.ds(pl.multiple_of(which * features + slab * width, width), width)
    dk_acc[...] = jnp.zeros_like(dk_acc)
    dv_acc[...] = jnp.zeros_like(dv_acc)
    out_ref[:, lanes(0)] = jnp.zeros((length, width), out_ref.dtype)

    def queries(i, _):
        rows = pl.ds(pl.multiple_of(i * qb, qb), qb)
        q, do = q_ref[rows, :], do_ref[rows, :]
        first = first_ref[0:1, rows]
        row = i * qb + lax.broadcasted_iota(jnp.int32, (1, qb), 1)
        limit = jnp.minimum(row, live_end - 1)
        dots = (do.astype(f32) * o_ref[rows, :].astype(f32)).T
        masks = [head_mask(h, (qb, width)) for h in range(heads)]
        kmasks = [head_mask(h, (kb, width)) for h in range(heads)]
        zero = jnp.zeros_like(q)
        q_heads = [jnp.where(mask, q, zero) for mask in masks]
        do_heads = [jnp.where(mask, do, zero) for mask in masks]
        logs = [log_ref[0, h : h + 1, rows] for h in range(heads)]
        deltas = [
            jnp.sum(dots[h * HEAD_DIM : (h + 1) * HEAD_DIM], axis=0, keepdims=True)
            for h in range(heads)
        ]
        def keys(j, dq):
            columns = pl.ds(pl.multiple_of(j * kb, kb), kb)
            k, v = k_ref[columns, :], v_ref[columns, :]
            column = j * kb + lax.broadcasted_iota(jnp.int32, (kb, 1), 0)
            allowed = permitted(first, limit, row, column)
            dk, dv = dk_acc[columns, :], dv_acc[columns, :]
            for h in range(heads):
                scores = jnp.where(allowed, nt(k, q_heads[h]) - logs[h], masked_score)
                probs = jnp.exp(scores)
                prob_grad = nt(v, do_heads[h])
                score_grad = (probs * (prob_grad - deltas[h])).astype(bf16)
                dv = dv + nn(probs.astype(bf16), do_heads[h])
                dk = dk + nn(score_grad, q_heads[h])
                dq = dq + tn(score_grad, jnp.where(kmasks[h], k, jnp.zeros_like(k)))
            dk_acc[columns, :] = dk
            dv_acc[columns, :] = dv
            return dq
        lo = lax.div(info_ref[1 + i], kb)
        hi = lax.div(i * qb + qb - 1, kb) + 1
        dq = lax.fori_loop(lo, hi, keys, jnp.zeros((qb, width), f32))
        out_ref[rows, lanes(0)] = (dq * factor).astype(out_ref.dtype)
        return 0
    lax.fori_loop(0, count, queries, 0)
    sum_ref[...] = jnp.zeros_like(sum_ref)

    def store(i, _):
        rows = pl.ds(pl.multiple_of(i * kb, kb), kb)
        dv = dv_acc[rows, :].astype(out_ref.dtype)
        out_ref[rows, lanes(1)] = dk_acc[rows, :].astype(out_ref.dtype)
        out_ref[rows, lanes(2)] = dv
        dq = out_ref[rows, lanes(0)].astype(f32)
        sum_ref[0, 0:1, :] += jnp.sum(dq, axis=0, keepdims=True)
        sum_ref[0, 1:2, :] += jnp.sum(dv.astype(f32), axis=0, keepdims=True)
        return 0
    lax.fori_loop(0, length // kb, store, 0)


def attention_specs(length, features):
    width = min(256, features)
    slabs = features // width

    plain = pl.BlockSpec((length, width), lambda i, info: (0, i))

    def piece(which):
        if features % 128:
            return plain
        return pl.BlockSpec((length, width), lambda i, info, w=which: (0, w * slabs + i))

    logs = pl.BlockSpec((1, 8, length), lambda i, info: (i, 0, 0))
    first = pl.BlockSpec((1, length), lambda i, info: (0, 0))
    return width, slabs, piece, plain, logs, first


def three(qkv, features):
    if features % 128:
        return [qkv[:, w * features : (w + 1) * features] for w in range(3)]
    return [qkv] * 3


def attend(qkv, info, first, qb, kb):
    length, features = qkv.shape[0], qkv.shape[1] // 3
    width, slabs, piece, plain, logs, first_spec = attention_specs(length, features)
    return pl.pallas_call(
        functools.partial(attend_kernel, qb, kb),
        out_shape=(
            jax.ShapeDtypeStruct((length, features), bf16),
            jax.ShapeDtypeStruct((slabs, 8, length), f32),
        ),
        grid_spec=pltpu.PrefetchScalarGridSpec(
            num_scalar_prefetch=1,
            grid=(slabs,),
            in_specs=[first_spec, piece(0), piece(1), piece(2)],
            out_specs=(plain, logs),
            scratch_shapes=[pltpu.VMEM((width, length), bf16)],
        ),
        compiler_params=pltpu.CompilerParams(vmem_limit_bytes=48 * 2**20),
        cost_estimate=takes(30),
        name="attend",
    )(info, first, *three(qkv, features))


def attend_back(qkv, mixed, grad, log_total, info, first, qb, kb):
    length, features = qkv.shape[0], qkv.shape[1] // 3
    width, slabs, piece, plain, logs, first_spec = attention_specs(length, features)
    return pl.pallas_call(
        functools.partial(attend_back_kernel, qb, kb),
        out_shape=(
            jax.ShapeDtypeStruct((length, 3 * features), bf16),
            jax.ShapeDtypeStruct((slabs, 8, width), f32),
        ),
        grid_spec=pltpu.PrefetchScalarGridSpec(
            num_scalar_prefetch=1,
            grid=(slabs,),
            in_specs=[first_spec, piece(0), piece(1), piece(2), plain, plain, logs],
            out_specs=(
                pl.BlockSpec((length, 3 * features), lambda i, info: (0, 0)),
                pl.BlockSpec((1, 8, width), lambda i, info: (i, 0, 0)),
            ),
            scratch_shapes=[pltpu.VMEM((length, width), f32), pltpu.VMEM((length, width), f32)],
        ),
        compiler_params=pltpu.CompilerParams(vmem_limit_bytes=48 * 2**20),
        cost_estimate=takes(34),
        name="attend_back",
    )(info, first, *three(qkv, features), mixed, grad, log_total)


def body(
    tokens,
    positions,
    doc_lengths,
    exit_depth,
    w_query,
    w_key,
    w_value,
    w_out,
    w_up,
    w_down,
    b_query,
    b_value,
    b_out,
    b_up,
    b_down,
    attn_gain,
    attn_bias,
    ffn_gain,
    ffn_bias,
    cotangent,
):
    seqs, local_rows, width = tokens.shape
    inner = b_query.shape[0]
    bands, tps = lax.axis_size("band"), lax.axis_size("tp")
    group = bands // seqs
    piece = local_rows // (group * tps)
    band, tp = lax.axis_index("band"), lax.axis_index("tp")
    seq, member = band // group, lax.rem(band, group)
    features = inner // group
    length = exit_depth.shape[1]
    own = bands * piece
    rows = tps * own
    block, half_block = min(512, length), min(256, length)

    def by_group(*parts):
        split = [p.reshape(p.shape[:-1] + (group, features)) for p in parts]
        return jnp.stack(split, axis=-2).reshape(parts[0].shape[:-1] + (-1,))

    def share(grad):
        return lax.psum_scatter(grad, "band", scatter_dimension=0, tiled=True)

    w_in_out = jnp.concatenate([by_group(w_query, w_key, w_value), w_out.T], axis=1)
    w_in_out = lax.all_gather(w_in_out, "band", axis=0, tiled=True)
    w_in, w_out_t = w_in_out[:, : 3 * inner], w_in_out[:, 3 * inner :]
    w_up_all = lax.all_gather(w_up, "band", axis=0, tiled=True)
    w_down_t = lax.all_gather(w_down.T, "band", axis=0, tiled=True)

    def my_share(array):
        split = array.reshape(seqs, group, tps, piece, width)
        return lax.dynamic_index_in_dim(split, tp, 2, keepdims=False).reshape(bands, piece, width)

    token_own, all_pos = transfer([Swap(my_share(tokens), positions)], 0, name="swap_in")
    seq_pos = lax.dynamic_index_in_dim(all_pos, seq, 1, keepdims=False)
    seq_pos = seq_pos.reshape(bands, group, tps, piece).transpose(1, 2, 0, 3)
    row_pos = seq_pos.reshape(length)
    member_pos = lax.dynamic_index_in_dim(seq_pos, member, 0, keepdims=False)
    own_pos = lax.dynamic_index_in_dim(member_pos, tp, 0, keepdims=False).reshape(own)
    depths = lax.dynamic_index_in_dim(exit_depth, seq, 0, keepdims=False)
    live_end = jnp.sum((depths > LAYER).astype(jnp.int32))
    live_own = (own_pos < live_end).astype(f32)[:, None]
    ends = jnp.cumsum(lax.dynamic_index_in_dim(doc_lengths, seq, 0, keepdims=False))
    places = jnp.arange(length, dtype=jnp.int32)
    first = jnp.max(jnp.where(ends[:, None] <= places[None, :], ends[:, None], 0), axis=0)
    info = jnp.concatenate([live_end[None], first[::block]]).astype(jnp.int32)
    first = first[None, :].astype(jnp.int32)
    to_sorted = (row_pos[None, :] == places[:, None]).astype(bf16)
    to_rows = (row_pos[:, None] == places[None, :]).astype(bf16)

    inputs = token_own.reshape(own, width).astype(f32)
    normed_in, unit_in, inverse_in = layer_norm(inputs, attn_gain, attn_bias)
    z1, grad_low = transfer([Gather(normed_in.astype(bf16)), Swap(my_share(cotangent))], 1, name="gather_in")
    z1 = z1.reshape(rows, width)
    grad_own = grad_low.reshape(own, width).astype(f32)
    down_grad_own = (live_own * grad_own).astype(bf16)
    down_grad = gather_later(down_grad_own)

    bias_in = by_group(b_query, jnp.zeros_like(b_query), b_value)
    scale_in = by_group(
        jnp.full_like(b_query, HEAD_DIM ** (-0.5)), jnp.ones_like(b_query), jnp.ones_like(b_query)
    )
    qkv = project(z1, w_in_out, bias_in, scale_in, group)
    qkv = swap_heads(qkv, group, 4, "plain").reshape(length, 3 * features)
    qkv = nn(to_sorted, qkv).astype(bf16)
    mixed_sorted, log_total = attend(qkv, info, first, block, block)
    mixed_sorted, down_grad = lax.optimization_barrier((mixed_sorted, down_grad))
    down_grad = down_grad.reshape(rows, width)
    mixed = nn(to_rows, mixed_sorted).astype(bf16).reshape(group, rows, features)
    mixed = swap_heads(mixed, group, 5, "join")

    attn_part = nt(mixed, w_out_t).astype(bf16).reshape(tps, own, width)
    (attn_out,) = transfer([Scatter(attn_part)], 6, name="scatter_attn")
    attn_out = attn_out + b_out
    residual = inputs + attn_out
    normed_mid, unit_mid, inverse_mid = layer_norm(residual, ffn_gain, ffn_bias)
    (z2,) = transfer([Gather(normed_mid.astype(bf16))], 7, name="gather_mid")
    z2 = z2.reshape(rows, width)
    pre_act = nn(z2, w_up_all) + b_up
    below = 0.5 * (1.0 + lax.erf(pre_act * 0.5**0.5))
    act = (pre_act * below).astype(bf16)
    slope = (below + pre_act * jnp.exp(-0.5 * pre_act * pre_act) * (2 * math.pi) ** -0.5).astype(bf16)

    grad_w_down_t = tn(down_grad, act).astype(bf16)
    grad_w_down_t, act = lax.optimization_barrier((grad_w_down_t, act))
    shared_down = share(grad_w_down_t)
    ffn_part = nt(act, w_down_t).astype(bf16).reshape(tps, own, width)
    ffn_out, up_grad, mid_part = transfer(
        [Scatter(ffn_part)],
        8,
        Work(
            [down_grad, w_down_t, slope, w_up_all],
            [("nn", 0, 1, 2, 0), ("nt", 4, 3, None, 1)],
            1,
        ),
        name="scatter_ffn",
    )
    output = (inputs + live_own * (attn_out + ffn_out + b_down)).astype(bf16)
    output = output.reshape(bands, piece, width)

    mid_part = mid_part.reshape(tps, own, width)
    mid_grad, grad_w_up, up_sums = transfer(
        [Scatter(mid_part)],
        9,
        Work([z2, up_grad], [("tn", 0, 1, None, 0), ("sum", 1, None, None, 1)], 1),
        name="scatter_mid",
    )
    resid_grad = norm_back(mid_grad, unit_mid, inverse_mid, ffn_gain)
    attn_grad_own = (live_own * grad_own + resid_grad).astype(bf16)
    attn_grad, output = transfer([Gather(attn_grad_own), Swap(output)], 10, name="gather_back")
    attn_grad = attn_grad.reshape(rows, width)
    attn_grad, output = lax.optimization_barrier((attn_grad, output))
    output = gather_later(output)

    mixed_grad = nn(attn_grad, w_out_t).astype(bf16)
    mixed_grad = swap_heads(mixed_grad, group, 13, "cut").reshape(length, features)
    mixed_grad = nn(to_sorted, mixed_grad).astype(bf16)
    grad_w_up, shared_down = lax.optimization_barrier((grad_w_up, shared_down))
    shared_up = share(grad_w_up)
    in_grad, in_sums = attend_back(
        qkv, mixed_sorted, mixed_grad, log_total, info, first, block, half_block
    )
    in_sums = in_sums.transpose(1, 0, 2).reshape(8, features)
    mine = (jnp.arange(group) == member).astype(f32)[:, None]
    in_grad = nn(to_rows, in_grad).astype(bf16).reshape(group, rows, 3 * features)
    in_grad = swap_heads(in_grad, group, 14, "join")
    in_grad, output = lax.optimization_barrier((in_grad, output))
    grad_w_in_out = two_products(z1, in_grad, attn_grad, mixed)
    grad_w_in_out, shared_up = lax.optimization_barrier((grad_w_in_out, shared_up))
    shared_in_out = share(grad_w_in_out)
    in_grad, grad_w_in_out = lax.optimization_barrier((in_grad, grad_w_in_out))
    in_part = nt(in_grad, w_in).astype(bf16).reshape(tps, bands, piece, width)

    def over_rows(array):
        return jnp.sum(array.astype(f32), axis=0)

    wide = [
        over_rows(attn_grad_own),
        over_rows(down_grad_own),
        over_rows(mid_grad * unit_mid),
        over_rows(mid_grad),
    ]
    wide = jnp.concatenate(wide).astype(bf16).reshape(16, width // 4)
    narrow = jnp.concatenate(
        [(mine * in_sums[0]).reshape(-1), (mine * in_sums[1]).reshape(-1), up_sums[0]]
    )
    count = narrow.shape[0]
    narrow = jnp.pad(narrow, (0, -count % 2048)).astype(bf16).reshape(16, -1)
    token_grad, wide, narrow = finish(
        in_part,
        unit_in.reshape(bands, piece, width),
        grad_low,
        resid_grad.reshape(bands, piece, width),
        inverse_in.reshape(bands, piece, 1),
        attn_gain[None],
        wide,
        narrow,
        15,
    )
    token_grad, output, shared_up, shared_down, *small = settle(
        token_grad, output, shared_up, shared_down, wide, narrow, (inner, inner, b_up.shape[0])
    )
    token_grad, output = token_grad.reshape(tokens.shape), output.reshape(tokens.shape)
    small = [vector.reshape(-1) for vector in small]
    shared_q, shared_k, shared_v, shared_out = split_shared(shared_in_out, group, features)
    return (
        output,
        token_grad,
        shared_q,
        shared_k,
        shared_v,
        shared_out,
        shared_up,
        shared_down,
        small[6],
        small[7],
        small[0],
        small[8],
        small[1],
        small[4],
        small[5],
        small[2],
        small[3],
    )


def solution(mesh):
    return jax.shard_map(
        body,
        mesh=mesh,
        in_specs=(
            P(None, "band", None),
            P(None, "band"),
            P(),
            P(),
            P("band", "tp"),
            P("band", "tp"),
            P("band", "tp"),
            P("tp", "band"),
            P("band", "tp"),
            P("tp", "band"),
            P("tp"),
            P("tp"),
            P(),
            P("tp"),
            P(),
            P(),
            P(),
            P(),
            P(),
            P(None, "band", None),
        ),
        out_specs=(
            P(None, "band", None),
            P(None, "band", None),
            P("band", "tp"),
            P("band", "tp"),
            P("band", "tp"),
            P("tp", "band"),
            P("band", "tp"),
            P("tp", "band"),
            P("tp"),
            P("tp"),
            P(),
            P("tp"),
            P(),
            P(),
            P(),
            P(),
            P(),
        ),
        check_vma=False,
    )
```

```python
import functools
import math

import jax
import jax.numpy as jnp
from jax import lax
from jax.experimental import pallas as pl
from jax.experimental.pallas import tpu as pltpu
from jax.sharding import PartitionSpec as P

HEAD_DIM = 64
LAYER = 12
MESH = pl.DeviceIdType.MESH

epsilon = 1e-05
masked_score = -1e30
bf16 = jnp.bfloat16
f32 = jnp.float32


def layer_norm(values, gain, shift):
    center = values - jnp.mean(values, axis=-1, keepdims=True)
    inverse = lax.rsqrt(jnp.mean(center * center, axis=-1, keepdims=True) + epsilon)
    normed = center * inverse
    return (normed * gain + shift, normed, inverse)


def norm_back(grad_out, normed, inverse, gain):
    scaled = grad_out * gain
    return inverse * (
        scaled
        - jnp.mean(scaled, axis=-1, keepdims=True)
        - normed * jnp.mean(scaled * normed, axis=-1, keepdims=True)
    )


def nn(left, right):
    return jnp.dot(left, right, preferred_element_type=f32)


def nt(left, right):
    return lax.dot_general(left, right, (((1,), (1,)), ((), ())), preferred_element_type=f32)


def tn(left, right):
    return lax.dot_general(left, right, (((0,), (0,)), ((), ())), preferred_element_type=f32)


def gelu_exact(values):
    return jax.nn.gelu(values, approximate=False)


def halves(count):
    return (count // 2, 2) if count % 2 == 0 else (count, 1)


def takes(microseconds):
    return pl.CostEstimate(
        flops=int(microseconds * 1e9), bytes_accessed=int(microseconds * 2e6), transcendentals=0
    )


class Sems:
    def __init__(self, send_sem, recv_sem, local_sem):
        self.send_sem, self.recv_sem, self.local_sem = send_sem, recv_sem, local_sem
        self.sent = self.local = 0

    def send(self, source, target, device):
        k = self.sent
        self.sent += 1
        copy = pltpu.make_async_remote_copy(
            source, target, self.send_sem.at[k], self.recv_sem.at[k],
            device_id=device, device_id_type=MESH,
        )
        copy.start()
        return copy

    def copy(self, source, target):
        k = self.local
        self.local += 1
        copy = pltpu.make_async_copy(source, target, self.local_sem.at[k])
        copy.start()
        return copy


class Grid:
    def __init__(self, count):
        self.na, self.nb = na, nb = halves(count)
        self.me, band = lax.axis_index("tp"), lax.axis_index("band")
        self.a, self.b = a, b = self.me // nb, lax.rem(self.me, nb)
        self.along_b = [(band, a * nb + lax.rem(b + d, nb)) for d in range(1, nb)]
        self.along_a = [(band, lax.rem(a + d, na) * nb + b) for d in range(1, na)]
        self.from_b = [a * nb + lax.rem(b + nb - d, nb) for d in range(1, nb)]
        self.from_a = [lax.rem(a + na - d, na) * nb + b for d in range(1, na)]


def tp_peers():
    grid = Grid(lax.axis_size("tp"))
    return grid.along_a + grid.along_b


def band_peers():
    size = lax.axis_size("band")
    me, tp = lax.axis_index("band"), lax.axis_index("tp")
    return [(lax.rem(me + d, size), tp) for d in range(1, size)]


anywhere = pl.BlockSpec(memory_space=pl.ANY)
vmem = pl.BlockSpec(memory_space=pltpu.VMEM)


class Gather:
    peers = "tp"

    def __init__(self, x, inner_slot=False, extra=None):
        self.count = count = lax.axis_size("tp")
        na, nb = halves(count)
        self.inner_slot, self.extra = inner_slot, extra is not None
        self.sends = 2 * (na - 1 + nb - 1) + 2 * (na - 1) * (nb - 1)
        self.locals = 2
        shape = (x.shape[0], count) + x.shape[1:] if inner_slot else (count,) + x.shape
        self.operands, self.in_specs = [x], [anywhere]
        self.shapes, self.out_specs = [jax.ShapeDtypeStruct(shape, x.dtype)], [anywhere]
        self.scratch = [pltpu.VMEM(x.shape, x.dtype)]
        if self.extra:
            self.operands.append(extra)
            self.in_specs.append(vmem)
            self.shapes.append(jax.ShapeDtypeStruct(extra.shape, extra.dtype))
            self.out_specs.append(vmem)
            self.sends += na - 1 + nb - 1
            self.scratch += [
                pltpu.VMEM(extra.shape, extra.dtype),
                pltpu.VMEM((max(nb - 1, 1),) + extra.shape, extra.dtype),
                pltpu.VMEM((max(na - 1, 1),) + extra.shape, extra.dtype),
            ]

    def slot(self, index, which):
        part = self.part[which]
        return self.out.at[part, index] if self.inner_slot else self.out.at[index, part]

    def begin(self, ins, outs, scratch, sems):
        self.grid = grid = Grid(self.count)
        self.sems = sems
        x, self.out = ins[0], outs[0]
        half = x.shape[0] // 2
        self.part = part = (pl.ds(0, half), pl.ds(half, half))
        self.through = scratch[0]
        self.load = sems.copy(x, self.through)
        me = grid.me
        if self.extra:
            self.more = (ins[1], outs[1], *scratch[1:])
            self.extra_b = [
                sems.send(ins[1], scratch[2].at[k], device) for k, device in enumerate(grid.along_b)
            ]
        top, low = x.at[part[0]], x.at[part[1]]
        self.first_b = [sems.send(top, self.slot(me, 0), device) for device in grid.along_b]
        self.first_a = [sems.send(low, self.slot(me, 1), device) for device in grid.along_a]
        self.second = [sems.send(top, self.slot(me, 0), device) for device in grid.along_a]
        self.second += [sems.send(low, self.slot(me, 1), device) for device in grid.along_b]

    def middle(self):
        grid, sems = self.grid, self.sems
        self.load.wait()
        whole = self.out.at[:, grid.me] if self.inner_slot else self.out.at[grid.me]
        self.store = sems.copy(self.through, whole)
        if self.extra:
            own, _, part_ref, in_b, in_a = self.more
            total = own[...]
            for k, copy in enumerate(self.extra_b):
                copy.wait_recv()
                total = total + in_b[k]
            part_ref[...] = total
            self.extra_a = [
                sems.send(part_ref, in_a.at[k], device) for k, device in enumerate(grid.along_a)
            ]
        for copy, source in zip(self.first_b, grid.from_b):
            copy.wait_recv()
            held = self.slot(source, 0)
            self.second += [sems.send(held, held, device) for device in grid.along_a]
        for copy, source in zip(self.first_a, grid.from_a):
            copy.wait_recv()
            held = self.slot(source, 1)
            self.second += [sems.send(held, held, device) for device in grid.along_b]

    def end(self):
        if self.extra:
            _, total_ref, part_ref, _, in_a = self.more
            total = part_ref[...]
            for k, copy in enumerate(self.extra_a):
                copy.wait_recv()
                total = total + in_a[k]
            total_ref[...] = total
            for copy in self.extra_a + self.extra_b:
                copy.wait_send()
        for copy in self.first_a + self.first_b:
            copy.wait_send()
        for copy in self.second:
            copy.wait()
        self.store.wait()


class Scatter:
    peers = "tp"

    def __init__(self, partial):
        self.count, rows, width = partial.shape
        na, nb = halves(self.count)
        block = (rows // 2, width)
        self.sends = 2 * (na - 1) * (nb - 1) + 2 * (na - 1 + nb - 1)
        self.locals = na + nb
        self.operands, self.in_specs = [partial], [anywhere]
        self.shapes, self.out_specs = [jax.ShapeDtypeStruct((rows, width), f32)], [vmem]

        def buffer(*lead):
            return pltpu.VMEM(tuple(max(n, 1) for n in lead) + block, partial.dtype)

        self.scratch = [
            buffer(na), buffer(nb), buffer(nb - 1, na), buffer(na - 1, nb),
            buffer(na - 1), buffer(nb - 1), buffer(na - 1), buffer(nb - 1),
        ]

    def begin(self, ins, outs, scratch, sems):
        self.grid = grid = Grid(self.count)
        self.sems, self.out, self.scratch_refs = sems, outs[0], scratch
        own_a, own_b, one_a, one_b = scratch[:4]
        part = ins[0]
        na, nb, a, b = grid.na, grid.nb, grid.a, grid.b
        half = part.shape[1] // 2
        self.top, self.low = top, low = pl.ds(0, half), pl.ds(half, half)
        self.order_a = order_a = list(range(1, na)) + [0]
        self.order_b = order_b = list(range(1, nb)) + [0]
        self.first_a, self.first_b = {}, {}
        for step in range(max(na, nb)):
            if step < na:
                e = order_a[step]
                row = lax.rem(a + e, na) * nb
                for d in range(1, nb):
                    source = part.at[row + lax.rem(b + d, nb), top]
                    self.first_b[d, e] = sems.send(source, one_a.at[d - 1, e], grid.along_b[d - 1])
            if step < nb:
                e = order_b[step]
                column = lax.rem(b + e, nb)
                for d in range(1, na):
                    source = part.at[lax.rem(a + d, na) * nb + column, low]
                    self.first_a[d, e] = sems.send(source, one_b.at[d - 1, e], grid.along_a[d - 1])
        self.local_a = {
            e: sems.copy(part.at[lax.rem(a + e, na) * nb + b, top], own_a.at[e]) for e in order_a
        }
        self.local_b = {
            e: sems.copy(part.at[a * nb + lax.rem(b + e, nb), low], own_b.at[e]) for e in order_b
        }

    def sum_a(self, e):
        own_a, _, one_a = self.scratch_refs[:3]
        self.local_a[e].wait()
        total = own_a[e].astype(f32)
        for d in range(1, self.grid.nb):
            self.first_b[d, e].wait_recv()
            total = total + one_a[d - 1, e].astype(f32)
        return total

    def sum_b(self, e):
        _, own_b, _, one_b = self.scratch_refs[:4]
        self.local_b[e].wait()
        total = own_b[e].astype(f32)
        for d in range(1, self.grid.na):
            self.first_a[d, e].wait_recv()
            total = total + one_b[d - 1, e].astype(f32)
        return total

    def middle(self):
        grid, sems = self.grid, self.sems
        out_a, out_b, two_a, two_b = self.scratch_refs[4:]
        self.second_a, self.second_b = {}, {}
        for e in self.order_a[:-1]:
            out_a[e - 1] = self.sum_a(e).astype(out_a.dtype)
            self.second_a[e] = sems.send(out_a.at[e - 1], two_a.at[e - 1], grid.along_a[e - 1])
        for e in self.order_b[:-1]:
            out_b[e - 1] = self.sum_b(e).astype(out_b.dtype)
            self.second_b[e] = sems.send(out_b.at[e - 1], two_b.at[e - 1], grid.along_b[e - 1])

    def end(self):
        _, _, two_a, two_b = self.scratch_refs[4:]
        total = self.sum_a(0)
        for e in self.order_a[:-1]:
            self.second_a[e].wait_recv()
            total = total + two_a[e - 1].astype(f32)
        self.out[self.top] = total
        total = self.sum_b(0)
        for e in self.order_b[:-1]:
            self.second_b[e].wait_recv()
            total = total + two_b[e - 1].astype(f32)
        self.out[self.low] = total
        for group in (self.first_a, self.first_b, self.second_a, self.second_b):
            for copy in group.values():
                copy.wait_send()


class Swap:
    peers = "band"

    def __init__(self, x, extra=None):
        size = lax.axis_size("band")
        arrays = [x] if extra is None else [x, extra]
        self.operands, self.in_specs = arrays, [anywhere] * len(arrays)
        self.shapes = [jax.ShapeDtypeStruct(x.shape, x.dtype)]
        self.scratch = [pltpu.VMEM(x.shape[1:], x.dtype)]
        if extra is not None:
            self.shapes.append(jax.ShapeDtypeStruct((size,) + extra.shape, extra.dtype))
            self.scratch.append(pltpu.VMEM(extra.shape, extra.dtype))
        self.out_specs = [anywhere] * len(arrays)
        self.sends = (size - 1) * len(arrays)
        self.locals = 2 * len(arrays)

    def begin(self, ins, outs, scratch, sems):
        me = lax.axis_index("band")
        self.sems, self.scratch_refs = sems, scratch
        self.slots = [out.at[me] for out in outs]
        self.loads = [sems.copy(ins[0].at[me], scratch[0])]
        if len(ins) > 1:
            self.loads.append(sems.copy(ins[1], scratch[1]))
        self.copies = []
        for peer in band_peers():
            if len(ins) > 1:
                self.copies.append(sems.send(ins[1], self.slots[1], peer))
            self.copies.append(sems.send(ins[0].at[peer[0]], self.slots[0], peer))

    def middle(self):
        self.stores = []
        for load, through, slot in zip(self.loads, self.scratch_refs, self.slots):
            load.wait()
            self.stores.append(self.sems.copy(through, slot))

    def end(self):
        for copy in self.copies + self.stores:
            copy.wait()


class Work:
    def __init__(self, operands, tasks, early):
        self.tasks, self.early = tasks, early
        self.operands = operands
        self.shapes = []
        for kind, left, right, _, _ in tasks:
            known = [*operands, *self.shapes]
            if kind == "sum":
                self.shapes.append(jax.ShapeDtypeStruct((1, known[left].shape[1]), f32))
                continue
            rows = known[left].shape[1 if kind == "tn" else 0]
            columns = known[right].shape[0 if kind == "nt" else 1]
            self.shapes.append(jax.ShapeDtypeStruct((rows, columns), bf16))
        self.scratch = [pltpu.VMEM(x.shape, x.dtype) for x in [*operands, *self.shapes]]
        self.locals = len(operands) + len(tasks)

    def begin(self, ins, outs, scratch, sems):
        self.sems, self.outs = sems, outs
        self.held, self.made = scratch[: len(ins)], scratch[len(ins) :]
        self.loads = [sems.copy(source, target) for source, target in zip(ins, self.held)]
        self.stores = []

    def ready(self, k):
        if k < len(self.loads) and self.loads[k] is not None:
            self.loads[k].wait()
            self.loads[k] = None

    def run(self, tasks):
        for kind, left, right, scale, out in tasks:
            for k in (left, right, scale):
                if k is not None:
                    self.ready(k)
            known = [*self.held, *self.made]
            x, made = known[left], self.made[out]
            if kind == "sum":
                rows = min(128, x.shape[0])
                made[...] = jnp.zeros_like(made)

                def add(k, _, x=x, made=made, rows=rows):
                    r = pl.ds(pl.multiple_of(k * rows, rows), rows)
                    made[...] += jnp.sum(x[r, :].astype(f32), axis=0, keepdims=True)
                    return 0

                lax.fori_loop(0, x.shape[0] // rows, add, 0)
                self.stores.append(self.sems.copy(made, self.outs[out]))
                continue
            y = known[right]
            factor = None if scale is None else self.held[scale]
            tile_r, tile_c = min(512, made.shape[0]), min(512, made.shape[1])
            columns = made.shape[1] // tile_c

            def tile(k, _, kind=kind, x=x, y=y, made=made, factor=factor):
                i, j = k // columns, lax.rem(k, columns)
                r = pl.ds(pl.multiple_of(i * tile_r, tile_r), tile_r)
                c = pl.ds(pl.multiple_of(j * tile_c, tile_c), tile_c)
                if kind == "tn":
                    total = tn(x[:, r], y[:, c])
                elif kind == "nt":
                    total = nt(x[r, :], y[c, :])
                else:
                    total = nn(x[r, :], y[:, c])
                if factor is not None:
                    total = total * factor[r, c].astype(f32)
                made[r, c] = total.astype(made.dtype)
                return 0

            lax.fori_loop(0, (made.shape[0] // tile_r) * columns, tile, 0)
            self.stores.append(self.sems.copy(made, self.outs[out]))

    def end(self):
        for store in self.stores:
            store.wait()


def transfer(parts, cid, work=None, name="transfer", time=36):
    items = list(parts) + ([work] if work is not None else [])
    sends = sum(part.sends for part in parts)
    locals_ = sum(item.locals for item in items)

    def kernel(*refs):
        refs = list(refs)

        def take(number):
            taken = refs[:number]
            del refs[:number]
            return taken

        ins = [take(len(item.operands)) for item in items]
        outs = [take(len(item.shapes)) for item in items]
        scratch = [take(len(item.scratch)) for item in items]
        sems = Sems(*refs)
        devices = []
        if any(part.peers == "tp" for part in parts):
            devices += tp_peers()
        if any(part.peers == "band" for part in parts):
            devices += band_peers()
        barrier = pltpu.get_barrier_semaphore()
        for device in devices:
            pl.semaphore_signal(barrier, inc=1, device_id=device, device_id_type=MESH)
        if work is not None:
            work.begin(ins[-1], outs[-1], scratch[-1], sems)
        pl.semaphore_wait(barrier, len(devices))
        for part, i, o, t in zip(parts, ins, outs, scratch):
            part.begin(i, o, t, sems)
        if work is not None:
            work.run(work.tasks[: work.early])
        for part in parts:
            part.middle()
        if work is not None:
            work.run(work.tasks[work.early :])
        for part in parts:
            part.end()
        if work is not None:
            work.end()

    in_specs = [spec for part in parts for spec in part.in_specs]
    out_specs = [spec for part in parts for spec in part.out_specs]
    if work is not None:
        in_specs += [anywhere] * len(work.operands)
        out_specs += [anywhere] * len(work.shapes)
    return pl.pallas_call(
        kernel,
        out_shape=tuple(shape for item in items for shape in item.shapes),
        in_specs=in_specs,
        out_specs=tuple(out_specs),
        scratch_shapes=[
            *(scratch for item in items for scratch in item.scratch),
            pltpu.SemaphoreType.DMA((sends,)),
            pltpu.SemaphoreType.DMA((sends,)),
            pltpu.SemaphoreType.DMA((locals_,)),
        ],
        compiler_params=pltpu.CompilerParams(
            collective_id=cid, has_side_effects=True, vmem_limit_bytes=(58 if work else 32) * 2**20
        ),
        cost_estimate=takes(time),
        name=name,
    )(*(operand for item in items for operand in item.operands))


def gather_later(x, axis=0):
    x = jnp.expand_dims(x, axis)
    copies = jnp.broadcast_to(x, x.shape[:axis] + (lax.axis_size("tp"),) + x.shape[axis + 1 :])
    return lax.all_to_all(copies, "tp", axis, axis)


class Block:
    def __init__(self, order, shift, grid, size):
        band = lax.axis_index("band")
        self.order, self.shift = order, shift
        self.to, self.source = lax.rem(band + shift, size), lax.rem(band + size - shift, size)
        if order % 2 == 0:
            self.n1, self.n2 = grid.nb, grid.na
            self.first, self.second, self.origin = grid.along_b, grid.along_a, grid.from_b
            self.index = lambda d, e: lax.rem(grid.a + e, grid.na) * grid.nb + lax.rem(
                grid.b + d, grid.nb
            )
        else:
            self.n1, self.n2 = grid.na, grid.nb
            self.first, self.second, self.origin = grid.along_a, grid.along_b, grid.from_a
            self.index = lambda d, e: lax.rem(grid.a + d, grid.na) * grid.nb + lax.rem(
                grid.b + e, grid.nb
            )


def finish_kernel(
    count, size, part, unit, above, resid, inverse, gain, wide, narrow,
    out, wide_out, narrow_out,
    own, one, two_out, two, made, arrived, late, late_in, wide_in, narrow_in, pair, pair_b, pair_a,
    send_sem, recv_sem, local_sem,
):
    grid = Grid(count)
    sems = Sems(send_sem, recv_sem, local_sem)
    band = lax.axis_index("band")
    peers = band_peers()
    devices = grid.along_a + grid.along_b + peers
    barrier = pltpu.get_barrier_semaphore()
    for device in devices:
        pl.semaphore_signal(barrier, inc=1, device_id=device, device_id_type=MESH)
    shifts = list(range(1, size)) + [0]
    blocks = [Block(k, shift, grid, size) for k, shift in enumerate(shifts)]
    late[...] = jnp.zeros_like(late)
    pl.semaphore_wait(barrier, len(devices))
    done = []

    for blk in blocks:
        k = blk.order
        seconds = list(range(1, blk.n2)) + [0]
        blk.one = {
            (d, e): sems.send(
                part.at[blk.index(d, e), blk.to], one.at[k, d - 1, e], blk.first[d - 1]
            )
            for e in seconds
            for d in range(1, blk.n1)
        }
        blk.own = {e: sems.copy(part.at[blk.index(0, e), blk.to], own.at[k, e]) for e in seconds}
    early = []
    for peer in peers:
        early.append(sems.send(wide, wide_in.at[band], peer))
        early.append(sems.send(narrow, narrow_in.at[band], peer))

    def first_sum(blk, e):
        k = blk.order
        blk.own[e].wait()
        total = own[k, e].astype(f32)
        for d in range(1, blk.n1):
            blk.one[d, e].wait_recv()
            total = total + one[k, d - 1, e].astype(f32)
        return total

    def pass_on(blk):
        k = blk.order
        blk.two = []
        for e in range(1, blk.n2):
            two_out[k, e - 1] = first_sum(blk, e).astype(bf16)
            blk.two.append(sems.send(two_out.at[k, e - 1], two.at[k, e - 1], blk.second[e - 1]))

    def complete(blk):
        k = blk.order
        grad = first_sum(blk, 0)
        for e, copy in enumerate(blk.two):
            copy.wait_recv()
            grad = grad + two[k, e].astype(f32)
        normed = unit[blk.to]
        scaled = grad * gain[...]
        mean = jnp.mean(scaled, axis=-1, keepdims=True)
        along = jnp.mean(scaled * normed, axis=-1, keepdims=True)
        base = above[blk.to].astype(f32) + resid[blk.to]
        token = base + inverse[blk.to] * (scaled - mean - normed * along)
        made[k] = token.astype(bf16)
        sums = (jnp.sum(grad * normed, axis=0, keepdims=True), jnp.sum(grad, axis=0, keepdims=True))
        quarter = late.shape[1]
        for which, total in enumerate(sums):
            for i in range(4):
                row = slice(4 * which + i, 4 * which + i + 1)
                late[row, :] = late[row, :] + total[:, i * quarter : (i + 1) * quarter]
        if blk.shift:
            blk.swap = sems.send(made.at[k], arrived.at[k], (blk.to, lax.axis_index("tp")))

    def relay(blk):
        k = blk.order
        if blk.shift:
            blk.swap.wait_recv()
            held = arrived.at[k]
        else:
            held = made.at[k]
        slot = out.at[blk.source, grid.me]
        blk.near = [sems.send(held, slot, device) for device in blk.first]
        blk.far = [sems.send(held, slot, device) for device in blk.second]
        done.append(sems.copy(held, slot))

    def forward(blk):
        for copy, source in zip(blk.near, blk.origin):
            copy.wait_recv()
            held = out.at[blk.source, source]
            blk.far += [sems.send(held, held, device) for device in blk.second]

    pairs = [blocks[k : k + 2] for k in range(0, size, 2)]
    stages = (pass_on, complete, relay, forward)
    for step in range(len(pairs) + len(stages) - 1):
        for behind, stage in enumerate(stages):
            if 0 <= step - behind < len(pairs):
                for blk in pairs[step - behind]:
                    stage(blk)
        if step == len(pairs):
            last = [sems.send(late, late_in.at[band], peer) for peer in peers]

    for copy in early + last:
        copy.wait_recv()
    wide_in[band] = wide[...]
    narrow_in[band] = narrow[...]
    late_in[band] = late[...]
    total, narrow_total, late_total = (
        sum(array[k].astype(f32) for k in range(size)) for array in (wide_in, narrow_in, late_in)
    )
    narrow_out[...] = narrow_total
    pair[0:16, :] = total
    pair[16:24, :] = late_total
    near = [sems.send(pair, pair_b.at[k], device) for k, device in enumerate(grid.along_b)]
    total = pair[...]
    for k, copy in enumerate(near):
        copy.wait_recv()
        total = total + pair_b[k]
    for copy in near:
        copy.wait_send()
    pair[...] = total
    far = [sems.send(pair, pair_a.at[k], device) for k, device in enumerate(grid.along_a)]
    for k, copy in enumerate(far):
        copy.wait_recv()
        total = total + pair_a[k]
    wide_out[...] = total

    for copy in early + last + far:
        copy.wait_send()
    for blk in blocks:
        for copy in [*blk.one.values(), *blk.two, *blk.near]:
            copy.wait_send()
        if blk.shift:
            blk.swap.wait_send()
        for copy in blk.far:
            copy.wait()
    for copy in done:
        copy.wait()


def finish(part, unit, above, resid, inverse, gain, wide, narrow, cid):
    count, size, rows, width = part.shape
    na, nb = halves(count)
    most = max(na, nb)
    sends = locals_ = 0
    for k in range(size):
        n1, n2 = (nb, na) if k % 2 == 0 else (na, nb)
        sends += (n1 - 1) * n2 + 2 * (n2 - 1) + (n1 - 1) + (n1 - 1) * (n2 - 1)
        locals_ += n2 + 1
    sends += 4 * (size - 1) + na - 1 + nb - 1
    lanes = wide.shape[1]

    def blocks(*lead):
        return pltpu.VMEM(tuple(max(n, 1) for n in lead) + (rows, width), bf16)

    return pl.pallas_call(
        functools.partial(finish_kernel, count, size),
        out_shape=(
            jax.ShapeDtypeStruct((size, count, rows, width), bf16),
            jax.ShapeDtypeStruct((24, lanes), f32),
            jax.ShapeDtypeStruct(narrow.shape, f32),
        ),
        in_specs=[anywhere] + [vmem] * 7,
        out_specs=(anywhere, vmem, vmem),
        scratch_shapes=[
            blocks(size, most), blocks(size, most - 1, most),
            blocks(size, most - 1), blocks(size, most - 1),
            blocks(size), blocks(size),
            pltpu.VMEM((8, lanes), f32),
            pltpu.VMEM((size, 8, lanes), f32),
            pltpu.VMEM((size,) + wide.shape, bf16),
            pltpu.VMEM((size,) + narrow.shape, bf16),
            pltpu.VMEM((24, lanes), f32),
            pltpu.VMEM((max(nb - 1, 1), 24, lanes), f32),
            pltpu.VMEM((max(na - 1, 1), 24, lanes), f32),
            pltpu.SemaphoreType.DMA((sends,)),
            pltpu.SemaphoreType.DMA((sends,)),
            pltpu.SemaphoreType.DMA((locals_,)),
        ],
        compiler_params=pltpu.CompilerParams(
            collective_id=cid, has_side_effects=True, vmem_limit_bytes=48 * 2**20
        ),
        cost_estimate=takes(90),
        name="finish",
    )(part, unit, above, resid, inverse, gain, wide, narrow)


def heads_kernel(group, kind, x_ref, o_ref, through, local_sem, send_sem, recv_sem):
    band, tp = lax.axis_index("band"), lax.axis_index("tp")
    mine = lax.rem(band, group)
    base = band - mine
    others = [lax.rem(mine + d, group) for d in range(1, group)]
    sems = Sems(send_sem, recv_sem, local_sem)
    width = through.shape[1]

    def columns(index):
        return pl.ds(pl.multiple_of(index * width, width), width)

    def source(index):
        return x_ref.at[:, columns(index)] if kind == "cut" else x_ref.at[index]

    target = o_ref.at[:, columns(mine)] if kind == "join" else o_ref.at[mine]
    barrier = pltpu.get_barrier_semaphore()
    for other in others:
        pl.semaphore_signal(barrier, inc=1, device_id=(base + other, tp), device_id_type=MESH)
    load = sems.copy(source(mine), through)
    pl.semaphore_wait(barrier, group - 1)
    copies = [sems.send(source(other), target, (base + other, tp)) for other in others]
    load.wait()
    for copy in [sems.copy(through, target), *copies]:
        copy.wait()


def swap_heads(x, group, cid, kind):
    if kind == "cut":
        rows, width = x.shape[0], x.shape[1] // group
    else:
        rows, width = x.shape[1:]
    if width % 128 and kind == "cut":
        x = x.reshape(rows, group, width).transpose(1, 0, 2)
        return swap_heads(x, group, cid, "plain")
    if width % 128 and kind == "join":
        x = swap_heads(x, group, cid, "plain")
        return x.transpose(1, 0, 2).reshape(rows, group * width)
    shape = (rows, group * width) if kind == "join" else (group, rows, width)
    return pl.pallas_call(
        functools.partial(heads_kernel, group, kind),
        out_shape=jax.ShapeDtypeStruct(shape, x.dtype),
        in_specs=[anywhere],
        out_specs=anywhere,
        scratch_shapes=[
            pltpu.VMEM((rows, width), x.dtype),
            pltpu.SemaphoreType.DMA((2,)),
            pltpu.SemaphoreType.DMA((group - 1,)),
            pltpu.SemaphoreType.DMA((group - 1,)),
        ],
        compiler_params=pltpu.CompilerParams(collective_id=cid, has_side_effects=True),
        cost_estimate=takes(4),
        name="swap_heads",
    )(x)


def settle_kernel(
    wides, grad_ref, out_ref, up_ref, down_ref, wide_ref, narrow_ref,
    grad_to, out_to, up_to, down_to, *small,
):
    grad_to[...] = grad_ref[...].astype(f32)
    out_to[0] = out_ref[:, 0]
    up_to[...] = up_ref[...].astype(f32)
    down_to[...] = down_ref[...].astype(f32).T

    @pl.when(pl.program_id(0) == 0)
    def _():
        for refs, source in ((small[:wides], wide_ref), (small[wides:], narrow_ref)):
            lanes, row = source.shape[1], 0
            for ref in refs:
                for i in range(ref.shape[1] // lanes):
                    ref[0:1, i * lanes : (i + 1) * lanes] = source[row : row + 1, :]
                    row += 1


def settle(grad, out, up, down, wide, narrow, widths):
    size, count, rows, width = grad.shape
    wides = wide.shape[0] * wide.shape[1] // width
    slab = down.shape[1] // size
    small = [width] * wides + list(widths)
    block = pl.BlockSpec((1, count, rows, width), lambda i: (i, 0, 0, 0))
    across = pl.BlockSpec((up.shape[0] // size, up.shape[1]), lambda i: (i, 0))
    if up.shape[0] // size % 16:
        across = pl.BlockSpec(up.shape, lambda i: (0, 0))
    return pl.pallas_call(
        functools.partial(settle_kernel, wides),
        out_shape=(
            jax.ShapeDtypeStruct(grad.shape, f32),
            jax.ShapeDtypeStruct(grad.shape, out.dtype),
            jax.ShapeDtypeStruct(up.shape, f32),
            jax.ShapeDtypeStruct(down.shape[::-1], f32),
            *(jax.ShapeDtypeStruct((1, n), f32) for n in small),
        ),
        grid=(size,),
        in_specs=[
            block,
            pl.BlockSpec((count, 1, rows, width), lambda i: (0, i, 0, 0)),
            across,
            pl.BlockSpec((down.shape[0], slab), lambda i: (0, i)) if slab % 128 == 0 else vmem,
            pl.BlockSpec(wide.shape, lambda i: (0, 0)),
            pl.BlockSpec(narrow.shape, lambda i: (0, 0)),
        ],
        out_specs=(
            block,
            block,
            across,
            pl.BlockSpec((slab, down.shape[0]), lambda i: (i, 0)) if slab % 128 == 0 else vmem,
            *(pl.BlockSpec((1, n), lambda i: (0, 0)) for n in small),
        ),
        compiler_params=pltpu.CompilerParams(vmem_limit_bytes=40 * 2**20),
        cost_estimate=takes(10),
        name="settle",
    )(grad, out, up, down, wide, narrow)


def split_kernel(group, features, x_ref, q_ref, k_ref, v_ref, out_ref):
    for g in range(group):
        for which, ref in enumerate((q_ref, k_ref, v_ref)):
            start = (3 * g + which) * features
            ref[:, g * features : (g + 1) * features] = x_ref[:, start : start + features].astype(f32)
    out_ref[...] = x_ref[:, 3 * group * features :].astype(f32).T


def split_shared(x, group, features):
    rows, inner = x.shape[0], group * features
    return pl.pallas_call(
        functools.partial(split_kernel, group, features),
        out_shape=(
            *[jax.ShapeDtypeStruct((rows, inner), f32)] * 3,
            jax.ShapeDtypeStruct((x.shape[1] - 3 * inner, rows), f32),
        ),
        in_specs=[vmem],
        out_specs=(vmem,) * 4,
        compiler_params=pltpu.CompilerParams(vmem_limit_bytes=32 * 2**20),
        cost_estimate=takes(2),
        name="split_shared",
    )(x)


def project_kernel(x_ref, w_ref, bias_ref, scale_ref, o_ref):
    total = nn(x_ref[...], w_ref[...]) + bias_ref[...]
    o_ref[0] = total.astype(bf16) * scale_ref[...].astype(bf16)


def project(x, weight, bias, scale, group):
    rows, depth = x.shape
    total_width = bias.shape[0]
    width = total_width // group
    if width % 128:
        total = (nn(x, weight[:, :total_width]) + bias).astype(bf16) * scale.astype(bf16)
        return total.reshape(rows, group, width).transpose(1, 0, 2)
    block = min(256, rows)
    return pl.pallas_call(
        project_kernel,
        out_shape=jax.ShapeDtypeStruct((group, rows, width), bf16),
        grid=(group, rows // block),
        in_specs=[
            pl.BlockSpec((block, depth), lambda g, i: (i, 0)),
            pl.BlockSpec((depth, width), lambda g, i: (0, g)),
            pl.BlockSpec((1, width), lambda g, i: (0, g)),
            pl.BlockSpec((1, width), lambda g, i: (0, g)),
        ],
        out_specs=pl.BlockSpec((1, block, width), lambda g, i: (g, i, 0)),
        compiler_params=pltpu.CompilerParams(vmem_limit_bytes=40 * 2**20),
        cost_estimate=pl.CostEstimate(
            flops=2 * rows * depth * width * group, bytes_accessed=12 * 2**20, transcendentals=0
        ),
        name="project",
    )(x, weight, bias[None], scale[None])


def products_kernel(left_ref, right_ref, other_ref, last_ref, o_ref):
    tile, width = last_ref.shape[1], right_ref.shape[1]

    def step(k, _):
        columns = pl.ds(pl.multiple_of(k * tile, tile), tile)
        o_ref[:, columns] = tn(left_ref[...], right_ref[:, columns]).astype(o_ref.dtype)
        return 0

    lax.fori_loop(0, width // tile, step, 0)
    o_ref[:, width:] = tn(other_ref[...], last_ref[...]).astype(o_ref.dtype)


def product_kernel(left_ref, right_ref, o_ref):
    tile = min(512, o_ref.shape[1])

    def step(k, _):
        columns = pl.ds(pl.multiple_of(k * tile, tile), tile)
        o_ref[:, columns] = tn(left_ref[...], right_ref[:, columns]).astype(o_ref.dtype)
        return 0

    lax.fori_loop(0, o_ref.shape[1] // tile, step, 0)


def product(left, right):
    rows, depth = left.shape
    width = right.shape[1]
    tile = min(512, depth)
    return pl.pallas_call(
        product_kernel,
        out_shape=jax.ShapeDtypeStruct((depth, width), bf16),
        grid=(depth // tile,),
        in_specs=[
            pl.BlockSpec((rows, tile), lambda i: (0, i)),
            pl.BlockSpec((rows, width), lambda i: (0, 0)),
        ],
        out_specs=pl.BlockSpec((tile, width), lambda i: (i, 0)),
        compiler_params=pltpu.CompilerParams(vmem_limit_bytes=40 * 2**20),
        cost_estimate=takes(12),
        name="product",
    )(left, right)


def two_products(left, right, other, last):
    rows, depth = left.shape
    width, more = right.shape[1], last.shape[1]
    tile = min(512, depth)
    cut = pl.BlockSpec((rows, tile), lambda i: (0, i))
    return pl.pallas_call(
        products_kernel,
        out_shape=jax.ShapeDtypeStruct((depth, width + more), bf16),
        grid=(depth // tile,),
        in_specs=[
            cut,
            pl.BlockSpec((rows, width), lambda i: (0, 0)),
            cut,
            pl.BlockSpec((rows, more), lambda i: (0, 0)),
        ],
        out_specs=pl.BlockSpec((tile, width + more), lambda i: (i, 0)),
        compiler_params=pltpu.CompilerParams(vmem_limit_bytes=48 * 2**20),
        cost_estimate=takes(12),
        name="two_products",
    )(left, right, other, last)


def permitted(first, limit, row, column):
    return ((column >= first) & (column <= limit)) | (column == row)


def head_mask(head, shape):
    lane = lax.broadcasted_iota(jnp.int32, shape, 1)
    return (lane >= head * HEAD_DIM) & (lane < (head + 1) * HEAD_DIM)


def attend_kernel(qb, kb, info_ref, first_ref, q_ref, k_ref, v_ref, o_ref, log_ref, vt_ref):
    length, width = q_ref.shape
    heads = width // HEAD_DIM
    live_end = info_ref[0]
    count = lax.div(live_end + qb - 1, qb)
    vt_ref[...] = v_ref[...].T
    o_ref[...] = jnp.zeros_like(o_ref)
    log_ref[...] = jnp.zeros_like(log_ref)

    def queries(i, _):
        rows = pl.ds(pl.multiple_of(i * qb, qb), qb)
        q = q_ref[rows, :]
        first = first_ref[0:1, rows]
        row = i * qb + lax.broadcasted_iota(jnp.int32, (1, qb), 1)
        limit = jnp.minimum(row, live_end - 1)
        q_heads = [
            jnp.where(head_mask(h, (qb, width)), q, jnp.zeros_like(q)) for h in range(heads)
        ]
        def keys(j, carry):
            columns = pl.ds(pl.multiple_of(j * kb, kb), kb)
            k = k_ref[columns, :]
            column = j * kb + lax.broadcasted_iota(jnp.int32, (kb, 1), 0)
            allowed = permitted(first, limit, row, column)
            out = []
            for h in range(heads):
                top, total, summed = carry[h]
                scores = jnp.where(allowed, nt(k, q_heads[h]), masked_score)
                new_top = jnp.maximum(top, jnp.max(scores, axis=0, keepdims=True))
                weights = jnp.exp(scores - new_top)
                scale = jnp.exp(top - new_top)
                total = total * scale + jnp.sum(weights, axis=0, keepdims=True)
                vt = vt_ref[h * HEAD_DIM : (h + 1) * HEAD_DIM, columns]
                summed = summed * scale + nn(vt, weights.astype(bf16))
                out.append((new_top, total, summed))
            return tuple(out)
        start = tuple(
            (
                jnp.full((1, qb), masked_score, f32),
                jnp.zeros((1, qb), f32),
                jnp.zeros((HEAD_DIM, qb), f32),
            )
            for _ in range(heads)
        )
        lo = lax.div(info_ref[1 + i], kb)
        hi = lax.div(i * qb + qb - 1, kb) + 1
        done = lax.fori_loop(lo, hi, keys, start)
        mixed = jnp.concatenate([summed / total for _, total, summed in done], axis=0)
        o_ref[rows, :] = mixed.T.astype(o_ref.dtype)
        for h, (top, total, _) in enumerate(done):
            log_ref[0, h : h + 1, rows] = top + jnp.log(total)
        return 0
    lax.fori_loop(0, count, queries, 0)


def attend_back_kernel(
    qb, kb, info_ref, first_ref, q_ref, k_ref, v_ref, o_ref, do_ref, log_ref, out_ref, sum_ref,
    dk_acc, dv_acc,
):
    length, width = q_ref.shape
    heads = width // HEAD_DIM
    features = out_ref.shape[1] // 3
    slab = pl.program_id(0)
    factor = HEAD_DIM ** (-0.5)
    live_end = info_ref[0]
    count = lax.div(live_end + qb - 1, qb)

    def lanes(which):
        if features == width:
            return pl.ds(which * features, width)
        return pl.ds(pl.multiple_of(which * features + slab * width, width), width)
    dk_acc[...] = jnp.zeros_like(dk_acc)
    dv_acc[...] = jnp.zeros_like(dv_acc)
    out_ref[:, lanes(0)] = jnp.zeros((length, width), out_ref.dtype)

    def queries(i, _):
        rows = pl.ds(pl.multiple_of(i * qb, qb), qb)
        q, do = q_ref[rows, :], do_ref[rows, :]
        first = first_ref[0:1, rows]
        row = i * qb + lax.broadcasted_iota(jnp.int32, (1, qb), 1)
        limit = jnp.minimum(row, live_end - 1)
        dots = (do.astype(f32) * o_ref[rows, :].astype(f32)).T
        masks = [head_mask(h, (qb, width)) for h in range(heads)]
        kmasks = [head_mask(h, (kb, width)) for h in range(heads)]
        zero = jnp.zeros_like(q)
        q_heads = [jnp.where(mask, q, zero) for mask in masks]
        do_heads = [jnp.where(mask, do, zero) for mask in masks]
        logs = [log_ref[0, h : h + 1, rows] for h in range(heads)]
        deltas = [
            jnp.sum(dots[h * HEAD_DIM : (h + 1) * HEAD_DIM], axis=0, keepdims=True)
            for h in range(heads)
        ]
        def keys(j, dq):
            columns = pl.ds(pl.multiple_of(j * kb, kb), kb)
            k, v = k_ref[columns, :], v_ref[columns, :]
            column = j * kb + lax.broadcasted_iota(jnp.int32, (kb, 1), 0)
            allowed = permitted(first, limit, row, column)
            dk, dv = dk_acc[columns, :], dv_acc[columns, :]
            for h in range(heads):
                scores = jnp.where(allowed, nt(k, q_heads[h]) - logs[h], masked_score)
                probs = jnp.exp(scores)
                prob_grad = nt(v, do_heads[h])
                score_grad = (probs * (prob_grad - deltas[h])).astype(bf16)
                dv = dv + nn(probs.astype(bf16), do_heads[h])
                dk = dk + nn(score_grad, q_heads[h])
                dq = dq + tn(score_grad, jnp.where(kmasks[h], k, jnp.zeros_like(k)))
            dk_acc[columns, :] = dk
            dv_acc[columns, :] = dv
            return dq
        lo = lax.div(info_ref[1 + i], kb)
        hi = lax.div(i * qb + qb - 1, kb) + 1
        dq = lax.fori_loop(lo, hi, keys, jnp.zeros((qb, width), f32))
        out_ref[rows, lanes(0)] = (dq * factor).astype(out_ref.dtype)
        return 0
    lax.fori_loop(0, count, queries, 0)
    sum_ref[...] = jnp.zeros_like(sum_ref)

    def store(i, _):
        rows = pl.ds(pl.multiple_of(i * kb, kb), kb)
        dv = dv_acc[rows, :].astype(out_ref.dtype)
        out_ref[rows, lanes(1)] = dk_acc[rows, :].astype(out_ref.dtype)
        out_ref[rows, lanes(2)] = dv
        dq = out_ref[rows, lanes(0)].astype(f32)
        sum_ref[0, 0:1, :] += jnp.sum(dq, axis=0, keepdims=True)
        sum_ref[0, 1:2, :] += jnp.sum(dv.astype(f32), axis=0, keepdims=True)
        return 0
    lax.fori_loop(0, length // kb, store, 0)


def attention_specs(length, features):
    width = min(256, features)
    slabs = features // width

    plain = pl.BlockSpec((length, width), lambda i, info: (0, i))

    def piece(which):
        if features % 128:
            return plain
        return pl.BlockSpec((length, width), lambda i, info, w=which: (0, w * slabs + i))

    logs = pl.BlockSpec((1, 8, length), lambda i, info: (i, 0, 0))
    first = pl.BlockSpec((1, length), lambda i, info: (0, 0))
    return width, slabs, piece, plain, logs, first


def three(qkv, features):
    if features % 128:
        return [qkv[:, w * features : (w + 1) * features] for w in range(3)]
    return [qkv] * 3


def attend(qkv, info, first, qb, kb):
    length, features = qkv.shape[0], qkv.shape[1] // 3
    width, slabs, piece, plain, logs, first_spec = attention_specs(length, features)
    return pl.pallas_call(
        functools.partial(attend_kernel, qb, kb),
        out_shape=(
            jax.ShapeDtypeStruct((length, features), bf16),
            jax.ShapeDtypeStruct((slabs, 8, length), f32),
        ),
        grid_spec=pltpu.PrefetchScalarGridSpec(
            num_scalar_prefetch=1,
            grid=(slabs,),
            in_specs=[first_spec, piece(0), piece(1), piece(2)],
            out_specs=(plain, logs),
            scratch_shapes=[pltpu.VMEM((width, length), bf16)],
        ),
        compiler_params=pltpu.CompilerParams(vmem_limit_bytes=48 * 2**20),
        cost_estimate=takes(30),
        name="attend",
    )(info, first, *three(qkv, features))


def attend_back(qkv, mixed, grad, log_total, info, first, qb, kb):
    length, features = qkv.shape[0], qkv.shape[1] // 3
    width, slabs, piece, plain, logs, first_spec = attention_specs(length, features)
    return pl.pallas_call(
        functools.partial(attend_back_kernel, qb, kb),
        out_shape=(
            jax.ShapeDtypeStruct((length, 3 * features), bf16),
            jax.ShapeDtypeStruct((slabs, 8, width), f32),
        ),
        grid_spec=pltpu.PrefetchScalarGridSpec(
            num_scalar_prefetch=1,
            grid=(slabs,),
            in_specs=[first_spec, piece(0), piece(1), piece(2), plain, plain, logs],
            out_specs=(
                pl.BlockSpec((length, 3 * features), lambda i, info: (0, 0)),
                pl.BlockSpec((1, 8, width), lambda i, info: (i, 0, 0)),
            ),
            scratch_shapes=[pltpu.VMEM((length, width), f32), pltpu.VMEM((length, width), f32)],
        ),
        compiler_params=pltpu.CompilerParams(vmem_limit_bytes=48 * 2**20),
        cost_estimate=takes(34),
        name="attend_back",
    )(info, first, *three(qkv, features), mixed, grad, log_total)


def body(
    tokens,
    positions,
    doc_lengths,
    exit_depth,
    w_query,
    w_key,
    w_value,
    w_out,
    w_up,
    w_down,
    b_query,
    b_value,
    b_out,
    b_up,
    b_down,
    attn_gain,
    attn_bias,
    ffn_gain,
    ffn_bias,
    cotangent,
):
    seqs, local_rows, width = tokens.shape
    inner = b_query.shape[0]
    bands, tps = lax.axis_size("band"), lax.axis_size("tp")
    group = bands // seqs
    piece = local_rows // (group * tps)
    band, tp = lax.axis_index("band"), lax.axis_index("tp")
    seq, member = band // group, lax.rem(band, group)
    features = inner // group
    length = exit_depth.shape[1]
    own = bands * piece
    rows = tps * own
    block, half_block = min(512, length), min(256, length)

    def by_group(*parts):
        split = [p.reshape(p.shape[:-1] + (group, features)) for p in parts]
        return jnp.stack(split, axis=-2).reshape(parts[0].shape[:-1] + (-1,))

    def share(grad):
        return lax.psum_scatter(grad, "band", scatter_dimension=0, tiled=True)

    w_in_out = jnp.concatenate([by_group(w_query, w_key, w_value), w_out.T], axis=1)
    w_in_out = lax.all_gather(w_in_out, "band", axis=0, tiled=True)
    w_in, w_out_t = w_in_out[:, : 3 * inner], w_in_out[:, 3 * inner :]
    w_up_all = lax.all_gather(w_up, "band", axis=0, tiled=True)
    w_down_t = lax.all_gather(w_down.T, "band", axis=0, tiled=True)

    def my_share(array):
        split = array.reshape(seqs, group, tps, piece, width)
        return lax.dynamic_index_in_dim(split, tp, 2, keepdims=False).reshape(bands, piece, width)

    token_own, all_pos = transfer([Swap(my_share(tokens), positions)], 0, name="swap_in")
    seq_pos = lax.dynamic_index_in_dim(all_pos, seq, 1, keepdims=False)
    seq_pos = seq_pos.reshape(bands, group, tps, piece).transpose(1, 2, 0, 3)
    row_pos = seq_pos.reshape(length)
    member_pos = lax.dynamic_index_in_dim(seq_pos, member, 0, keepdims=False)
    own_pos = lax.dynamic_index_in_dim(member_pos, tp, 0, keepdims=False).reshape(own)
    depths = lax.dynamic_index_in_dim(exit_depth, seq, 0, keepdims=False)
    live_end = jnp.sum((depths > LAYER).astype(jnp.int32))
    live_own = (own_pos < live_end).astype(f32)[:, None]
    ends = jnp.cumsum(lax.dynamic_index_in_dim(doc_lengths, seq, 0, keepdims=False))
    places = jnp.arange(length, dtype=jnp.int32)
    first = jnp.max(jnp.where(ends[:, None] <= places[None, :], ends[:, None], 0), axis=0)
    info = jnp.concatenate([live_end[None], first[::block]]).astype(jnp.int32)
    first = first[None, :].astype(jnp.int32)
    to_sorted = (row_pos[None, :] == places[:, None]).astype(bf16)
    to_rows = (row_pos[:, None] == places[None, :]).astype(bf16)

    inputs = token_own.reshape(own, width).astype(f32)
    normed_in, unit_in, inverse_in = layer_norm(inputs, attn_gain, attn_bias)
    z1, grad_low = transfer([Gather(normed_in.astype(bf16)), Swap(my_share(cotangent))], 1, name="gather_in")
    z1 = z1.reshape(rows, width)
    grad_own = grad_low.reshape(own, width).astype(f32)
    down_grad_own = (live_own * grad_own).astype(bf16)
    down_grad = gather_later(down_grad_own)

    bias_in = by_group(b_query, jnp.zeros_like(b_query), b_value)
    scale_in = by_group(
        jnp.full_like(b_query, HEAD_DIM ** (-0.5)), jnp.ones_like(b_query), jnp.ones_like(b_query)
    )
    qkv = project(z1, w_in_out, bias_in, scale_in, group)
    qkv = swap_heads(qkv, group, 4, "plain").reshape(length, 3 * features)
    qkv = nn(to_sorted, qkv).astype(bf16)
    mixed_sorted, log_total = attend(qkv, info, first, block, block)
    mixed_sorted, down_grad = lax.optimization_barrier((mixed_sorted, down_grad))
    down_grad = down_grad.reshape(rows, width)
    mixed = nn(to_rows, mixed_sorted).astype(bf16).reshape(group, rows, features)
    mixed = swap_heads(mixed, group, 5, "join")

    attn_part = nt(mixed, w_out_t).astype(bf16).reshape(tps, own, width)
    (attn_out,) = transfer([Scatter(attn_part)], 6, name="scatter_attn")
    attn_out = attn_out + b_out
    residual = inputs + attn_out
    normed_mid, unit_mid, inverse_mid = layer_norm(residual, ffn_gain, ffn_bias)
    (z2,) = transfer([Gather(normed_mid.astype(bf16))], 7, name="gather_mid")
    z2 = z2.reshape(rows, width)
    pre_act = nn(z2, w_up_all) + b_up
    below = 0.5 * (1.0 + lax.erf(pre_act * 0.5**0.5))
    act = (pre_act * below).astype(bf16)
    slope = (below + pre_act * jnp.exp(-0.5 * pre_act * pre_act) * (2 * math.pi) ** -0.5).astype(bf16)

    grad_w_down_t = product(down_grad, act)
    grad_w_down_t, act = lax.optimization_barrier((grad_w_down_t, act))
    shared_down = share(grad_w_down_t)
    ffn_part = nt(act, w_down_t).astype(bf16).reshape(tps, own, width)
    ffn_out, up_grad, mid_part = transfer(
        [Scatter(ffn_part)],
        8,
        Work(
            [down_grad, w_down_t, slope, w_up_all],
            [("nn", 0, 1, 2, 0), ("nt", 4, 3, None, 1)],
            1,
        ),
        name="scatter_ffn",
    )
    output = (inputs + live_own * (attn_out + ffn_out + b_down)).astype(bf16)
    output = output.reshape(bands, piece, width)

    mid_part = mid_part.reshape(tps, own, width)
    mid_grad, grad_w_up, up_sums = transfer(
        [Scatter(mid_part)],
        9,
        Work([z2, up_grad], [("tn", 0, 1, None, 0), ("sum", 1, None, None, 1)], 1),
        name="scatter_mid",
    )
    resid_grad = norm_back(mid_grad, unit_mid, inverse_mid, ffn_gain)
    attn_grad_own = (live_own * grad_own + resid_grad).astype(bf16)
    attn_grad, output = transfer([Gather(attn_grad_own), Swap(output)], 10, name="gather_back")
    attn_grad = attn_grad.reshape(rows, width)
    attn_grad, output = lax.optimization_barrier((attn_grad, output))
    output = gather_later(output)

    mixed_grad = nn(attn_grad, w_out_t).astype(bf16)
    mixed_grad = swap_heads(mixed_grad, group, 13, "cut").reshape(length, features)
    mixed_grad = nn(to_sorted, mixed_grad).astype(bf16)
    grad_w_up, shared_down = lax.optimization_barrier((grad_w_up, shared_down))
    shared_up = share(grad_w_up)
    in_grad, in_sums = attend_back(
        qkv, mixed_sorted, mixed_grad, log_total, info, first, block, half_block
    )
    in_sums = in_sums.transpose(1, 0, 2).reshape(8, features)
    mine = (jnp.arange(group) == member).astype(f32)[:, None]
    in_grad = nn(to_rows, in_grad).astype(bf16).reshape(group, rows, 3 * features)
    in_grad = swap_heads(in_grad, group, 14, "join")
    in_grad, output = lax.optimization_barrier((in_grad, output))
    grad_w_in_out = two_products(z1, in_grad, attn_grad, mixed)
    grad_w_in_out, shared_up = lax.optimization_barrier((grad_w_in_out, shared_up))
    shared_in_out = share(grad_w_in_out)
    in_grad, grad_w_in_out = lax.optimization_barrier((in_grad, grad_w_in_out))
    in_part = nt(in_grad, w_in).astype(bf16).reshape(tps, bands, piece, width)

    def over_rows(array):
        return jnp.sum(array.astype(f32), axis=0)

    wide = [
        over_rows(attn_grad_own),
        over_rows(down_grad_own),
        over_rows(mid_grad * unit_mid),
        over_rows(mid_grad),
    ]
    wide = jnp.concatenate(wide).astype(bf16).reshape(16, width // 4)
    narrow = jnp.concatenate(
        [(mine * in_sums[0]).reshape(-1), (mine * in_sums[1]).reshape(-1), up_sums[0]]
    )
    count = narrow.shape[0]
    narrow = jnp.pad(narrow, (0, -count % 2048)).astype(bf16).reshape(16, -1)
    token_grad, wide, narrow = finish(
        in_part,
        unit_in.reshape(bands, piece, width),
        grad_low,
        resid_grad.reshape(bands, piece, width),
        inverse_in.reshape(bands, piece, 1),
        attn_gain[None],
        wide,
        narrow,
        15,
    )
    token_grad, output, shared_up, shared_down, *small = settle(
        token_grad, output, shared_up, shared_down, wide, narrow, (inner, inner, b_up.shape[0])
    )
    token_grad, output = token_grad.reshape(tokens.shape), output.reshape(tokens.shape)
    small = [vector.reshape(-1) for vector in small]
    shared_q, shared_k, shared_v, shared_out = split_shared(shared_in_out, group, features)
    return (
        output,
        token_grad,
        shared_q,
        shared_k,
        shared_v,
        shared_out,
        shared_up,
        shared_down,
        small[6],
        small[7],
        small[0],
        small[8],
        small[1],
        small[4],
        small[5],
        small[2],
        small[3],
    )


def solution(mesh):
    return jax.shard_map(
        body,
        mesh=mesh,
        in_specs=(
            P(None, "band", None),
            P(None, "band"),
            P(),
            P(),
            P("band", "tp"),
            P("band", "tp"),
            P("band", "tp"),
            P("tp", "band"),
            P("band", "tp"),
            P("tp", "band"),
            P("tp"),
            P("tp"),
            P(),
            P("tp"),
            P(),
            P(),
            P(),
            P(),
            P(),
            P(None, "band", None),
        ),
        out_specs=(
            P(None, "band", None),
            P(None, "band", None),
            P("band", "tp"),
            P("band", "tp"),
            P("band", "tp"),
            P("tp", "band"),
            P("band", "tp"),
            P("tp", "band"),
            P("tp"),
            P("tp"),
            P(),
            P("tp"),
            P(),
            P(),
            P(),
            P(),
            P(),
        ),
        check_vma=False,
    )
```

```python
import functools
import math

import jax
import jax.numpy as jnp
from jax import lax
from jax.experimental import pallas as pl
from jax.experimental.pallas import tpu as pltpu
from jax.sharding import PartitionSpec as P

HEAD_DIM = 64
LAYER = 12
MESH = pl.DeviceIdType.MESH

epsilon = 1e-05
masked_score = -1e30
bf16 = jnp.bfloat16
f32 = jnp.float32


def layer_norm(values, gain, shift):
    center = values - jnp.mean(values, axis=-1, keepdims=True)
    inverse = lax.rsqrt(jnp.mean(center * center, axis=-1, keepdims=True) + epsilon)
    normed = center * inverse
    return (normed * gain + shift, normed, inverse)


def norm_back(grad_out, normed, inverse, gain):
    scaled = grad_out * gain
    return inverse * (
        scaled
        - jnp.mean(scaled, axis=-1, keepdims=True)
        - normed * jnp.mean(scaled * normed, axis=-1, keepdims=True)
    )


def nn(left, right):
    return jnp.dot(left, right, preferred_element_type=f32)


def nt(left, right):
    return lax.dot_general(left, right, (((1,), (1,)), ((), ())), preferred_element_type=f32)


def tn(left, right):
    return lax.dot_general(left, right, (((0,), (0,)), ((), ())), preferred_element_type=f32)


def gelu_exact(values):
    return jax.nn.gelu(values, approximate=False)


def halves(count):
    return (count // 2, 2) if count % 2 == 0 else (count, 1)


def takes(microseconds):
    return pl.CostEstimate(
        flops=int(microseconds * 1e9), bytes_accessed=int(microseconds * 2e6), transcendentals=0
    )


class Sems:
    def __init__(self, send_sem, recv_sem, local_sem):
        self.send_sem, self.recv_sem, self.local_sem = send_sem, recv_sem, local_sem
        self.sent = self.local = 0

    def send(self, source, target, device):
        k = self.sent
        self.sent += 1
        copy = pltpu.make_async_remote_copy(
            source, target, self.send_sem.at[k], self.recv_sem.at[k],
            device_id=device, device_id_type=MESH,
        )
        copy.start()
        return copy

    def copy(self, source, target):
        k = self.local
        self.local += 1
        copy = pltpu.make_async_copy(source, target, self.local_sem.at[k])
        copy.start()
        return copy


class Grid:
    def __init__(self, count):
        self.na, self.nb = na, nb = halves(count)
        self.me, band = lax.axis_index("tp"), lax.axis_index("band")
        self.a, self.b = a, b = self.me // nb, lax.rem(self.me, nb)
        self.along_b = [(band, a * nb + lax.rem(b + d, nb)) for d in range(1, nb)]
        self.along_a = [(band, lax.rem(a + d, na) * nb + b) for d in range(1, na)]
        self.from_b = [a * nb + lax.rem(b + nb - d, nb) for d in range(1, nb)]
        self.from_a = [lax.rem(a + na - d, na) * nb + b for d in range(1, na)]


def tp_peers():
    grid = Grid(lax.axis_size("tp"))
    return grid.along_a + grid.along_b


def band_peers():
    size = lax.axis_size("band")
    me, tp = lax.axis_index("band"), lax.axis_index("tp")
    return [(lax.rem(me + d, size), tp) for d in range(1, size)]


anywhere = pl.BlockSpec(memory_space=pl.ANY)
vmem = pl.BlockSpec(memory_space=pltpu.VMEM)


class Gather:
    peers = "tp"

    def __init__(self, x, inner_slot=False, extra=None):
        self.count = count = lax.axis_size("tp")
        na, nb = halves(count)
        self.inner_slot, self.extra = inner_slot, extra is not None
        self.sends = 2 * (na - 1 + nb - 1) + 2 * (na - 1) * (nb - 1)
        self.locals = 2
        shape = (x.shape[0], count) + x.shape[1:] if inner_slot else (count,) + x.shape
        self.operands, self.in_specs = [x], [anywhere]
        self.shapes, self.out_specs = [jax.ShapeDtypeStruct(shape, x.dtype)], [anywhere]
        self.scratch = [pltpu.VMEM(x.shape, x.dtype)]
        if self.extra:
            self.operands.append(extra)
            self.in_specs.append(vmem)
            self.shapes.append(jax.ShapeDtypeStruct(extra.shape, extra.dtype))
            self.out_specs.append(vmem)
            self.sends += na - 1 + nb - 1
            self.scratch += [
                pltpu.VMEM(extra.shape, extra.dtype),
                pltpu.VMEM((max(nb - 1, 1),) + extra.shape, extra.dtype),
                pltpu.VMEM((max(na - 1, 1),) + extra.shape, extra.dtype),
            ]

    def slot(self, index, which):
        part = self.part[which]
        return self.out.at[part, index] if self.inner_slot else self.out.at[index, part]

    def begin(self, ins, outs, scratch, sems):
        self.grid = grid = Grid(self.count)
        self.sems = sems
        x, self.out = ins[0], outs[0]
        half = x.shape[0] // 2
        self.part = part = (pl.ds(0, half), pl.ds(half, half))
        self.through = scratch[0]
        self.load = sems.copy(x, self.through)
        me = grid.me
        if self.extra:
            self.more = (ins[1], outs[1], *scratch[1:])
            self.extra_b = [
                sems.send(ins[1], scratch[2].at[k], device) for k, device in enumerate(grid.along_b)
            ]
        top, low = x.at[part[0]], x.at[part[1]]
        self.first_b = [sems.send(top, self.slot(me, 0), device) for device in grid.along_b]
        self.first_a = [sems.send(low, self.slot(me, 1), device) for device in grid.along_a]
        self.second = [sems.send(top, self.slot(me, 0), device) for device in grid.along_a]
        self.second += [sems.send(low, self.slot(me, 1), device) for device in grid.along_b]

    def middle(self):
        grid, sems = self.grid, self.sems
        self.load.wait()
        whole = self.out.at[:, grid.me] if self.inner_slot else self.out.at[grid.me]
        self.store = sems.copy(self.through, whole)
        if self.extra:
            own, _, part_ref, in_b, in_a = self.more
            total = own[...]
            for k, copy in enumerate(self.extra_b):
                copy.wait_recv()
                total = total + in_b[k]
            part_ref[...] = total
            self.extra_a = [
                sems.send(part_ref, in_a.at[k], device) for k, device in enumerate(grid.along_a)
            ]
        for copy, source in zip(self.first_b, grid.from_b):
            copy.wait_recv()
            held = self.slot(source, 0)
            self.second += [sems.send(held, held, device) for device in grid.along_a]
        for copy, source in zip(self.first_a, grid.from_a):
            copy.wait_recv()
            held = self.slot(source, 1)
            self.second += [sems.send(held, held, device) for device in grid.along_b]

    def end(self):
        if self.extra:
            _, total_ref, part_ref, _, in_a = self.more
            total = part_ref[...]
            for k, copy in enumerate(self.extra_a):
                copy.wait_recv()
                total = total + in_a[k]
            total_ref[...] = total
            for copy in self.extra_a + self.extra_b:
                copy.wait_send()
        for copy in self.first_a + self.first_b:
            copy.wait_send()
        for copy in self.second:
            copy.wait()
        self.store.wait()


class Scatter:
    peers = "tp"

    def __init__(self, partial):
        self.count, rows, width = partial.shape
        na, nb = halves(self.count)
        block = (rows // 2, width)
        self.sends = 2 * (na - 1) * (nb - 1) + 2 * (na - 1 + nb - 1)
        self.locals = na + nb
        self.operands, self.in_specs = [partial], [anywhere]
        self.shapes, self.out_specs = [jax.ShapeDtypeStruct((rows, width), f32)], [vmem]

        def buffer(*lead):
            return pltpu.VMEM(tuple(max(n, 1) for n in lead) + block, partial.dtype)

        self.scratch = [
            buffer(na), buffer(nb), buffer(nb - 1, na), buffer(na - 1, nb),
            buffer(na - 1), buffer(nb - 1), buffer(na - 1), buffer(nb - 1),
        ]

    def begin(self, ins, outs, scratch, sems):
        self.grid = grid = Grid(self.count)
        self.sems, self.out, self.scratch_refs = sems, outs[0], scratch
        own_a, own_b, one_a, one_b = scratch[:4]
        part = ins[0]
        na, nb, a, b = grid.na, grid.nb, grid.a, grid.b
        half = part.shape[1] // 2
        self.top, self.low = top, low = pl.ds(0, half), pl.ds(half, half)
        self.order_a = order_a = list(range(1, na)) + [0]
        self.order_b = order_b = list(range(1, nb)) + [0]
        self.first_a, self.first_b = {}, {}
        for step in range(max(na, nb)):
            if step < na:
                e = order_a[step]
                row = lax.rem(a + e, na) * nb
                for d in range(1, nb):
                    source = part.at[row + lax.rem(b + d, nb), top]
                    self.first_b[d, e] = sems.send(source, one_a.at[d - 1, e], grid.along_b[d - 1])
            if step < nb:
                e = order_b[step]
                column = lax.rem(b + e, nb)
                for d in range(1, na):
                    source = part.at[lax.rem(a + d, na) * nb + column, low]
                    self.first_a[d, e] = sems.send(source, one_b.at[d - 1, e], grid.along_a[d - 1])
        self.local_a = {
            e: sems.copy(part.at[lax.rem(a + e, na) * nb + b, top], own_a.at[e]) for e in order_a
        }
        self.local_b = {
            e: sems.copy(part.at[a * nb + lax.rem(b + e, nb), low], own_b.at[e]) for e in order_b
        }

    def sum_a(self, e):
        own_a, _, one_a = self.scratch_refs[:3]
        self.local_a[e].wait()
        total = own_a[e].astype(f32)
        for d in range(1, self.grid.nb):
            self.first_b[d, e].wait_recv()
            total = total + one_a[d - 1, e].astype(f32)
        return total

    def sum_b(self, e):
        _, own_b, _, one_b = self.scratch_refs[:4]
        self.local_b[e].wait()
        total = own_b[e].astype(f32)
        for d in range(1, self.grid.na):
            self.first_a[d, e].wait_recv()
            total = total + one_b[d - 1, e].astype(f32)
        return total

    def middle(self):
        grid, sems = self.grid, self.sems
        out_a, out_b, two_a, two_b = self.scratch_refs[4:]
        self.second_a, self.second_b = {}, {}
        for e in self.order_a[:-1]:
            out_a[e - 1] = self.sum_a(e).astype(out_a.dtype)
            self.second_a[e] = sems.send(out_a.at[e - 1], two_a.at[e - 1], grid.along_a[e - 1])
        for e in self.order_b[:-1]:
            out_b[e - 1] = self.sum_b(e).astype(out_b.dtype)
            self.second_b[e] = sems.send(out_b.at[e - 1], two_b.at[e - 1], grid.along_b[e - 1])

    def end(self):
        _, _, two_a, two_b = self.scratch_refs[4:]
        total = self.sum_a(0)
        for e in self.order_a[:-1]:
            self.second_a[e].wait_recv()
            total = total + two_a[e - 1].astype(f32)
        self.out[self.top] = total
        total = self.sum_b(0)
        for e in self.order_b[:-1]:
            self.second_b[e].wait_recv()
            total = total + two_b[e - 1].astype(f32)
        self.out[self.low] = total
        for group in (self.first_a, self.first_b, self.second_a, self.second_b):
            for copy in group.values():
                copy.wait_send()


class Swap:
    peers = "band"

    def __init__(self, x, extra=None):
        size = lax.axis_size("band")
        arrays = [x] if extra is None else [x, extra]
        self.operands, self.in_specs = arrays, [anywhere] * len(arrays)
        self.shapes = [jax.ShapeDtypeStruct(x.shape, x.dtype)]
        self.scratch = [pltpu.VMEM(x.shape[1:], x.dtype)]
        if extra is not None:
            self.shapes.append(jax.ShapeDtypeStruct((size,) + extra.shape, extra.dtype))
            self.scratch.append(pltpu.VMEM(extra.shape, extra.dtype))
        self.out_specs = [anywhere] * len(arrays)
        self.sends = (size - 1) * len(arrays)
        self.locals = 2 * len(arrays)

    def begin(self, ins, outs, scratch, sems):
        me = lax.axis_index("band")
        self.sems, self.scratch_refs = sems, scratch
        self.slots = [out.at[me] for out in outs]
        self.loads = [sems.copy(ins[0].at[me], scratch[0])]
        if len(ins) > 1:
            self.loads.append(sems.copy(ins[1], scratch[1]))
        self.copies = []
        for peer in band_peers():
            if len(ins) > 1:
                self.copies.append(sems.send(ins[1], self.slots[1], peer))
            self.copies.append(sems.send(ins[0].at[peer[0]], self.slots[0], peer))

    def middle(self):
        self.stores = []
        for load, through, slot in zip(self.loads, self.scratch_refs, self.slots):
            load.wait()
            self.stores.append(self.sems.copy(through, slot))

    def end(self):
        for copy in self.copies + self.stores:
            copy.wait()


class Work:
    def __init__(self, operands, tasks, early):
        self.tasks, self.early = tasks, early
        self.operands = operands
        self.shapes = []
        for kind, left, right, _, _ in tasks:
            known = [*operands, *self.shapes]
            if kind == "sum":
                self.shapes.append(jax.ShapeDtypeStruct((1, known[left].shape[1]), f32))
                continue
            rows = known[left].shape[1 if kind == "tn" else 0]
            columns = known[right].shape[0 if kind == "nt" else 1]
            self.shapes.append(jax.ShapeDtypeStruct((rows, columns), bf16))
        self.scratch = [pltpu.VMEM(x.shape, x.dtype) for x in [*operands, *self.shapes]]
        self.locals = len(operands) + len(tasks)

    def begin(self, ins, outs, scratch, sems):
        self.sems, self.outs = sems, outs
        self.held, self.made = scratch[: len(ins)], scratch[len(ins) :]
        self.loads = [sems.copy(source, target) for source, target in zip(ins, self.held)]
        self.stores = []

    def ready(self, k):
        if k < len(self.loads) and self.loads[k] is not None:
            self.loads[k].wait()
            self.loads[k] = None

    def run(self, tasks):
        for kind, left, right, scale, out in tasks:
            for k in (left, right, scale):
                if k is not None:
                    self.ready(k)
            known = [*self.held, *self.made]
            x, made = known[left], self.made[out]
            if kind == "sum":
                rows = min(128, x.shape[0])
                made[...] = jnp.zeros_like(made)

                def add(k, _, x=x, made=made, rows=rows):
                    r = pl.ds(pl.multiple_of(k * rows, rows), rows)
                    made[...] += jnp.sum(x[r, :].astype(f32), axis=0, keepdims=True)
                    return 0

                lax.fori_loop(0, x.shape[0] // rows, add, 0)
                self.stores.append(self.sems.copy(made, self.outs[out]))
                continue
            y = known[right]
            factor = None if scale is None else self.held[scale]
            tile_r, tile_c = min(512, made.shape[0]), min(512, made.shape[1])
            columns = made.shape[1] // tile_c

            def tile(k, _, kind=kind, x=x, y=y, made=made, factor=factor):
                i, j = k // columns, lax.rem(k, columns)
                r = pl.ds(pl.multiple_of(i * tile_r, tile_r), tile_r)
                c = pl.ds(pl.multiple_of(j * tile_c, tile_c), tile_c)
                if kind == "tn":
                    total = tn(x[:, r], y[:, c])
                elif kind == "nt":
                    total = nt(x[r, :], y[c, :])
                else:
                    total = nn(x[r, :], y[:, c])
                if factor is not None:
                    total = total * factor[r, c].astype(f32)
                made[r, c] = total.astype(made.dtype)
                return 0

            lax.fori_loop(0, (made.shape[0] // tile_r) * columns, tile, 0)
            self.stores.append(self.sems.copy(made, self.outs[out]))

    def end(self):
        for store in self.stores:
            store.wait()


def transfer(parts, cid, work=None, name="transfer", time=36):
    items = list(parts) + ([work] if work is not None else [])
    sends = sum(part.sends for part in parts)
    locals_ = sum(item.locals for item in items)

    def kernel(*refs):
        refs = list(refs)

        def take(number):
            taken = refs[:number]
            del refs[:number]
            return taken

        ins = [take(len(item.operands)) for item in items]
        outs = [take(len(item.shapes)) for item in items]
        scratch = [take(len(item.scratch)) for item in items]
        sems = Sems(*refs)
        devices = []
        if any(part.peers == "tp" for part in parts):
            devices += tp_peers()
        if any(part.peers == "band" for part in parts):
            devices += band_peers()
        barrier = pltpu.get_barrier_semaphore()
        for device in devices:
            pl.semaphore_signal(barrier, inc=1, device_id=device, device_id_type=MESH)
        if work is not None:
            work.begin(ins[-1], outs[-1], scratch[-1], sems)
        pl.semaphore_wait(barrier, len(devices))
        for part, i, o, t in zip(parts, ins, outs, scratch):
            part.begin(i, o, t, sems)
        if work is not None:
            work.run(work.tasks[: work.early])
        for part in parts:
            part.middle()
        if work is not None:
            work.run(work.tasks[work.early :])
        for part in parts:
            part.end()
        if work is not None:
            work.end()

    in_specs = [spec for part in parts for spec in part.in_specs]
    out_specs = [spec for part in parts for spec in part.out_specs]
    if work is not None:
        in_specs += [anywhere] * len(work.operands)
        out_specs += [anywhere] * len(work.shapes)
    return pl.pallas_call(
        kernel,
        out_shape=tuple(shape for item in items for shape in item.shapes),
        in_specs=in_specs,
        out_specs=tuple(out_specs),
        scratch_shapes=[
            *(scratch for item in items for scratch in item.scratch),
            pltpu.SemaphoreType.DMA((sends,)),
            pltpu.SemaphoreType.DMA((sends,)),
            pltpu.SemaphoreType.DMA((locals_,)),
        ],
        compiler_params=pltpu.CompilerParams(
            collective_id=cid, has_side_effects=True, vmem_limit_bytes=(58 if work else 32) * 2**20
        ),
        cost_estimate=takes(time),
        name=name,
    )(*(operand for item in items for operand in item.operands))


def gather_later(x, axis=0):
    x = jnp.expand_dims(x, axis)
    copies = jnp.broadcast_to(x, x.shape[:axis] + (lax.axis_size("tp"),) + x.shape[axis + 1 :])
    return lax.all_to_all(copies, "tp", axis, axis)


class Block:
    def __init__(self, order, shift, grid, size):
        band = lax.axis_index("band")
        self.order, self.shift = order, shift
        self.to, self.source = lax.rem(band + shift, size), lax.rem(band + size - shift, size)
        if order % 2 == 0:
            self.n1, self.n2 = grid.nb, grid.na
            self.first, self.second, self.origin = grid.along_b, grid.along_a, grid.from_b
            self.index = lambda d, e: lax.rem(grid.a + e, grid.na) * grid.nb + lax.rem(
                grid.b + d, grid.nb
            )
        else:
            self.n1, self.n2 = grid.na, grid.nb
            self.first, self.second, self.origin = grid.along_a, grid.along_b, grid.from_a
            self.index = lambda d, e: lax.rem(grid.a + d, grid.na) * grid.nb + lax.rem(
                grid.b + e, grid.nb
            )


def finish_kernel(
    count, size, part, unit, above, resid, inverse, gain, wide, narrow,
    out, wide_out, narrow_out,
    own, one, two_out, two, made, arrived, late, late_in, wide_in, narrow_in, pair, pair_b, pair_a,
    send_sem, recv_sem, local_sem,
):
    grid = Grid(count)
    sems = Sems(send_sem, recv_sem, local_sem)
    band = lax.axis_index("band")
    peers = band_peers()
    devices = grid.along_a + grid.along_b + peers
    barrier = pltpu.get_barrier_semaphore()
    for device in devices:
        pl.semaphore_signal(barrier, inc=1, device_id=device, device_id_type=MESH)
    shifts = list(range(1, size)) + [0]
    blocks = [Block(k, shift, grid, size) for k, shift in enumerate(shifts)]
    late[...] = jnp.zeros_like(late)
    pl.semaphore_wait(barrier, len(devices))
    done = []

    for blk in blocks:
        k = blk.order
        seconds = list(range(1, blk.n2)) + [0]
        blk.one = {
            (d, e): sems.send(
                part.at[blk.index(d, e), blk.to], one.at[k, d - 1, e], blk.first[d - 1]
            )
            for e in seconds
            for d in range(1, blk.n1)
        }
        blk.own = {e: sems.copy(part.at[blk.index(0, e), blk.to], own.at[k, e]) for e in seconds}
    early = []
    for peer in peers:
        early.append(sems.send(wide, wide_in.at[band], peer))
        early.append(sems.send(narrow, narrow_in.at[band], peer))

    def first_sum(blk, e):
        k = blk.order
        blk.own[e].wait()
        total = own[k, e].astype(f32)
        for d in range(1, blk.n1):
            blk.one[d, e].wait_recv()
            total = total + one[k, d - 1, e].astype(f32)
        return total

    def pass_on(blk):
        k = blk.order
        blk.two = []
        for e in range(1, blk.n2):
            two_out[k, e - 1] = first_sum(blk, e).astype(bf16)
            blk.two.append(sems.send(two_out.at[k, e - 1], two.at[k, e - 1], blk.second[e - 1]))

    def complete(blk):
        k = blk.order
        grad = first_sum(blk, 0)
        for e, copy in enumerate(blk.two):
            copy.wait_recv()
            grad = grad + two[k, e].astype(f32)
        normed = unit[blk.to]
        scaled = grad * gain[...]
        mean = jnp.mean(scaled, axis=-1, keepdims=True)
        along = jnp.mean(scaled * normed, axis=-1, keepdims=True)
        base = above[blk.to].astype(f32) + resid[blk.to]
        token = base + inverse[blk.to] * (scaled - mean - normed * along)
        made[k] = token.astype(bf16)
        sums = (jnp.sum(grad * normed, axis=0, keepdims=True), jnp.sum(grad, axis=0, keepdims=True))
        quarter = late.shape[1]
        for which, total in enumerate(sums):
            for i in range(4):
                row = slice(4 * which + i, 4 * which + i + 1)
                late[row, :] = late[row, :] + total[:, i * quarter : (i + 1) * quarter]
        if blk.shift:
            blk.swap = sems.send(made.at[k], arrived.at[k], (blk.to, lax.axis_index("tp")))

    def relay(blk):
        k = blk.order
        if blk.shift:
            blk.swap.wait_recv()
            held = arrived.at[k]
        else:
            held = made.at[k]
        slot = out.at[blk.source, grid.me]
        blk.near = [sems.send(held, slot, device) for device in blk.first]
        blk.far = [sems.send(held, slot, device) for device in blk.second]
        done.append(sems.copy(held, slot))

    def forward(blk):
        for copy, source in zip(blk.near, blk.origin):
            copy.wait_recv()
            held = out.at[blk.source, source]
            blk.far += [sems.send(held, held, device) for device in blk.second]

    pairs = [blocks[k : k + 2] for k in range(0, size, 2)]
    stages = (pass_on, complete, relay, forward)
    for step in range(len(pairs) + len(stages) - 1):
        for behind, stage in enumerate(stages):
            if 0 <= step - behind < len(pairs):
                for blk in pairs[step - behind]:
                    stage(blk)
        if step == len(pairs):
            last = [sems.send(late, late_in.at[band], peer) for peer in peers]

    for copy in early + last:
        copy.wait_recv()
    wide_in[band] = wide[...]
    narrow_in[band] = narrow[...]
    late_in[band] = late[...]
    total, narrow_total, late_total = (
        sum(array[k].astype(f32) for k in range(size)) for array in (wide_in, narrow_in, late_in)
    )
    narrow_out[...] = narrow_total
    pair[0:16, :] = total
    pair[16:24, :] = late_total
    near = [sems.send(pair, pair_b.at[k], device) for k, device in enumerate(grid.along_b)]
    total = pair[...]
    for k, copy in enumerate(near):
        copy.wait_recv()
        total = total + pair_b[k]
    for copy in near:
        copy.wait_send()
    pair[...] = total
    far = [sems.send(pair, pair_a.at[k], device) for k, device in enumerate(grid.along_a)]
    for k, copy in enumerate(far):
        copy.wait_recv()
        total = total + pair_a[k]
    wide_out[...] = total

    for copy in early + last + far:
        copy.wait_send()
    for blk in blocks:
        for copy in [*blk.one.values(), *blk.two, *blk.near]:
            copy.wait_send()
        if blk.shift:
            blk.swap.wait_send()
        for copy in blk.far:
            copy.wait()
    for copy in done:
        copy.wait()


def finish(part, unit, above, resid, inverse, gain, wide, narrow, cid):
    count, size, rows, width = part.shape
    na, nb = halves(count)
    most = max(na, nb)
    sends = locals_ = 0
    for k in range(size):
        n1, n2 = (nb, na) if k % 2 == 0 else (na, nb)
        sends += (n1 - 1) * n2 + 2 * (n2 - 1) + (n1 - 1) + (n1 - 1) * (n2 - 1)
        locals_ += n2 + 1
    sends += 4 * (size - 1) + na - 1 + nb - 1
    lanes = wide.shape[1]

    def blocks(*lead):
        return pltpu.VMEM(tuple(max(n, 1) for n in lead) + (rows, width), bf16)

    return pl.pallas_call(
        functools.partial(finish_kernel, count, size),
        out_shape=(
            jax.ShapeDtypeStruct((size, count, rows, width), bf16),
            jax.ShapeDtypeStruct((24, lanes), f32),
            jax.ShapeDtypeStruct(narrow.shape, f32),
        ),
        in_specs=[anywhere] + [vmem] * 7,
        out_specs=(anywhere, vmem, vmem),
        scratch_shapes=[
            blocks(size, most), blocks(size, most - 1, most),
            blocks(size, most - 1), blocks(size, most - 1),
            blocks(size), blocks(size),
            pltpu.VMEM((8, lanes), f32),
            pltpu.VMEM((size, 8, lanes), f32),
            pltpu.VMEM((size,) + wide.shape, bf16),
            pltpu.VMEM((size,) + narrow.shape, bf16),
            pltpu.VMEM((24, lanes), f32),
            pltpu.VMEM((max(nb - 1, 1), 24, lanes), f32),
            pltpu.VMEM((max(na - 1, 1), 24, lanes), f32),
            pltpu.SemaphoreType.DMA((sends,)),
            pltpu.SemaphoreType.DMA((sends,)),
            pltpu.SemaphoreType.DMA((locals_,)),
        ],
        compiler_params=pltpu.CompilerParams(
            collective_id=cid, has_side_effects=True, vmem_limit_bytes=48 * 2**20
        ),
        cost_estimate=takes(90),
        name="finish",
    )(part, unit, above, resid, inverse, gain, wide, narrow)


def heads_kernel(group, kind, x_ref, o_ref, through, local_sem, send_sem, recv_sem):
    band, tp = lax.axis_index("band"), lax.axis_index("tp")
    mine = lax.rem(band, group)
    base = band - mine
    others = [lax.rem(mine + d, group) for d in range(1, group)]
    sems = Sems(send_sem, recv_sem, local_sem)
    width = through.shape[1]

    def columns(index):
        return pl.ds(pl.multiple_of(index * width, width), width)

    def source(index):
        return x_ref.at[:, columns(index)] if kind == "cut" else x_ref.at[index]

    target = o_ref.at[:, columns(mine)] if kind == "join" else o_ref.at[mine]
    barrier = pltpu.get_barrier_semaphore()
    for other in others:
        pl.semaphore_signal(barrier, inc=1, device_id=(base + other, tp), device_id_type=MESH)
    load = sems.copy(source(mine), through)
    pl.semaphore_wait(barrier, group - 1)
    copies = [sems.send(source(other), target, (base + other, tp)) for other in others]
    load.wait()
    for copy in [sems.copy(through, target), *copies]:
        copy.wait()


def swap_heads(x, group, cid, kind):
    if kind == "cut":
        rows, width = x.shape[0], x.shape[1] // group
    else:
        rows, width = x.shape[1:]
    if width % 128 and kind == "cut":
        x = x.reshape(rows, group, width).transpose(1, 0, 2)
        return swap_heads(x, group, cid, "plain")
    if width % 128 and kind == "join":
        x = swap_heads(x, group, cid, "plain")
        return x.transpose(1, 0, 2).reshape(rows, group * width)
    shape = (rows, group * width) if kind == "join" else (group, rows, width)
    return pl.pallas_call(
        functools.partial(heads_kernel, group, kind),
        out_shape=jax.ShapeDtypeStruct(shape, x.dtype),
        in_specs=[anywhere],
        out_specs=anywhere,
        scratch_shapes=[
            pltpu.VMEM((rows, width), x.dtype),
            pltpu.SemaphoreType.DMA((2,)),
            pltpu.SemaphoreType.DMA((group - 1,)),
            pltpu.SemaphoreType.DMA((group - 1,)),
        ],
        compiler_params=pltpu.CompilerParams(collective_id=cid, has_side_effects=True),
        cost_estimate=takes(4),
        name="swap_heads",
    )(x)


def settle_kernel(
    wides, grad_ref, out_ref, up_ref, down_ref, wide_ref, narrow_ref,
    grad_to, out_to, up_to, down_to, *small,
):
    grad_to[...] = grad_ref[...].astype(f32)
    out_to[0] = out_ref[:, 0]
    up_to[...] = up_ref[...].astype(f32)
    down_to[...] = down_ref[...].astype(f32).T

    @pl.when(pl.program_id(0) == 0)
    def _():
        for refs, source in ((small[:wides], wide_ref), (small[wides:], narrow_ref)):
            lanes, row = source.shape[1], 0
            for ref in refs:
                for i in range(ref.shape[1] // lanes):
                    ref[0:1, i * lanes : (i + 1) * lanes] = source[row : row + 1, :]
                    row += 1


def settle(grad, out, up, down, wide, narrow, widths):
    size, count, rows, width = grad.shape
    wides = wide.shape[0] * wide.shape[1] // width
    slab = down.shape[1] // size
    small = [width] * wides + list(widths)
    block = pl.BlockSpec((1, count, rows, width), lambda i: (i, 0, 0, 0))
    across = pl.BlockSpec((up.shape[0] // size, up.shape[1]), lambda i: (i, 0))
    if up.shape[0] // size % 16:
        across = pl.BlockSpec(up.shape, lambda i: (0, 0))
    return pl.pallas_call(
        functools.partial(settle_kernel, wides),
        out_shape=(
            jax.ShapeDtypeStruct(grad.shape, f32),
            jax.ShapeDtypeStruct(grad.shape, out.dtype),
            jax.ShapeDtypeStruct(up.shape, f32),
            jax.ShapeDtypeStruct(down.shape[::-1], f32),
            *(jax.ShapeDtypeStruct((1, n), f32) for n in small),
        ),
        grid=(size,),
        in_specs=[
            block,
            pl.BlockSpec((count, 1, rows, width), lambda i: (0, i, 0, 0)),
            across,
            pl.BlockSpec((down.shape[0], slab), lambda i: (0, i)) if slab % 128 == 0 else vmem,
            pl.BlockSpec(wide.shape, lambda i: (0, 0)),
            pl.BlockSpec(narrow.shape, lambda i: (0, 0)),
        ],
        out_specs=(
            block,
            block,
            across,
            pl.BlockSpec((slab, down.shape[0]), lambda i: (i, 0)) if slab % 128 == 0 else vmem,
            *(pl.BlockSpec((1, n), lambda i: (0, 0)) for n in small),
        ),
        compiler_params=pltpu.CompilerParams(vmem_limit_bytes=40 * 2**20),
        cost_estimate=takes(10),
        name="settle",
    )(grad, out, up, down, wide, narrow)


def split_kernel(group, features, x_ref, q_ref, k_ref, v_ref, out_ref):
    for g in range(group):
        for which, ref in enumerate((q_ref, k_ref, v_ref)):
            start = (3 * g + which) * features
            ref[:, g * features : (g + 1) * features] = x_ref[:, start : start + features].astype(f32)
    out_ref[...] = x_ref[:, 3 * group * features :].astype(f32).T


def split_shared(x, group, features):
    rows, inner = x.shape[0], group * features
    return pl.pallas_call(
        functools.partial(split_kernel, group, features),
        out_shape=(
            *[jax.ShapeDtypeStruct((rows, inner), f32)] * 3,
            jax.ShapeDtypeStruct((x.shape[1] - 3 * inner, rows), f32),
        ),
        in_specs=[vmem],
        out_specs=(vmem,) * 4,
        compiler_params=pltpu.CompilerParams(vmem_limit_bytes=32 * 2**20),
        cost_estimate=takes(2),
        name="split_shared",
    )(x)


def project_kernel(x_ref, w_ref, bias_ref, scale_ref, o_ref):
    total = nn(x_ref[...], w_ref[...]) + bias_ref[...]
    o_ref[0] = total.astype(bf16) * scale_ref[...].astype(bf16)


def project(x, weight, bias, scale, group):
    rows, depth = x.shape
    total_width = bias.shape[0]
    width = total_width // group
    if width % 128:
        total = (nn(x, weight[:, :total_width]) + bias).astype(bf16) * scale.astype(bf16)
        return total.reshape(rows, group, width).transpose(1, 0, 2)
    block = min(256, rows)
    return pl.pallas_call(
        project_kernel,
        out_shape=jax.ShapeDtypeStruct((group, rows, width), bf16),
        grid=(group, rows // block),
        in_specs=[
            pl.BlockSpec((block, depth), lambda g, i: (i, 0)),
            pl.BlockSpec((depth, width), lambda g, i: (0, g)),
            pl.BlockSpec((1, width), lambda g, i: (0, g)),
            pl.BlockSpec((1, width), lambda g, i: (0, g)),
        ],
        out_specs=pl.BlockSpec((1, block, width), lambda g, i: (g, i, 0)),
        compiler_params=pltpu.CompilerParams(vmem_limit_bytes=40 * 2**20),
        cost_estimate=pl.CostEstimate(
            flops=2 * rows * depth * width * group, bytes_accessed=12 * 2**20, transcendentals=0
        ),
        name="project",
    )(x, weight, bias[None], scale[None])


def products_kernel(left_ref, right_ref, other_ref, last_ref, o_ref):
    tile, width = last_ref.shape[1], right_ref.shape[1]

    def step(k, _):
        columns = pl.ds(pl.multiple_of(k * tile, tile), tile)
        o_ref[:, columns] = tn(left_ref[...], right_ref[:, columns]).astype(o_ref.dtype)
        return 0

    lax.fori_loop(0, width // tile, step, 0)
    o_ref[:, width:] = tn(other_ref[...], last_ref[...]).astype(o_ref.dtype)


def product_kernel(left_ref, right_ref, o_ref):
    tile = min(512, o_ref.shape[1])

    def step(k, _):
        columns = pl.ds(pl.multiple_of(k * tile, tile), tile)
        o_ref[:, columns] = tn(left_ref[...], right_ref[:, columns]).astype(o_ref.dtype)
        return 0

    lax.fori_loop(0, o_ref.shape[1] // tile, step, 0)


def product(left, right):
    rows, depth = left.shape
    width = right.shape[1]
    tile = min(512, depth)
    return pl.pallas_call(
        product_kernel,
        out_shape=jax.ShapeDtypeStruct((depth, width), bf16),
        grid=(depth // tile,),
        in_specs=[
            pl.BlockSpec((rows, tile), lambda i: (0, i)),
            pl.BlockSpec((rows, width), lambda i: (0, 0)),
        ],
        out_specs=pl.BlockSpec((tile, width), lambda i: (i, 0)),
        compiler_params=pltpu.CompilerParams(vmem_limit_bytes=40 * 2**20),
        cost_estimate=takes(12),
        name="product",
    )(left, right)


def two_products(left, right, other, last):
    rows, depth = left.shape
    width, more = right.shape[1], last.shape[1]
    tile = min(512, depth)
    cut = pl.BlockSpec((rows, tile), lambda i: (0, i))
    return pl.pallas_call(
        products_kernel,
        out_shape=jax.ShapeDtypeStruct((depth, width + more), bf16),
        grid=(depth // tile,),
        in_specs=[
            cut,
            pl.BlockSpec((rows, width), lambda i: (0, 0)),
            cut,
            pl.BlockSpec((rows, more), lambda i: (0, 0)),
        ],
        out_specs=pl.BlockSpec((tile, width + more), lambda i: (i, 0)),
        compiler_params=pltpu.CompilerParams(vmem_limit_bytes=48 * 2**20),
        cost_estimate=takes(12),
        name="two_products",
    )(left, right, other, last)


def permitted(first, limit, row, column):
    return ((column >= first) & (column <= limit)) | (column == row)


def head_mask(head, shape):
    lane = lax.broadcasted_iota(jnp.int32, shape, 1)
    return (lane >= head * HEAD_DIM) & (lane < (head + 1) * HEAD_DIM)


def attend_kernel(qb, kb, info_ref, first_ref, q_ref, k_ref, v_ref, o_ref, log_ref, vt_ref):
    length, width = q_ref.shape
    heads = width // HEAD_DIM
    live_end = info_ref[0]
    count = lax.div(live_end + qb - 1, qb)
    vt_ref[...] = v_ref[...].T
    o_ref[...] = jnp.zeros_like(o_ref)
    log_ref[...] = jnp.zeros_like(log_ref)

    def queries(i, _):
        rows = pl.ds(pl.multiple_of(i * qb, qb), qb)
        q = q_ref[rows, :]
        first = first_ref[0:1, rows]
        row = i * qb + lax.broadcasted_iota(jnp.int32, (1, qb), 1)
        limit = jnp.minimum(row, live_end - 1)
        q_heads = [
            jnp.where(head_mask(h, (qb, width)), q, jnp.zeros_like(q)) for h in range(heads)
        ]
        def keys(j, carry):
            columns = pl.ds(pl.multiple_of(j * kb, kb), kb)
            k = k_ref[columns, :]
            column = j * kb + lax.broadcasted_iota(jnp.int32, (kb, 1), 0)
            allowed = permitted(first, limit, row, column)
            out = []
            for h in range(heads):
                top, total, summed = carry[h]
                scores = jnp.where(allowed, nt(k, q_heads[h]), masked_score)
                new_top = jnp.maximum(top, jnp.max(scores, axis=0, keepdims=True))
                weights = jnp.exp(scores - new_top)
                scale = jnp.exp(top - new_top)
                total = total * scale + jnp.sum(weights, axis=0, keepdims=True)
                vt = vt_ref[h * HEAD_DIM : (h + 1) * HEAD_DIM, columns]
                summed = summed * scale + nn(vt, weights.astype(bf16))
                out.append((new_top, total, summed))
            return tuple(out)
        start = tuple(
            (
                jnp.full((1, qb), masked_score, f32),
                jnp.zeros((1, qb), f32),
                jnp.zeros((HEAD_DIM, qb), f32),
            )
            for _ in range(heads)
        )
        lo = lax.div(info_ref[1 + i], kb)
        hi = lax.div(i * qb + qb - 1, kb) + 1
        done = lax.fori_loop(lo, hi, keys, start)
        mixed = jnp.concatenate([summed / total for _, total, summed in done], axis=0)
        o_ref[rows, :] = mixed.T.astype(o_ref.dtype)
        for h, (top, total, _) in enumerate(done):
            log_ref[0, h : h + 1, rows] = top + jnp.log(total)
        return 0
    lax.fori_loop(0, count, queries, 0)


def attend_back_kernel(
    qb, kb, info_ref, first_ref, q_ref, k_ref, v_ref, o_ref, do_ref, log_ref, out_ref, sum_ref,
    dk_acc, dv_acc,
):
    length, width = q_ref.shape
    heads = width // HEAD_DIM
    features = out_ref.shape[1] // 3
    slab = pl.program_id(0)
    factor = HEAD_DIM ** (-0.5)
    live_end = info_ref[0]
    count = lax.div(live_end + qb - 1, qb)

    def lanes(which):
        if features == width:
            return pl.ds(which * features, width)
        return pl.ds(pl.multiple_of(which * features + slab * width, width), width)
    dk_acc[...] = jnp.zeros_like(dk_acc)
    dv_acc[...] = jnp.zeros_like(dv_acc)
    out_ref[:, lanes(0)] = jnp.zeros((length, width), out_ref.dtype)

    def queries(i, _):
        rows = pl.ds(pl.multiple_of(i * qb, qb), qb)
        q, do = q_ref[rows, :], do_ref[rows, :]
        first = first_ref[0:1, rows]
        row = i * qb + lax.broadcasted_iota(jnp.int32, (1, qb), 1)
        limit = jnp.minimum(row, live_end - 1)
        dots = (do.astype(f32) * o_ref[rows, :].astype(f32)).T
        masks = [head_mask(h, (qb, width)) for h in range(heads)]
        kmasks = [head_mask(h, (kb, width)) for h in range(heads)]
        zero = jnp.zeros_like(q)
        q_heads = [jnp.where(mask, q, zero) for mask in masks]
        do_heads = [jnp.where(mask, do, zero) for mask in masks]
        logs = [log_ref[0, h : h + 1, rows] for h in range(heads)]
        deltas = [
            jnp.sum(dots[h * HEAD_DIM : (h + 1) * HEAD_DIM], axis=0, keepdims=True)
            for h in range(heads)
        ]
        def keys(j, dq):
            columns = pl.ds(pl.multiple_of(j * kb, kb), kb)
            k, v = k_ref[columns, :], v_ref[columns, :]
            column = j * kb + lax.broadcasted_iota(jnp.int32, (kb, 1), 0)
            allowed = permitted(first, limit, row, column)
            dk, dv = dk_acc[columns, :], dv_acc[columns, :]
            for h in range(heads):
                scores = jnp.where(allowed, nt(k, q_heads[h]) - logs[h], masked_score)
                probs = jnp.exp(scores)
                prob_grad = nt(v, do_heads[h])
                score_grad = (probs * (prob_grad - deltas[h])).astype(bf16)
                dv = dv + nn(probs.astype(bf16), do_heads[h])
                dk = dk + nn(score_grad, q_heads[h])
                dq = dq + tn(score_grad, jnp.where(kmasks[h], k, jnp.zeros_like(k)))
            dk_acc[columns, :] = dk
            dv_acc[columns, :] = dv
            return dq
        lo = lax.div(info_ref[1 + i], kb)
        hi = lax.div(i * qb + qb - 1, kb) + 1
        dq = lax.fori_loop(lo, hi, keys, jnp.zeros((qb, width), f32))
        out_ref[rows, lanes(0)] = (dq * factor).astype(out_ref.dtype)
        return 0
    lax.fori_loop(0, count, queries, 0)
    sum_ref[...] = jnp.zeros_like(sum_ref)

    def store(i, _):
        rows = pl.ds(pl.multiple_of(i * kb, kb), kb)
        dv = dv_acc[rows, :].astype(out_ref.dtype)
        out_ref[rows, lanes(1)] = dk_acc[rows, :].astype(out_ref.dtype)
        out_ref[rows, lanes(2)] = dv
        dq = out_ref[rows, lanes(0)].astype(f32)
        sum_ref[0, 0:1, :] += jnp.sum(dq, axis=0, keepdims=True)
        sum_ref[0, 1:2, :] += jnp.sum(dv.astype(f32), axis=0, keepdims=True)
        return 0
    lax.fori_loop(0, length // kb, store, 0)


def attention_specs(length, features):
    width = min(256, features)
    slabs = features // width

    plain = pl.BlockSpec((length, width), lambda i, info: (0, i))

    def piece(which):
        if features % 128:
            return plain
        return pl.BlockSpec((length, width), lambda i, info, w=which: (0, w * slabs + i))

    logs = pl.BlockSpec((1, 8, length), lambda i, info: (i, 0, 0))
    first = pl.BlockSpec((1, length), lambda i, info: (0, 0))
    return width, slabs, piece, plain, logs, first


def three(qkv, features):
    if features % 128:
        return [qkv[:, w * features : (w + 1) * features] for w in range(3)]
    return [qkv] * 3


def attend(qkv, info, first, qb, kb):
    length, features = qkv.shape[0], qkv.shape[1] // 3
    width, slabs, piece, plain, logs, first_spec = attention_specs(length, features)
    return pl.pallas_call(
        functools.partial(attend_kernel, qb, kb),
        out_shape=(
            jax.ShapeDtypeStruct((length, features), bf16),
            jax.ShapeDtypeStruct((slabs, 8, length), f32),
        ),
        grid_spec=pltpu.PrefetchScalarGridSpec(
            num_scalar_prefetch=1,
            grid=(slabs,),
            in_specs=[first_spec, piece(0), piece(1), piece(2)],
            out_specs=(plain, logs),
            scratch_shapes=[pltpu.VMEM((width, length), bf16)],
        ),
        compiler_params=pltpu.CompilerParams(vmem_limit_bytes=48 * 2**20),
        cost_estimate=takes(30),
        name="attend",
    )(info, first, *three(qkv, features))


def attend_back(qkv, mixed, grad, log_total, info, first, qb, kb):
    length, features = qkv.shape[0], qkv.shape[1] // 3
    width, slabs, piece, plain, logs, first_spec = attention_specs(length, features)
    return pl.pallas_call(
        functools.partial(attend_back_kernel, qb, kb),
        out_shape=(
            jax.ShapeDtypeStruct((length, 3 * features), bf16),
            jax.ShapeDtypeStruct((slabs, 8, width), f32),
        ),
        grid_spec=pltpu.PrefetchScalarGridSpec(
            num_scalar_prefetch=1,
            grid=(slabs,),
            in_specs=[first_spec, piece(0), piece(1), piece(2), plain, plain, logs],
            out_specs=(
                pl.BlockSpec((length, 3 * features), lambda i, info: (0, 0)),
                pl.BlockSpec((1, 8, width), lambda i, info: (i, 0, 0)),
            ),
            scratch_shapes=[pltpu.VMEM((length, width), f32), pltpu.VMEM((length, width), f32)],
        ),
        compiler_params=pltpu.CompilerParams(vmem_limit_bytes=48 * 2**20),
        cost_estimate=takes(34),
        name="attend_back",
    )(info, first, *three(qkv, features), mixed, grad, log_total)


def body(
    tokens,
    positions,
    doc_lengths,
    exit_depth,
    w_query,
    w_key,
    w_value,
    w_out,
    w_up,
    w_down,
    b_query,
    b_value,
    b_out,
    b_up,
    b_down,
    attn_gain,
    attn_bias,
    ffn_gain,
    ffn_bias,
    cotangent,
):
    seqs, local_rows, width = tokens.shape
    inner = b_query.shape[0]
    bands, tps = lax.axis_size("band"), lax.axis_size("tp")
    group = bands // seqs
    piece = local_rows // (group * tps)
    band, tp = lax.axis_index("band"), lax.axis_index("tp")
    seq, member = band // group, lax.rem(band, group)
    features = inner // group
    length = exit_depth.shape[1]
    own = bands * piece
    rows = tps * own
    block, half_block = min(512, length), min(256, length)

    def by_group(*parts):
        split = [p.reshape(p.shape[:-1] + (group, features)) for p in parts]
        return jnp.stack(split, axis=-2).reshape(parts[0].shape[:-1] + (-1,))

    def share(grad):
        return lax.psum_scatter(grad, "band", scatter_dimension=0, tiled=True)

    w_in_out = jnp.concatenate([by_group(w_query, w_key, w_value), w_out.T], axis=1)
    w_in_out = lax.all_gather(w_in_out, "band", axis=0, tiled=True)
    w_in, w_out_t = w_in_out[:, : 3 * inner], w_in_out[:, 3 * inner :]
    w_up_all = lax.all_gather(w_up, "band", axis=0, tiled=True)
    w_down_t = lax.all_gather(w_down.T, "band", axis=0, tiled=True)

    def my_share(array):
        split = array.reshape(seqs, group, tps, piece, width)
        return lax.dynamic_index_in_dim(split, tp, 2, keepdims=False).reshape(bands, piece, width)

    token_own, all_pos = transfer([Swap(my_share(tokens), positions)], 0, name="swap_in")
    seq_pos = lax.dynamic_index_in_dim(all_pos, seq, 1, keepdims=False)
    seq_pos = seq_pos.reshape(bands, group, tps, piece).transpose(1, 2, 0, 3)
    row_pos = seq_pos.reshape(length)
    member_pos = lax.dynamic_index_in_dim(seq_pos, member, 0, keepdims=False)
    own_pos = lax.dynamic_index_in_dim(member_pos, tp, 0, keepdims=False).reshape(own)
    depths = lax.dynamic_index_in_dim(exit_depth, seq, 0, keepdims=False)
    live_end = jnp.sum((depths > LAYER).astype(jnp.int32))
    live_own = (own_pos < live_end).astype(f32)[:, None]
    ends = jnp.cumsum(lax.dynamic_index_in_dim(doc_lengths, seq, 0, keepdims=False))
    places = jnp.arange(length, dtype=jnp.int32)
    first = jnp.max(jnp.where(ends[:, None] <= places[None, :], ends[:, None], 0), axis=0)
    info = jnp.concatenate([live_end[None], first[::block]]).astype(jnp.int32)
    first = first[None, :].astype(jnp.int32)
    to_sorted = (row_pos[None, :] == places[:, None]).astype(bf16)
    to_rows = (row_pos[:, None] == places[None, :]).astype(bf16)

    inputs = token_own.reshape(own, width).astype(f32)
    normed_in, unit_in, inverse_in = layer_norm(inputs, attn_gain, attn_bias)
    z1, grad_low = transfer([Gather(normed_in.astype(bf16)), Swap(my_share(cotangent))], 1, name="gather_in")
    z1 = z1.reshape(rows, width)
    grad_own = grad_low.reshape(own, width).astype(f32)
    down_grad_own = (live_own * grad_own).astype(bf16)
    down_grad = gather_later(down_grad_own)

    bias_in = by_group(b_query, jnp.zeros_like(b_query), b_value)
    scale_in = by_group(
        jnp.full_like(b_query, HEAD_DIM ** (-0.5)), jnp.ones_like(b_query), jnp.ones_like(b_query)
    )
    qkv = project(z1, w_in_out, bias_in, scale_in, group)
    qkv = swap_heads(qkv, group, 4, "plain").reshape(length, 3 * features)
    qkv = nn(to_sorted, qkv).astype(bf16)
    mixed_sorted, log_total = attend(qkv, info, first, block, block)
    mixed_sorted, down_grad = lax.optimization_barrier((mixed_sorted, down_grad))
    down_grad = down_grad.reshape(rows, width)
    mixed = nn(to_rows, mixed_sorted).astype(bf16).reshape(group, rows, features)
    mixed = swap_heads(mixed, group, 5, "join")

    attn_part = nt(mixed, w_out_t).astype(bf16).reshape(tps, own, width)
    (attn_out,) = transfer([Scatter(attn_part)], 6, name="scatter_attn")
    attn_out = attn_out + b_out
    residual = inputs + attn_out
    normed_mid, unit_mid, inverse_mid = layer_norm(residual, ffn_gain, ffn_bias)
    (z2,) = transfer([Gather(normed_mid.astype(bf16))], 7, name="gather_mid")
    z2 = z2.reshape(rows, width)
    pre_act = nn(z2, w_up_all) + b_up
    below = 0.5 * (1.0 + lax.erf(pre_act * 0.5**0.5))
    act = (pre_act * below).astype(bf16)
    slope = (below + pre_act * jnp.exp(-0.5 * pre_act * pre_act) * (2 * math.pi) ** -0.5).astype(bf16)

    grad_w_down_t = product(down_grad, act)
    grad_w_down_t, act = lax.optimization_barrier((grad_w_down_t, act))
    shared_down = share(grad_w_down_t)
    ffn_part = nt(act, w_down_t).astype(bf16).reshape(tps, own, width)
    ffn_out, up_grad, mid_part = transfer(
        [Scatter(ffn_part)],
        8,
        Work(
            [down_grad, w_down_t, slope, w_up_all],
            [("nn", 0, 1, 2, 0), ("nt", 4, 3, None, 1)],
            1,
        ),
        name="scatter_ffn",
    )
    output = (inputs + live_own * (attn_out + ffn_out + b_down)).astype(bf16)
    output = output.reshape(bands, piece, width)

    mid_part = mid_part.reshape(tps, own, width)
    mid_grad, grad_w_up, up_sums = transfer(
        [Scatter(mid_part)],
        9,
        Work([z2, up_grad], [("tn", 0, 1, None, 0), ("sum", 1, None, None, 1)], 1),
        name="scatter_mid",
    )
    resid_grad = norm_back(mid_grad, unit_mid, inverse_mid, ffn_gain)
    attn_grad_own = (live_own * grad_own + resid_grad).astype(bf16)
    attn_grad, output = transfer([Gather(attn_grad_own), Swap(output)], 10, name="gather_back")
    attn_grad = attn_grad.reshape(rows, width)
    attn_grad, output, grad_w_up = lax.optimization_barrier((attn_grad, output, grad_w_up))
    output = gather_later(output)

    mixed_grad = nn(attn_grad, w_out_t).astype(bf16)
    mixed_grad = swap_heads(mixed_grad, group, 13, "cut").reshape(length, features)
    mixed_grad = nn(to_sorted, mixed_grad).astype(bf16)
    grad_w_up, shared_down = lax.optimization_barrier((grad_w_up, shared_down))
    shared_up = share(grad_w_up)
    in_grad, in_sums = attend_back(
        qkv, mixed_sorted, mixed_grad, log_total, info, first, block, half_block
    )
    in_sums = in_sums.transpose(1, 0, 2).reshape(8, features)
    mine = (jnp.arange(group) == member).astype(f32)[:, None]
    in_grad = nn(to_rows, in_grad).astype(bf16).reshape(group, rows, 3 * features)
    in_grad = swap_heads(in_grad, group, 14, "join")
    in_grad, output = lax.optimization_barrier((in_grad, output))
    grad_w_in_out = two_products(z1, in_grad, attn_grad, mixed)
    in_grad, grad_w_in_out = lax.optimization_barrier((in_grad, grad_w_in_out))
    in_part = nt(in_grad, w_in).astype(bf16).reshape(tps, bands, piece, width)
    grad_w_in_out, shared_up, in_part = lax.optimization_barrier((grad_w_in_out, shared_up, in_part))
    shared_in_out = share(grad_w_in_out)

    def over_rows(array):
        return jnp.sum(array.astype(f32), axis=0)

    wide = [
        over_rows(attn_grad_own),
        over_rows(down_grad_own),
        over_rows(mid_grad * unit_mid),
        over_rows(mid_grad),
    ]
    wide = jnp.concatenate(wide).astype(bf16).reshape(16, width // 4)
    narrow = jnp.concatenate(
        [(mine * in_sums[0]).reshape(-1), (mine * in_sums[1]).reshape(-1), up_sums[0]]
    )
    count = narrow.shape[0]
    narrow = jnp.pad(narrow, (0, -count % 2048)).astype(bf16).reshape(16, -1)
    token_grad, wide, narrow = finish(
        in_part,
        unit_in.reshape(bands, piece, width),
        grad_low,
        resid_grad.reshape(bands, piece, width),
        inverse_in.reshape(bands, piece, 1),
        attn_gain[None],
        wide,
        narrow,
        15,
    )
    token_grad, output, shared_up, shared_down, *small = settle(
        token_grad, output, shared_up, shared_down, wide, narrow, (inner, inner, b_up.shape[0])
    )
    token_grad, output = token_grad.reshape(tokens.shape), output.reshape(tokens.shape)
    small = [vector.reshape(-1) for vector in small]
    shared_q, shared_k, shared_v, shared_out = split_shared(shared_in_out, group, features)
    return (
        output,
        token_grad,
        shared_q,
        shared_k,
        shared_v,
        shared_out,
        shared_up,
        shared_down,
        small[6],
        small[7],
        small[0],
        small[8],
        small[1],
        small[4],
        small[5],
        small[2],
        small[3],
    )


def solution(mesh):
    return jax.shard_map(
        body,
        mesh=mesh,
        in_specs=(
            P(None, "band", None),
            P(None, "band"),
            P(),
            P(),
            P("band", "tp"),
            P("band", "tp"),
            P("band", "tp"),
            P("tp", "band"),
            P("band", "tp"),
            P("tp", "band"),
            P("tp"),
            P("tp"),
            P(),
            P("tp"),
            P(),
            P(),
            P(),
            P(),
            P(),
            P(None, "band", None),
        ),
        out_specs=(
            P(None, "band", None),
            P(None, "band", None),
            P("band", "tp"),
            P("band", "tp"),
            P("band", "tp"),
            P("tp", "band"),
            P("band", "tp"),
            P("tp", "band"),
            P("tp"),
            P("tp"),
            P(),
            P("tp"),
            P(),
            P(),
            P(),
            P(),
            P(),
        ),
        check_vma=False,
    )
```

```python
import functools
import math

import jax
import jax.numpy as jnp
from jax import lax
from jax.experimental import pallas as pl
from jax.experimental.pallas import tpu as pltpu
from jax.sharding import PartitionSpec as P

HEAD_DIM = 64
LAYER = 12
MESH = pl.DeviceIdType.MESH

epsilon = 1e-05
masked_score = -1e30
bf16 = jnp.bfloat16
f32 = jnp.float32


def layer_norm(values, gain, shift):
    center = values - jnp.mean(values, axis=-1, keepdims=True)
    inverse = lax.rsqrt(jnp.mean(center * center, axis=-1, keepdims=True) + epsilon)
    normed = center * inverse
    return (normed * gain + shift, normed, inverse)


def norm_back(grad_out, normed, inverse, gain):
    scaled = grad_out * gain
    return inverse * (
        scaled
        - jnp.mean(scaled, axis=-1, keepdims=True)
        - normed * jnp.mean(scaled * normed, axis=-1, keepdims=True)
    )


def nn(left, right):
    return jnp.dot(left, right, preferred_element_type=f32)


def nt(left, right):
    return lax.dot_general(left, right, (((1,), (1,)), ((), ())), preferred_element_type=f32)


def tn(left, right):
    return lax.dot_general(left, right, (((0,), (0,)), ((), ())), preferred_element_type=f32)


def gelu_exact(values):
    return jax.nn.gelu(values, approximate=False)


def halves(count):
    return (count // 2, 2) if count % 2 == 0 else (count, 1)


def takes(microseconds):
    return pl.CostEstimate(
        flops=int(microseconds * 1e9), bytes_accessed=int(microseconds * 2e6), transcendentals=0
    )


class Sems:
    def __init__(self, send_sem, recv_sem, local_sem):
        self.send_sem, self.recv_sem, self.local_sem = send_sem, recv_sem, local_sem
        self.sent = self.local = 0

    def send(self, source, target, device):
        k = self.sent
        self.sent += 1
        copy = pltpu.make_async_remote_copy(
            source, target, self.send_sem.at[k], self.recv_sem.at[k],
            device_id=device, device_id_type=MESH,
        )
        copy.start()
        return copy

    def copy(self, source, target):
        k = self.local
        self.local += 1
        copy = pltpu.make_async_copy(source, target, self.local_sem.at[k])
        copy.start()
        return copy


class Grid:
    def __init__(self, count):
        self.na, self.nb = na, nb = halves(count)
        self.me, band = lax.axis_index("tp"), lax.axis_index("band")
        self.a, self.b = a, b = self.me // nb, lax.rem(self.me, nb)
        self.along_b = [(band, a * nb + lax.rem(b + d, nb)) for d in range(1, nb)]
        self.along_a = [(band, lax.rem(a + d, na) * nb + b) for d in range(1, na)]
        self.from_b = [a * nb + lax.rem(b + nb - d, nb) for d in range(1, nb)]
        self.from_a = [lax.rem(a + na - d, na) * nb + b for d in range(1, na)]


def tp_peers():
    grid = Grid(lax.axis_size("tp"))
    return grid.along_a + grid.along_b


def band_peers():
    size = lax.axis_size("band")
    me, tp = lax.axis_index("band"), lax.axis_index("tp")
    return [(lax.rem(me + d, size), tp) for d in range(1, size)]


anywhere = pl.BlockSpec(memory_space=pl.ANY)
vmem = pl.BlockSpec(memory_space=pltpu.VMEM)


class Gather:
    peers = "tp"

    def __init__(self, x, inner_slot=False, extra=None):
        self.count = count = lax.axis_size("tp")
        na, nb = halves(count)
        self.inner_slot, self.extra = inner_slot, extra is not None
        self.sends = 2 * (na - 1 + nb - 1) + 2 * (na - 1) * (nb - 1)
        self.locals = 2
        shape = (x.shape[0], count) + x.shape[1:] if inner_slot else (count,) + x.shape
        self.operands, self.in_specs = [x], [anywhere]
        self.shapes, self.out_specs = [jax.ShapeDtypeStruct(shape, x.dtype)], [anywhere]
        self.scratch = [pltpu.VMEM(x.shape, x.dtype)]
        if self.extra:
            self.operands.append(extra)
            self.in_specs.append(vmem)
            self.shapes.append(jax.ShapeDtypeStruct(extra.shape, extra.dtype))
            self.out_specs.append(vmem)
            self.sends += na - 1 + nb - 1
            self.scratch += [
                pltpu.VMEM(extra.shape, extra.dtype),
                pltpu.VMEM((max(nb - 1, 1),) + extra.shape, extra.dtype),
                pltpu.VMEM((max(na - 1, 1),) + extra.shape, extra.dtype),
            ]

    def slot(self, index, which):
        part = self.part[which]
        return self.out.at[part, index] if self.inner_slot else self.out.at[index, part]

    def begin(self, ins, outs, scratch, sems):
        self.grid = grid = Grid(self.count)
        self.sems = sems
        x, self.out = ins[0], outs[0]
        half = x.shape[0] // 2
        self.part = part = (pl.ds(0, half), pl.ds(half, half))
        self.through = scratch[0]
        self.load = sems.copy(x, self.through)
        me = grid.me
        if self.extra:
            self.more = (ins[1], outs[1], *scratch[1:])
            self.extra_b = [
                sems.send(ins[1], scratch[2].at[k], device) for k, device in enumerate(grid.along_b)
            ]
        top, low = x.at[part[0]], x.at[part[1]]
        self.first_b = [sems.send(top, self.slot(me, 0), device) for device in grid.along_b]
        self.first_a = [sems.send(low, self.slot(me, 1), device) for device in grid.along_a]
        self.second = [sems.send(top, self.slot(me, 0), device) for device in grid.along_a]
        self.second += [sems.send(low, self.slot(me, 1), device) for device in grid.along_b]

    def middle(self):
        grid, sems = self.grid, self.sems
        self.load.wait()
        whole = self.out.at[:, grid.me] if self.inner_slot else self.out.at[grid.me]
        self.store = sems.copy(self.through, whole)
        if self.extra:
            own, _, part_ref, in_b, in_a = self.more
            total = own[...]
            for k, copy in enumerate(self.extra_b):
                copy.wait_recv()
                total = total + in_b[k]
            part_ref[...] = total
            self.extra_a = [
                sems.send(part_ref, in_a.at[k], device) for k, device in enumerate(grid.along_a)
            ]
        for copy, source in zip(self.first_b, grid.from_b):
            copy.wait_recv()
            held = self.slot(source, 0)
            self.second += [sems.send(held, held, device) for device in grid.along_a]
        for copy, source in zip(self.first_a, grid.from_a):
            copy.wait_recv()
            held = self.slot(source, 1)
            self.second += [sems.send(held, held, device) for device in grid.along_b]

    def end(self):
        if self.extra:
            _, total_ref, part_ref, _, in_a = self.more
            total = part_ref[...]
            for k, copy in enumerate(self.extra_a):
                copy.wait_recv()
                total = total + in_a[k]
            total_ref[...] = total
            for copy in self.extra_a + self.extra_b:
                copy.wait_send()
        for copy in self.first_a + self.first_b:
            copy.wait_send()
        for copy in self.second:
            copy.wait()
        self.store.wait()


class Scatter:
    peers = "tp"

    def __init__(self, partial):
        self.count, rows, width = partial.shape
        na, nb = halves(self.count)
        block = (rows // 2, width)
        self.sends = 2 * (na - 1) * (nb - 1) + 2 * (na - 1 + nb - 1)
        self.locals = na + nb
        self.operands, self.in_specs = [partial], [anywhere]
        self.shapes, self.out_specs = [jax.ShapeDtypeStruct((rows, width), f32)], [vmem]

        def buffer(*lead):
            return pltpu.VMEM(tuple(max(n, 1) for n in lead) + block, partial.dtype)

        self.scratch = [
            buffer(na), buffer(nb), buffer(nb - 1, na), buffer(na - 1, nb),
            buffer(na - 1), buffer(nb - 1), buffer(na - 1), buffer(nb - 1),
        ]

    def begin(self, ins, outs, scratch, sems):
        self.grid = grid = Grid(self.count)
        self.sems, self.out, self.scratch_refs = sems, outs[0], scratch
        own_a, own_b, one_a, one_b = scratch[:4]
        part = ins[0]
        na, nb, a, b = grid.na, grid.nb, grid.a, grid.b
        half = part.shape[1] // 2
        self.top, self.low = top, low = pl.ds(0, half), pl.ds(half, half)
        self.order_a = order_a = list(range(1, na)) + [0]
        self.order_b = order_b = list(range(1, nb)) + [0]
        self.first_a, self.first_b = {}, {}
        for step in range(max(na, nb)):
            if step < na:
                e = order_a[step]
                row = lax.rem(a + e, na) * nb
                for d in range(1, nb):
                    source = part.at[row + lax.rem(b + d, nb), top]
                    self.first_b[d, e] = sems.send(source, one_a.at[d - 1, e], grid.along_b[d - 1])
            if step < nb:
                e = order_b[step]
                column = lax.rem(b + e, nb)
                for d in range(1, na):
                    source = part.at[lax.rem(a + d, na) * nb + column, low]
                    self.first_a[d, e] = sems.send(source, one_b.at[d - 1, e], grid.along_a[d - 1])
        self.local_a = {
            e: sems.copy(part.at[lax.rem(a + e, na) * nb + b, top], own_a.at[e]) for e in order_a
        }
        self.local_b = {
            e: sems.copy(part.at[a * nb + lax.rem(b + e, nb), low], own_b.at[e]) for e in order_b
        }

    def sum_a(self, e):
        own_a, _, one_a = self.scratch_refs[:3]
        self.local_a[e].wait()
        total = own_a[e].astype(f32)
        for d in range(1, self.grid.nb):
            self.first_b[d, e].wait_recv()
            total = total + one_a[d - 1, e].astype(f32)
        return total

    def sum_b(self, e):
        _, own_b, _, one_b = self.scratch_refs[:4]
        self.local_b[e].wait()
        total = own_b[e].astype(f32)
        for d in range(1, self.grid.na):
            self.first_a[d, e].wait_recv()
            total = total + one_b[d - 1, e].astype(f32)
        return total

    def middle(self):
        grid, sems = self.grid, self.sems
        out_a, out_b, two_a, two_b = self.scratch_refs[4:]
        self.second_a, self.second_b = {}, {}
        for e in self.order_a[:-1]:
            out_a[e - 1] = self.sum_a(e).astype(out_a.dtype)
            self.second_a[e] = sems.send(out_a.at[e - 1], two_a.at[e - 1], grid.along_a[e - 1])
        for e in self.order_b[:-1]:
            out_b[e - 1] = self.sum_b(e).astype(out_b.dtype)
            self.second_b[e] = sems.send(out_b.at[e - 1], two_b.at[e - 1], grid.along_b[e - 1])

    def end(self):
        _, _, two_a, two_b = self.scratch_refs[4:]
        total = self.sum_a(0)
        for e in self.order_a[:-1]:
            self.second_a[e].wait_recv()
            total = total + two_a[e - 1].astype(f32)
        self.out[self.top] = total
        total = self.sum_b(0)
        for e in self.order_b[:-1]:
            self.second_b[e].wait_recv()
            total = total + two_b[e - 1].astype(f32)
        self.out[self.low] = total
        for group in (self.first_a, self.first_b, self.second_a, self.second_b):
            for copy in group.values():
                copy.wait_send()


class Swap:
    peers = "band"

    def __init__(self, x, extra=None):
        size = lax.axis_size("band")
        arrays = [x] if extra is None else [x, extra]
        self.operands, self.in_specs = arrays, [anywhere] * len(arrays)
        self.shapes = [jax.ShapeDtypeStruct(x.shape, x.dtype)]
        self.scratch = [pltpu.VMEM(x.shape[1:], x.dtype)]
        if extra is not None:
            self.shapes.append(jax.ShapeDtypeStruct((size,) + extra.shape, extra.dtype))
            self.scratch.append(pltpu.VMEM(extra.shape, extra.dtype))
        self.out_specs = [anywhere] * len(arrays)
        self.sends = (size - 1) * len(arrays)
        self.locals = 2 * len(arrays)

    def begin(self, ins, outs, scratch, sems):
        me = lax.axis_index("band")
        self.sems, self.scratch_refs = sems, scratch
        self.slots = [out.at[me] for out in outs]
        self.loads = [sems.copy(ins[0].at[me], scratch[0])]
        if len(ins) > 1:
            self.loads.append(sems.copy(ins[1], scratch[1]))
        self.copies = []
        for peer in band_peers():
            if len(ins) > 1:
                self.copies.append(sems.send(ins[1], self.slots[1], peer))
            self.copies.append(sems.send(ins[0].at[peer[0]], self.slots[0], peer))

    def middle(self):
        self.stores = []
        for load, through, slot in zip(self.loads, self.scratch_refs, self.slots):
            load.wait()
            self.stores.append(self.sems.copy(through, slot))

    def end(self):
        for copy in self.copies + self.stores:
            copy.wait()


class Work:
    def __init__(self, operands, tasks, early):
        self.tasks, self.early = tasks, early
        self.operands = operands
        self.shapes = []
        for kind, left, right, _, _ in tasks:
            known = [*operands, *self.shapes]
            if kind == "sum":
                self.shapes.append(jax.ShapeDtypeStruct((1, known[left].shape[1]), f32))
                continue
            rows = known[left].shape[1 if kind == "tn" else 0]
            columns = known[right].shape[0 if kind == "nt" else 1]
            self.shapes.append(jax.ShapeDtypeStruct((rows, columns), bf16))
        self.scratch = [pltpu.VMEM(x.shape, x.dtype) for x in [*operands, *self.shapes]]
        self.locals = len(operands) + len(tasks)

    def begin(self, ins, outs, scratch, sems):
        self.sems, self.outs = sems, outs
        self.held, self.made = scratch[: len(ins)], scratch[len(ins) :]
        self.loads = [sems.copy(source, target) for source, target in zip(ins, self.held)]
        self.stores = []

    def ready(self, k):
        if k < len(self.loads) and self.loads[k] is not None:
            self.loads[k].wait()
            self.loads[k] = None

    def run(self, tasks):
        for kind, left, right, scale, out in tasks:
            for k in (left, right, scale):
                if k is not None:
                    self.ready(k)
            known = [*self.held, *self.made]
            x, made = known[left], self.made[out]
            if kind == "sum":
                rows = min(128, x.shape[0])
                made[...] = jnp.zeros_like(made)

                def add(k, _, x=x, made=made, rows=rows):
                    r = pl.ds(pl.multiple_of(k * rows, rows), rows)
                    made[...] += jnp.sum(x[r, :].astype(f32), axis=0, keepdims=True)
                    return 0

                lax.fori_loop(0, x.shape[0] // rows, add, 0)
                self.stores.append(self.sems.copy(made, self.outs[out]))
                continue
            y = known[right]
            factor = None if scale is None else self.held[scale]
            tile_r, tile_c = min(512, made.shape[0]), min(512, made.shape[1])
            columns = made.shape[1] // tile_c

            def tile(k, _, kind=kind, x=x, y=y, made=made, factor=factor):
                i, j = k // columns, lax.rem(k, columns)
                r = pl.ds(pl.multiple_of(i * tile_r, tile_r), tile_r)
                c = pl.ds(pl.multiple_of(j * tile_c, tile_c), tile_c)
                if kind == "tn":
                    total = tn(x[:, r], y[:, c])
                elif kind == "nt":
                    total = nt(x[r, :], y[c, :])
                else:
                    total = nn(x[r, :], y[:, c])
                if factor is not None:
                    total = total * factor[r, c].astype(f32)
                made[r, c] = total.astype(made.dtype)
                return 0

            lax.fori_loop(0, (made.shape[0] // tile_r) * columns, tile, 0)
            self.stores.append(self.sems.copy(made, self.outs[out]))

    def end(self):
        for store in self.stores:
            store.wait()


def transfer(parts, cid, work=None, name="transfer", time=36):
    items = list(parts) + ([work] if work is not None else [])
    sends = sum(part.sends for part in parts)
    locals_ = sum(item.locals for item in items)

    def kernel(*refs):
        refs = list(refs)

        def take(number):
            taken = refs[:number]
            del refs[:number]
            return taken

        ins = [take(len(item.operands)) for item in items]
        outs = [take(len(item.shapes)) for item in items]
        scratch = [take(len(item.scratch)) for item in items]
        sems = Sems(*refs)
        devices = []
        if any(part.peers == "tp" for part in parts):
            devices += tp_peers()
        if any(part.peers == "band" for part in parts):
            devices += band_peers()
        barrier = pltpu.get_barrier_semaphore()
        for device in devices:
            pl.semaphore_signal(barrier, inc=1, device_id=device, device_id_type=MESH)
        if work is not None:
            work.begin(ins[-1], outs[-1], scratch[-1], sems)
        pl.semaphore_wait(barrier, len(devices))
        for part, i, o, t in zip(parts, ins, outs, scratch):
            part.begin(i, o, t, sems)
        if work is not None:
            work.run(work.tasks[: work.early])
        for part in parts:
            part.middle()
        if work is not None:
            work.run(work.tasks[work.early :])
        for part in parts:
            part.end()
        if work is not None:
            work.end()

    in_specs = [spec for part in parts for spec in part.in_specs]
    out_specs = [spec for part in parts for spec in part.out_specs]
    if work is not None:
        in_specs += [anywhere] * len(work.operands)
        out_specs += [anywhere] * len(work.shapes)
    return pl.pallas_call(
        kernel,
        out_shape=tuple(shape for item in items for shape in item.shapes),
        in_specs=in_specs,
        out_specs=tuple(out_specs),
        scratch_shapes=[
            *(scratch for item in items for scratch in item.scratch),
            pltpu.SemaphoreType.DMA((sends,)),
            pltpu.SemaphoreType.DMA((sends,)),
            pltpu.SemaphoreType.DMA((locals_,)),
        ],
        compiler_params=pltpu.CompilerParams(
            collective_id=cid, has_side_effects=True, vmem_limit_bytes=(58 if work else 32) * 2**20
        ),
        cost_estimate=takes(time),
        name=name,
    )(*(operand for item in items for operand in item.operands))


def gather_later(x, axis=0):
    x = jnp.expand_dims(x, axis)
    copies = jnp.broadcast_to(x, x.shape[:axis] + (lax.axis_size("tp"),) + x.shape[axis + 1 :])
    return lax.all_to_all(copies, "tp", axis, axis)


class Block:
    def __init__(self, order, shift, grid, size):
        band = lax.axis_index("band")
        self.order, self.shift = order, shift
        self.to, self.source = lax.rem(band + shift, size), lax.rem(band + size - shift, size)
        if order % 2 == 0:
            self.n1, self.n2 = grid.nb, grid.na
            self.first, self.second, self.origin = grid.along_b, grid.along_a, grid.from_b
            self.index = lambda d, e: lax.rem(grid.a + e, grid.na) * grid.nb + lax.rem(
                grid.b + d, grid.nb
            )
        else:
            self.n1, self.n2 = grid.na, grid.nb
            self.first, self.second, self.origin = grid.along_a, grid.along_b, grid.from_a
            self.index = lambda d, e: lax.rem(grid.a + d, grid.na) * grid.nb + lax.rem(
                grid.b + e, grid.nb
            )


def finish_kernel(
    count, size, part, unit, above, resid, inverse, gain, wide, narrow,
    out, wide_out, narrow_out,
    own, one, two_out, two, made, arrived, late, late_in, wide_in, narrow_in, pair, pair_b, pair_a,
    send_sem, recv_sem, local_sem,
):
    grid = Grid(count)
    sems = Sems(send_sem, recv_sem, local_sem)
    band = lax.axis_index("band")
    peers = band_peers()
    devices = grid.along_a + grid.along_b + peers
    barrier = pltpu.get_barrier_semaphore()
    for device in devices:
        pl.semaphore_signal(barrier, inc=1, device_id=device, device_id_type=MESH)
    shifts = sorted(range(1, size), key=lambda shift: abs(2 * shift - size)) + [0]
    blocks = [Block(k, shift, grid, size) for k, shift in enumerate(shifts)]
    late[...] = jnp.zeros_like(late)
    pl.semaphore_wait(barrier, len(devices))
    done = []

    for blk in blocks:
        k = blk.order
        seconds = list(range(1, blk.n2)) + [0]
        blk.one = {
            (d, e): sems.send(
                part.at[blk.index(d, e), blk.to], one.at[k, d - 1, e], blk.first[d - 1]
            )
            for e in seconds
            for d in range(1, blk.n1)
        }
        blk.own = {e: sems.copy(part.at[blk.index(0, e), blk.to], own.at[k, e]) for e in seconds}
    early = []
    for peer in peers:
        early.append(sems.send(wide, wide_in.at[band], peer))
        early.append(sems.send(narrow, narrow_in.at[band], peer))

    def first_sum(blk, e):
        k = blk.order
        blk.own[e].wait()
        total = own[k, e].astype(f32)
        for d in range(1, blk.n1):
            blk.one[d, e].wait_recv()
            total = total + one[k, d - 1, e].astype(f32)
        return total

    def pass_on(blk):
        k = blk.order
        blk.two = []
        for e in range(1, blk.n2):
            two_out[k, e - 1] = first_sum(blk, e).astype(bf16)
            blk.two.append(sems.send(two_out.at[k, e - 1], two.at[k, e - 1], blk.second[e - 1]))

    def complete(blk):
        k = blk.order
        grad = first_sum(blk, 0)
        for e, copy in enumerate(blk.two):
            copy.wait_recv()
            grad = grad + two[k, e].astype(f32)
        normed = unit[blk.to]
        scaled = grad * gain[...]
        mean = jnp.mean(scaled, axis=-1, keepdims=True)
        along = jnp.mean(scaled * normed, axis=-1, keepdims=True)
        base = above[blk.to].astype(f32) + resid[blk.to]
        token = base + inverse[blk.to] * (scaled - mean - normed * along)
        made[k] = token.astype(bf16)
        sums = (jnp.sum(grad * normed, axis=0, keepdims=True), jnp.sum(grad, axis=0, keepdims=True))
        quarter = late.shape[1]
        for which, total in enumerate(sums):
            for i in range(4):
                row = slice(4 * which + i, 4 * which + i + 1)
                late[row, :] = late[row, :] + total[:, i * quarter : (i + 1) * quarter]
        if blk.shift:
            blk.swap = sems.send(made.at[k], arrived.at[k], (blk.to, lax.axis_index("tp")))

    def relay(blk):
        k = blk.order
        if blk.shift:
            blk.swap.wait_recv()
            held = arrived.at[k]
        else:
            held = made.at[k]
        slot = out.at[blk.source, grid.me]
        blk.near = [sems.send(held, slot, device) for device in blk.first]
        blk.far = [sems.send(held, slot, device) for device in blk.second]
        done.append(sems.copy(held, slot))

    def forward(blk):
        for copy, source in zip(blk.near, blk.origin):
            copy.wait_recv()
            held = out.at[blk.source, source]
            blk.far += [sems.send(held, held, device) for device in blk.second]

    pairs = [blocks[k : k + 2] for k in range(0, size, 2)]
    stages = (pass_on, complete, relay, forward)
    for step in range(len(pairs) + len(stages) - 1):
        for behind, stage in enumerate(stages):
            if 0 <= step - behind < len(pairs):
                for blk in pairs[step - behind]:
                    stage(blk)
        if step == len(pairs):
            last = [sems.send(late, late_in.at[band], peer) for peer in peers]

    for copy in early + last:
        copy.wait_recv()
    wide_in[band] = wide[...]
    narrow_in[band] = narrow[...]
    late_in[band] = late[...]
    total, narrow_total, late_total = (
        sum(array[k].astype(f32) for k in range(size)) for array in (wide_in, narrow_in, late_in)
    )
    narrow_out[...] = narrow_total
    pair[0:16, :] = total
    pair[16:24, :] = late_total
    near = [sems.send(pair, pair_b.at[k], device) for k, device in enumerate(grid.along_b)]
    total = pair[...]
    for k, copy in enumerate(near):
        copy.wait_recv()
        total = total + pair_b[k]
    for copy in near:
        copy.wait_send()
    pair[...] = total
    far = [sems.send(pair, pair_a.at[k], device) for k, device in enumerate(grid.along_a)]
    for k, copy in enumerate(far):
        copy.wait_recv()
        total = total + pair_a[k]
    wide_out[...] = total

    for copy in early + last + far:
        copy.wait_send()
    for blk in blocks:
        for copy in [*blk.one.values(), *blk.two, *blk.near]:
            copy.wait_send()
        if blk.shift:
            blk.swap.wait_send()
        for copy in blk.far:
            copy.wait()
    for copy in done:
        copy.wait()


def finish(part, unit, above, resid, inverse, gain, wide, narrow, cid):
    count, size, rows, width = part.shape
    na, nb = halves(count)
    most = max(na, nb)
    sends = locals_ = 0
    for k in range(size):
        n1, n2 = (nb, na) if k % 2 == 0 else (na, nb)
        sends += (n1 - 1) * n2 + 2 * (n2 - 1) + (n1 - 1) + (n1 - 1) * (n2 - 1)
        locals_ += n2 + 1
    sends += 4 * (size - 1) + na - 1 + nb - 1
    lanes = wide.shape[1]

    def blocks(*lead):
        return pltpu.VMEM(tuple(max(n, 1) for n in lead) + (rows, width), bf16)

    return pl.pallas_call(
        functools.partial(finish_kernel, count, size),
        out_shape=(
            jax.ShapeDtypeStruct((size, count, rows, width), bf16),
            jax.ShapeDtypeStruct((24, lanes), f32),
            jax.ShapeDtypeStruct(narrow.shape, f32),
        ),
        in_specs=[anywhere] + [vmem] * 7,
        out_specs=(anywhere, vmem, vmem),
        scratch_shapes=[
            blocks(size, most), blocks(size, most - 1, most),
            blocks(size, most - 1), blocks(size, most - 1),
            blocks(size), blocks(size),
            pltpu.VMEM((8, lanes), f32),
            pltpu.VMEM((size, 8, lanes), f32),
            pltpu.VMEM((size,) + wide.shape, bf16),
            pltpu.VMEM((size,) + narrow.shape, bf16),
            pltpu.VMEM((24, lanes), f32),
            pltpu.VMEM((max(nb - 1, 1), 24, lanes), f32),
            pltpu.VMEM((max(na - 1, 1), 24, lanes), f32),
            pltpu.SemaphoreType.DMA((sends,)),
            pltpu.SemaphoreType.DMA((sends,)),
            pltpu.SemaphoreType.DMA((locals_,)),
        ],
        compiler_params=pltpu.CompilerParams(
            collective_id=cid, has_side_effects=True, vmem_limit_bytes=48 * 2**20
        ),
        cost_estimate=takes(90),
        name="finish",
    )(part, unit, above, resid, inverse, gain, wide, narrow)


def heads_kernel(group, kind, x_ref, o_ref, through, local_sem, send_sem, recv_sem):
    band, tp = lax.axis_index("band"), lax.axis_index("tp")
    mine = lax.rem(band, group)
    base = band - mine
    others = [lax.rem(mine + d, group) for d in range(1, group)]
    sems = Sems(send_sem, recv_sem, local_sem)
    width = through.shape[1]

    def columns(index):
        return pl.ds(pl.multiple_of(index * width, width), width)

    def source(index):
        return x_ref.at[:, columns(index)] if kind == "cut" else x_ref.at[index]

    target = o_ref.at[:, columns(mine)] if kind == "join" else o_ref.at[mine]
    barrier = pltpu.get_barrier_semaphore()
    for other in others:
        pl.semaphore_signal(barrier, inc=1, device_id=(base + other, tp), device_id_type=MESH)
    load = sems.copy(source(mine), through)
    pl.semaphore_wait(barrier, group - 1)
    copies = [sems.send(source(other), target, (base + other, tp)) for other in others]
    load.wait()
    for copy in [sems.copy(through, target), *copies]:
        copy.wait()


def swap_heads(x, group, cid, kind):
    if kind == "cut":
        rows, width = x.shape[0], x.shape[1] // group
    else:
        rows, width = x.shape[1:]
    if width % 128 and kind == "cut":
        x = x.reshape(rows, group, width).transpose(1, 0, 2)
        return swap_heads(x, group, cid, "plain")
    if width % 128 and kind == "join":
        x = swap_heads(x, group, cid, "plain")
        return x.transpose(1, 0, 2).reshape(rows, group * width)
    shape = (rows, group * width) if kind == "join" else (group, rows, width)
    return pl.pallas_call(
        functools.partial(heads_kernel, group, kind),
        out_shape=jax.ShapeDtypeStruct(shape, x.dtype),
        in_specs=[anywhere],
        out_specs=anywhere,
        scratch_shapes=[
            pltpu.VMEM((rows, width), x.dtype),
            pltpu.SemaphoreType.DMA((2,)),
            pltpu.SemaphoreType.DMA((group - 1,)),
            pltpu.SemaphoreType.DMA((group - 1,)),
        ],
        compiler_params=pltpu.CompilerParams(collective_id=cid, has_side_effects=True),
        cost_estimate=takes(4),
        name="swap_heads",
    )(x)


def settle_kernel(
    wides, grad_ref, out_ref, up_ref, down_ref, wide_ref, narrow_ref,
    grad_to, out_to, up_to, down_to, *small,
):
    grad_to[...] = grad_ref[...].astype(f32)
    out_to[0] = out_ref[:, 0]
    up_to[...] = up_ref[...].astype(f32)
    down_to[...] = down_ref[...].astype(f32).T

    @pl.when(pl.program_id(0) == 0)
    def _():
        for refs, source in ((small[:wides], wide_ref), (small[wides:], narrow_ref)):
            lanes, row = source.shape[1], 0
            for ref in refs:
                for i in range(ref.shape[1] // lanes):
                    ref[0:1, i * lanes : (i + 1) * lanes] = source[row : row + 1, :]
                    row += 1


def settle(grad, out, up, down, wide, narrow, widths):
    size, count, rows, width = grad.shape
    wides = wide.shape[0] * wide.shape[1] // width
    slab = down.shape[1] // size
    small = [width] * wides + list(widths)
    block = pl.BlockSpec((1, count, rows, width), lambda i: (i, 0, 0, 0))
    across = pl.BlockSpec((up.shape[0] // size, up.shape[1]), lambda i: (i, 0))
    if up.shape[0] // size % 16:
        across = pl.BlockSpec(up.shape, lambda i: (0, 0))
    return pl.pallas_call(
        functools.partial(settle_kernel, wides),
        out_shape=(
            jax.ShapeDtypeStruct(grad.shape, f32),
            jax.ShapeDtypeStruct(grad.shape, out.dtype),
            jax.ShapeDtypeStruct(up.shape, f32),
            jax.ShapeDtypeStruct(down.shape[::-1], f32),
            *(jax.ShapeDtypeStruct((1, n), f32) for n in small),
        ),
        grid=(size,),
        in_specs=[
            block,
            pl.BlockSpec((count, 1, rows, width), lambda i: (0, i, 0, 0)),
            across,
            pl.BlockSpec((down.shape[0], slab), lambda i: (0, i)) if slab % 128 == 0 else vmem,
            pl.BlockSpec(wide.shape, lambda i: (0, 0)),
            pl.BlockSpec(narrow.shape, lambda i: (0, 0)),
        ],
        out_specs=(
            block,
            block,
            across,
            pl.BlockSpec((slab, down.shape[0]), lambda i: (i, 0)) if slab % 128 == 0 else vmem,
            *(pl.BlockSpec((1, n), lambda i: (0, 0)) for n in small),
        ),
        compiler_params=pltpu.CompilerParams(vmem_limit_bytes=40 * 2**20),
        cost_estimate=takes(10),
        name="settle",
    )(grad, out, up, down, wide, narrow)


def split_kernel(group, features, x_ref, q_ref, k_ref, v_ref, out_ref):
    for g in range(group):
        for which, ref in enumerate((q_ref, k_ref, v_ref)):
            start = (3 * g + which) * features
            ref[:, g * features : (g + 1) * features] = x_ref[:, start : start + features].astype(f32)
    out_ref[...] = x_ref[:, 3 * group * features :].astype(f32).T


def split_shared(x, group, features):
    rows, inner = x.shape[0], group * features
    return pl.pallas_call(
        functools.partial(split_kernel, group, features),
        out_shape=(
            *[jax.ShapeDtypeStruct((rows, inner), f32)] * 3,
            jax.ShapeDtypeStruct((x.shape[1] - 3 * inner, rows), f32),
        ),
        in_specs=[vmem],
        out_specs=(vmem,) * 4,
        compiler_params=pltpu.CompilerParams(vmem_limit_bytes=32 * 2**20),
        cost_estimate=takes(2),
        name="split_shared",
    )(x)


def project_kernel(x_ref, w_ref, bias_ref, scale_ref, o_ref):
    total = nn(x_ref[...], w_ref[...]) + bias_ref[...]
    o_ref[0] = total.astype(bf16) * scale_ref[...].astype(bf16)


def project(x, weight, bias, scale, group):
    rows, depth = x.shape
    total_width = bias.shape[0]
    width = total_width // group
    if width % 128:
        total = (nn(x, weight[:, :total_width]) + bias).astype(bf16) * scale.astype(bf16)
        return total.reshape(rows, group, width).transpose(1, 0, 2)
    block = min(256, rows)
    return pl.pallas_call(
        project_kernel,
        out_shape=jax.ShapeDtypeStruct((group, rows, width), bf16),
        grid=(group, rows // block),
        in_specs=[
            pl.BlockSpec((block, depth), lambda g, i: (i, 0)),
            pl.BlockSpec((depth, width), lambda g, i: (0, g)),
            pl.BlockSpec((1, width), lambda g, i: (0, g)),
            pl.BlockSpec((1, width), lambda g, i: (0, g)),
        ],
        out_specs=pl.BlockSpec((1, block, width), lambda g, i: (g, i, 0)),
        compiler_params=pltpu.CompilerParams(vmem_limit_bytes=40 * 2**20),
        cost_estimate=pl.CostEstimate(
            flops=2 * rows * depth * width * group, bytes_accessed=12 * 2**20, transcendentals=0
        ),
        name="project",
    )(x, weight, bias[None], scale[None])


def products_kernel(left_ref, right_ref, other_ref, last_ref, o_ref):
    tile, width = last_ref.shape[1], right_ref.shape[1]

    def step(k, _):
        columns = pl.ds(pl.multiple_of(k * tile, tile), tile)
        o_ref[:, columns] = tn(left_ref[...], right_ref[:, columns]).astype(o_ref.dtype)
        return 0

    lax.fori_loop(0, width // tile, step, 0)
    o_ref[:, width:] = tn(other_ref[...], last_ref[...]).astype(o_ref.dtype)


def product_kernel(left_ref, right_ref, o_ref):
    tile = min(512, o_ref.shape[1])

    def step(k, _):
        columns = pl.ds(pl.multiple_of(k * tile, tile), tile)
        o_ref[:, columns] = tn(left_ref[...], right_ref[:, columns]).astype(o_ref.dtype)
        return 0

    lax.fori_loop(0, o_ref.shape[1] // tile, step, 0)


def product(left, right):
    rows, depth = left.shape
    width = right.shape[1]
    tile = min(512, depth)
    return pl.pallas_call(
        product_kernel,
        out_shape=jax.ShapeDtypeStruct((depth, width), bf16),
        grid=(depth // tile,),
        in_specs=[
            pl.BlockSpec((rows, tile), lambda i: (0, i)),
            pl.BlockSpec((rows, width), lambda i: (0, 0)),
        ],
        out_specs=pl.BlockSpec((tile, width), lambda i: (i, 0)),
        compiler_params=pltpu.CompilerParams(vmem_limit_bytes=40 * 2**20),
        cost_estimate=takes(12),
        name="product",
    )(left, right)


def two_products(left, right, other, last):
    rows, depth = left.shape
    width, more = right.shape[1], last.shape[1]
    tile = min(512, depth)
    cut = pl.BlockSpec((rows, tile), lambda i: (0, i))
    return pl.pallas_call(
        products_kernel,
        out_shape=jax.ShapeDtypeStruct((depth, width + more), bf16),
        grid=(depth // tile,),
        in_specs=[
            cut,
            pl.BlockSpec((rows, width), lambda i: (0, 0)),
            cut,
            pl.BlockSpec((rows, more), lambda i: (0, 0)),
        ],
        out_specs=pl.BlockSpec((tile, width + more), lambda i: (i, 0)),
        compiler_params=pltpu.CompilerParams(vmem_limit_bytes=48 * 2**20),
        cost_estimate=takes(12),
        name="two_products",
    )(left, right, other, last)


def permitted(first, limit, row, column):
    return ((column >= first) & (column <= limit)) | (column == row)


def head_mask(head, shape):
    lane = lax.broadcasted_iota(jnp.int32, shape, 1)
    return (lane >= head * HEAD_DIM) & (lane < (head + 1) * HEAD_DIM)


def attend_kernel(qb, kb, info_ref, first_ref, q_ref, k_ref, v_ref, o_ref, log_ref, vt_ref):
    length, width = q_ref.shape
    heads = width // HEAD_DIM
    live_end = info_ref[0]
    count = lax.div(live_end + qb - 1, qb)
    vt_ref[...] = v_ref[...].T
    o_ref[...] = jnp.zeros_like(o_ref)
    log_ref[...] = jnp.zeros_like(log_ref)

    def queries(i, _):
        rows = pl.ds(pl.multiple_of(i * qb, qb), qb)
        q = q_ref[rows, :]
        first = first_ref[0:1, rows]
        row = i * qb + lax.broadcasted_iota(jnp.int32, (1, qb), 1)
        limit = jnp.minimum(row, live_end - 1)
        q_heads = [
            jnp.where(head_mask(h, (qb, width)), q, jnp.zeros_like(q)) for h in range(heads)
        ]
        def keys(j, carry):
            columns = pl.ds(pl.multiple_of(j * kb, kb), kb)
            k = k_ref[columns, :]
            column = j * kb + lax.broadcasted_iota(jnp.int32, (kb, 1), 0)
            allowed = permitted(first, limit, row, column)
            out = []
            for h in range(heads):
                top, total, summed = carry[h]
                scores = jnp.where(allowed, nt(k, q_heads[h]), masked_score)
                new_top = jnp.maximum(top, jnp.max(scores, axis=0, keepdims=True))
                weights = jnp.exp(scores - new_top)
                scale = jnp.exp(top - new_top)
                total = total * scale + jnp.sum(weights, axis=0, keepdims=True)
                vt = vt_ref[h * HEAD_DIM : (h + 1) * HEAD_DIM, columns]
                summed = summed * scale + nn(vt, weights.astype(bf16))
                out.append((new_top, total, summed))
            return tuple(out)
        start = tuple(
            (
                jnp.full((1, qb), masked_score, f32),
                jnp.zeros((1, qb), f32),
                jnp.zeros((HEAD_DIM, qb), f32),
            )
            for _ in range(heads)
        )
        lo = lax.div(info_ref[1 + i], kb)
        hi = lax.div(i * qb + qb - 1, kb) + 1
        done = lax.fori_loop(lo, hi, keys, start)
        mixed = jnp.concatenate([summed / total for _, total, summed in done], axis=0)
        o_ref[rows, :] = mixed.T.astype(o_ref.dtype)
        for h, (top, total, _) in enumerate(done):
            log_ref[0, h : h + 1, rows] = top + jnp.log(total)
        return 0
    lax.fori_loop(0, count, queries, 0)


def attend_back_kernel(
    qb, kb, info_ref, first_ref, q_ref, k_ref, v_ref, o_ref, do_ref, log_ref, out_ref, sum_ref,
    dk_acc, dv_acc,
):
    length, width = q_ref.shape
    heads = width // HEAD_DIM
    features = out_ref.shape[1] // 3
    slab = pl.program_id(0)
    factor = HEAD_DIM ** (-0.5)
    live_end = info_ref[0]
    count = lax.div(live_end + qb - 1, qb)

    def lanes(which):
        if features == width:
            return pl.ds(which * features, width)
        return pl.ds(pl.multiple_of(which * features + slab * width, width), width)
    dk_acc[...] = jnp.zeros_like(dk_acc)
    dv_acc[...] = jnp.zeros_like(dv_acc)
    out_ref[:, lanes(0)] = jnp.zeros((length, width), out_ref.dtype)

    def queries(i, _):
        rows = pl.ds(pl.multiple_of(i * qb, qb), qb)
        q, do = q_ref[rows, :], do_ref[rows, :]
        first = first_ref[0:1, rows]
        row = i * qb + lax.broadcasted_iota(jnp.int32, (1, qb), 1)
        limit = jnp.minimum(row, live_end - 1)
        dots = (do.astype(f32) * o_ref[rows, :].astype(f32)).T
        masks = [head_mask(h, (qb, width)) for h in range(heads)]
        kmasks = [head_mask(h, (kb, width)) for h in range(heads)]
        zero = jnp.zeros_like(q)
        q_heads = [jnp.where(mask, q, zero) for mask in masks]
        do_heads = [jnp.where(mask, do, zero) for mask in masks]
        logs = [log_ref[0, h : h + 1, rows] for h in range(heads)]
        deltas = [
            jnp.sum(dots[h * HEAD_DIM : (h + 1) * HEAD_DIM], axis=0, keepdims=True)
            for h in range(heads)
        ]
        def keys(j, dq):
            columns = pl.ds(pl.multiple_of(j * kb, kb), kb)
            k, v = k_ref[columns, :], v_ref[columns, :]
            column = j * kb + lax.broadcasted_iota(jnp.int32, (kb, 1), 0)
            allowed = permitted(first, limit, row, column)
            dk, dv = dk_acc[columns, :], dv_acc[columns, :]
            for h in range(heads):
                scores = jnp.where(allowed, nt(k, q_heads[h]) - logs[h], masked_score)
                probs = jnp.exp(scores)
                prob_grad = nt(v, do_heads[h])
                score_grad = (probs * (prob_grad - deltas[h])).astype(bf16)
                dv = dv + nn(probs.astype(bf16), do_heads[h])
                dk = dk + nn(score_grad, q_heads[h])
                dq = dq + tn(score_grad, jnp.where(kmasks[h], k, jnp.zeros_like(k)))
            dk_acc[columns, :] = dk
            dv_acc[columns, :] = dv
            return dq
        lo = lax.div(info_ref[1 + i], kb)
        hi = lax.div(i * qb + qb - 1, kb) + 1
        dq = lax.fori_loop(lo, hi, keys, jnp.zeros((qb, width), f32))
        out_ref[rows, lanes(0)] = (dq * factor).astype(out_ref.dtype)
        return 0
    lax.fori_loop(0, count, queries, 0)
    sum_ref[...] = jnp.zeros_like(sum_ref)

    def store(i, _):
        rows = pl.ds(pl.multiple_of(i * kb, kb), kb)
        dv = dv_acc[rows, :].astype(out_ref.dtype)
        out_ref[rows, lanes(1)] = dk_acc[rows, :].astype(out_ref.dtype)
        out_ref[rows, lanes(2)] = dv
        dq = out_ref[rows, lanes(0)].astype(f32)
        sum_ref[0, 0:1, :] += jnp.sum(dq, axis=0, keepdims=True)
        sum_ref[0, 1:2, :] += jnp.sum(dv.astype(f32), axis=0, keepdims=True)
        return 0
    lax.fori_loop(0, length // kb, store, 0)


def attention_specs(length, features):
    width = min(256, features)
    slabs = features // width

    plain = pl.BlockSpec((length, width), lambda i, info: (0, i))

    def piece(which):
        if features % 128:
            return plain
        return pl.BlockSpec((length, width), lambda i, info, w=which: (0, w * slabs + i))

    logs = pl.BlockSpec((1, 8, length), lambda i, info: (i, 0, 0))
    first = pl.BlockSpec((1, length), lambda i, info: (0, 0))
    return width, slabs, piece, plain, logs, first


def three(qkv, features):
    if features % 128:
        return [qkv[:, w * features : (w + 1) * features] for w in range(3)]
    return [qkv] * 3


def attend(qkv, info, first, qb, kb):
    length, features = qkv.shape[0], qkv.shape[1] // 3
    width, slabs, piece, plain, logs, first_spec = attention_specs(length, features)
    return pl.pallas_call(
        functools.partial(attend_kernel, qb, kb),
        out_shape=(
            jax.ShapeDtypeStruct((length, features), bf16),
            jax.ShapeDtypeStruct((slabs, 8, length), f32),
        ),
        grid_spec=pltpu.PrefetchScalarGridSpec(
            num_scalar_prefetch=1,
            grid=(slabs,),
            in_specs=[first_spec, piece(0), piece(1), piece(2)],
            out_specs=(plain, logs),
            scratch_shapes=[pltpu.VMEM((width, length), bf16)],
        ),
        compiler_params=pltpu.CompilerParams(vmem_limit_bytes=48 * 2**20),
        cost_estimate=takes(30),
        name="attend",
    )(info, first, *three(qkv, features))


def attend_back(qkv, mixed, grad, log_total, info, first, qb, kb):
    length, features = qkv.shape[0], qkv.shape[1] // 3
    width, slabs, piece, plain, logs, first_spec = attention_specs(length, features)
    return pl.pallas_call(
        functools.partial(attend_back_kernel, qb, kb),
        out_shape=(
            jax.ShapeDtypeStruct((length, 3 * features), bf16),
            jax.ShapeDtypeStruct((slabs, 8, width), f32),
        ),
        grid_spec=pltpu.PrefetchScalarGridSpec(
            num_scalar_prefetch=1,
            grid=(slabs,),
            in_specs=[first_spec, piece(0), piece(1), piece(2), plain, plain, logs],
            out_specs=(
                pl.BlockSpec((length, 3 * features), lambda i, info: (0, 0)),
                pl.BlockSpec((1, 8, width), lambda i, info: (i, 0, 0)),
            ),
            scratch_shapes=[pltpu.VMEM((length, width), f32), pltpu.VMEM((length, width), f32)],
        ),
        compiler_params=pltpu.CompilerParams(vmem_limit_bytes=48 * 2**20),
        cost_estimate=takes(34),
        name="attend_back",
    )(info, first, *three(qkv, features), mixed, grad, log_total)


def body(
    tokens,
    positions,
    doc_lengths,
    exit_depth,
    w_query,
    w_key,
    w_value,
    w_out,
    w_up,
    w_down,
    b_query,
    b_value,
    b_out,
    b_up,
    b_down,
    attn_gain,
    attn_bias,
    ffn_gain,
    ffn_bias,
    cotangent,
):
    seqs, local_rows, width = tokens.shape
    inner = b_query.shape[0]
    bands, tps = lax.axis_size("band"), lax.axis_size("tp")
    group = bands // seqs
    piece = local_rows // (group * tps)
    band, tp = lax.axis_index("band"), lax.axis_index("tp")
    seq, member = band // group, lax.rem(band, group)
    features = inner // group
    length = exit_depth.shape[1]
    own = bands * piece
    rows = tps * own
    block, half_block = min(512, length), min(256, length)

    def by_group(*parts):
        split = [p.reshape(p.shape[:-1] + (group, features)) for p in parts]
        return jnp.stack(split, axis=-2).reshape(parts[0].shape[:-1] + (-1,))

    def share(grad):
        return lax.psum_scatter(grad, "band", scatter_dimension=0, tiled=True)

    w_in_out = jnp.concatenate([by_group(w_query, w_key, w_value), w_out.T], axis=1)
    w_in_out = lax.all_gather(w_in_out, "band", axis=0, tiled=True)
    w_in, w_out_t = w_in_out[:, : 3 * inner], w_in_out[:, 3 * inner :]
    w_up_all = lax.all_gather(w_up, "band", axis=0, tiled=True)
    w_down_t = lax.all_gather(w_down.T, "band", axis=0, tiled=True)

    def my_share(array):
        split = array.reshape(seqs, group, tps, piece, width)
        return lax.dynamic_index_in_dim(split, tp, 2, keepdims=False).reshape(bands, piece, width)

    token_own, all_pos = transfer([Swap(my_share(tokens), positions)], 0, name="swap_in")
    seq_pos = lax.dynamic_index_in_dim(all_pos, seq, 1, keepdims=False)
    seq_pos = seq_pos.reshape(bands, group, tps, piece).transpose(1, 2, 0, 3)
    row_pos = seq_pos.reshape(length)
    member_pos = lax.dynamic_index_in_dim(seq_pos, member, 0, keepdims=False)
    own_pos = lax.dynamic_index_in_dim(member_pos, tp, 0, keepdims=False).reshape(own)
    depths = lax.dynamic_index_in_dim(exit_depth, seq, 0, keepdims=False)
    live_end = jnp.sum((depths > LAYER).astype(jnp.int32))
    live_own = (own_pos < live_end).astype(f32)[:, None]
    ends = jnp.cumsum(lax.dynamic_index_in_dim(doc_lengths, seq, 0, keepdims=False))
    places = jnp.arange(length, dtype=jnp.int32)
    first = jnp.max(jnp.where(ends[:, None] <= places[None, :], ends[:, None], 0), axis=0)
    info = jnp.concatenate([live_end[None], first[::block]]).astype(jnp.int32)
    first = first[None, :].astype(jnp.int32)
    to_sorted = (row_pos[None, :] == places[:, None]).astype(bf16)
    to_rows = (row_pos[:, None] == places[None, :]).astype(bf16)

    inputs = token_own.reshape(own, width).astype(f32)
    normed_in, unit_in, inverse_in = layer_norm(inputs, attn_gain, attn_bias)
    z1, grad_low = transfer([Gather(normed_in.astype(bf16)), Swap(my_share(cotangent))], 1, name="gather_in")
    z1 = z1.reshape(rows, width)
    grad_own = grad_low.reshape(own, width).astype(f32)
    down_grad_own = (live_own * grad_own).astype(bf16)
    down_grad = gather_later(down_grad_own)

    bias_in = by_group(b_query, jnp.zeros_like(b_query), b_value)
    scale_in = by_group(
        jnp.full_like(b_query, HEAD_DIM ** (-0.5)), jnp.ones_like(b_query), jnp.ones_like(b_query)
    )
    qkv = project(z1, w_in_out, bias_in, scale_in, group)
    qkv = swap_heads(qkv, group, 4, "plain").reshape(length, 3 * features)
    qkv = nn(to_sorted, qkv).astype(bf16)
    mixed_sorted, log_total = attend(qkv, info, first, block, block)
    mixed_sorted, down_grad = lax.optimization_barrier((mixed_sorted, down_grad))
    down_grad = down_grad.reshape(rows, width)
    mixed = nn(to_rows, mixed_sorted).astype(bf16).reshape(group, rows, features)
    mixed = swap_heads(mixed, group, 5, "join")

    attn_part = nt(mixed, w_out_t).astype(bf16).reshape(tps, own, width)
    (attn_out,) = transfer([Scatter(attn_part)], 6, name="scatter_attn")
    attn_out = attn_out + b_out
    residual = inputs + attn_out
    normed_mid, unit_mid, inverse_mid = layer_norm(residual, ffn_gain, ffn_bias)
    (z2,) = transfer([Gather(normed_mid.astype(bf16))], 7, name="gather_mid")
    z2 = z2.reshape(rows, width)
    pre_act = nn(z2, w_up_all) + b_up
    below = 0.5 * (1.0 + lax.erf(pre_act * 0.5**0.5))
    act = (pre_act * below).astype(bf16)
    slope = (below + pre_act * jnp.exp(-0.5 * pre_act * pre_act) * (2 * math.pi) ** -0.5).astype(bf16)

    grad_w_down_t = product(down_grad, act)
    grad_w_down_t, act = lax.optimization_barrier((grad_w_down_t, act))
    shared_down = share(grad_w_down_t)
    ffn_part = nt(act, w_down_t).astype(bf16).reshape(tps, own, width)
    ffn_out, up_grad, mid_part = transfer(
        [Scatter(ffn_part)],
        8,
        Work(
            [down_grad, w_down_t, slope, w_up_all],
            [("nn", 0, 1, 2, 0), ("nt", 4, 3, None, 1)],
            1,
        ),
        name="scatter_ffn",
    )
    output = (inputs + live_own * (attn_out + ffn_out + b_down)).astype(bf16)
    output = output.reshape(bands, piece, width)

    mid_part = mid_part.reshape(tps, own, width)
    mid_grad, grad_w_up, up_sums = transfer(
        [Scatter(mid_part)],
        9,
        Work([z2, up_grad], [("tn", 0, 1, None, 0), ("sum", 1, None, None, 1)], 1),
        name="scatter_mid",
    )
    resid_grad = norm_back(mid_grad, unit_mid, inverse_mid, ffn_gain)
    attn_grad_own = (live_own * grad_own + resid_grad).astype(bf16)
    attn_grad, output = transfer([Gather(attn_grad_own), Swap(output)], 10, name="gather_back")
    attn_grad = attn_grad.reshape(rows, width)
    attn_grad, output, grad_w_up = lax.optimization_barrier((attn_grad, output, grad_w_up))
    output = gather_later(output)

    mixed_grad = nn(attn_grad, w_out_t).astype(bf16)
    mixed_grad = swap_heads(mixed_grad, group, 13, "cut").reshape(length, features)
    mixed_grad = nn(to_sorted, mixed_grad).astype(bf16)
    grad_w_up, shared_down = lax.optimization_barrier((grad_w_up, shared_down))
    shared_up = share(grad_w_up)
    in_grad, in_sums = attend_back(
        qkv, mixed_sorted, mixed_grad, log_total, info, first, block, half_block
    )
    in_sums = in_sums.transpose(1, 0, 2).reshape(8, features)
    mine = (jnp.arange(group) == member).astype(f32)[:, None]
    in_grad = nn(to_rows, in_grad).astype(bf16).reshape(group, rows, 3 * features)
    in_grad = swap_heads(in_grad, group, 14, "join")
    in_grad, output = lax.optimization_barrier((in_grad, output))
    grad_w_in_out = two_products(z1, in_grad, attn_grad, mixed)
    in_grad, grad_w_in_out = lax.optimization_barrier((in_grad, grad_w_in_out))
    in_part = nt(in_grad, w_in).astype(bf16).reshape(tps, bands, piece, width)
    grad_w_in_out, shared_up, in_part = lax.optimization_barrier((grad_w_in_out, shared_up, in_part))
    shared_in_out = share(grad_w_in_out)

    def over_rows(array):
        return jnp.sum(array.astype(f32), axis=0)

    wide = [
        over_rows(attn_grad_own),
        over_rows(down_grad_own),
        over_rows(mid_grad * unit_mid),
        over_rows(mid_grad),
    ]
    wide = jnp.concatenate(wide).astype(bf16).reshape(16, width // 4)
    narrow = jnp.concatenate(
        [(mine * in_sums[0]).reshape(-1), (mine * in_sums[1]).reshape(-1), up_sums[0]]
    )
    count = narrow.shape[0]
    narrow = jnp.pad(narrow, (0, -count % 2048)).astype(bf16).reshape(16, -1)
    token_grad, wide, narrow = finish(
        in_part,
        unit_in.reshape(bands, piece, width),
        grad_low,
        resid_grad.reshape(bands, piece, width),
        inverse_in.reshape(bands, piece, 1),
        attn_gain[None],
        wide,
        narrow,
        15,
    )
    token_grad, output, shared_up, shared_down, *small = settle(
        token_grad, output, shared_up, shared_down, wide, narrow, (inner, inner, b_up.shape[0])
    )
    token_grad, output = token_grad.reshape(tokens.shape), output.reshape(tokens.shape)
    small = [vector.reshape(-1) for vector in small]
    shared_q, shared_k, shared_v, shared_out = split_shared(shared_in_out, group, features)
    return (
        output,
        token_grad,
        shared_q,
        shared_k,
        shared_v,
        shared_out,
        shared_up,
        shared_down,
        small[6],
        small[7],
        small[0],
        small[8],
        small[1],
        small[4],
        small[5],
        small[2],
        small[3],
    )


def solution(mesh):
    return jax.shard_map(
        body,
        mesh=mesh,
        in_specs=(
            P(None, "band", None),
            P(None, "band"),
            P(),
            P(),
            P("band", "tp"),
            P("band", "tp"),
            P("band", "tp"),
            P("tp", "band"),
            P("band", "tp"),
            P("tp", "band"),
            P("tp"),
            P("tp"),
            P(),
            P("tp"),
            P(),
            P(),
            P(),
            P(),
            P(),
            P(None, "band", None),
        ),
        out_specs=(
            P(None, "band", None),
            P(None, "band", None),
            P("band", "tp"),
            P("band", "tp"),
            P("band", "tp"),
            P("tp", "band"),
            P("band", "tp"),
            P("tp", "band"),
            P("tp"),
            P("tp"),
            P(),
            P("tp"),
            P(),
            P(),
            P(),
            P(),
            P(),
        ),
        check_vma=False,
    )
```
